256 devices in a mesh: gx: 16 (over z, x_lo), gy: 16 (over x_hi, y, core).
Axes of the slice: x: 4 (x_hi: 2, x_lo: 2; x = x_hi * 2 + x_lo), y: 4, z: 8, core: 2. Of those that a mesh axis runs over, the one named last changes fastest.
Arguments:
- tokens: bfloat16 [128, 128, 24, 192], P('gx', 'gy'), may hold values from -8 to 8
- cotangent: bfloat16 [128, 128, 24, 192], P('gx', 'gy'), may hold values from -12 to 12
- ln_gain: float32 [192], replicated, may hold values from 0.1 to 1.9
- ln_bias: float32 [192], replicated, may hold values from -3 to 3
- qkv_weight: bfloat16 [192, 576], replicated, may hold values from -1 to 1
- proj_weight: bfloat16 [192, 192], replicated, may hold values from -0.4375 to 0.4375
Outputs:
- block_out: bfloat16 [128, 128, 24, 192], P('gx', 'gy')
- d_tokens: bfloat16 [128, 128, 24, 192], P('gx', 'gy')
- grad_qkv: float32 [192, 576], replicated
- grad_proj: float32 [192, 192], replicated
- grad_gain: float32 [192], replicated
- grad_bias: float32 [192], replicated
The draws below stay inside these ranges and needn't reach their ends.
All inputs are finite; a program needn't handle non-finite values.
Results may differ from the reference program's by a relative error of at most 0.005.
The reference program's roundings to bfloat16 on the way count: a program that leaves them out, or rounds other values in their place, can miss the bound.
Values may be sent and summed in bfloat16 or wider, within the bound.
No kernel may reach another device: no remote copies, remote signals or barrier semaphores. Data moves between devices by JAX's collectives and lax.ppermute only.
A program may use at most 192 MiB of HBM per device.

```python
import math
import jax
import jax.numpy as jnp
from jax import lax

C = 192
HEADS = 12
WIN = 8
NZ = 24
SHIFT = 4
NX = 128
NY = 128


def draw_tokens(key, part):
    key = jax.random.fold_in(key, 5)
    base_key = jax.random.fold_in(key, 0)
    base_draw = jax.random.normal(base_key, (NX, NY, NZ, C), jnp.float32)
    return jnp.clip(base_draw, -8.0, 8.0).astype(jnp.bfloat16)


def draw_qkv_weight(key, part):
    key = jax.random.fold_in(key, 7)
    weight_key = jax.random.fold_in(key, 0)
    scale = 2.0 / C ** 0.5
    weight_draw = jnp.clip(jax.random.normal(weight_key, (C, 3 * C), jnp.float32) * scale, -6.0 * scale, 6.0 * scale)
    return jnp.clip(weight_draw, -1.0, 1.0).astype(jnp.bfloat16)


def draw_cotangent(key, part):
    key = jax.random.fold_in(key, 11)
    normal_key = jax.random.fold_in(key, 0)
    ramp_x = jnp.arange(NX, dtype=jnp.float32) / max(NX - 1, 1)
    ramp_y = jnp.arange(NY, dtype=jnp.float32) / max(NY - 1, 1)
    ramp = jnp.exp((ramp_x[:, None] + ramp_y[None, :]) * 1.0986123) / 3.0
    ramp = ramp[:, :, None, None]
    base_draw = jax.random.normal(normal_key, (NX, NY, NZ, C), jnp.float32)
    return jnp.clip(base_draw * ramp, -12.0, 12.0).astype(jnp.bfloat16)


def scatter_about(stream_key, shape, width, most, kind=jnp.bfloat16):
    values = width * jax.random.normal(stream_key, shape, jnp.float32)
    return jnp.clip(values, min=-most, max=most).astype(kind)


def setup_inputs(seed: int = 0) -> dict:
    key_of = jax.random.split(jax.random.key(seed), 7)
    return {
        "tokens": draw_tokens(jax.random.fold_in(key_of[6], 71), 0),
        "cotangent": draw_cotangent(jax.random.fold_in(key_of[6], 71), 0),
        "ln_gain": jnp.clip(1.0 + 0.18 * jax.random.normal(key_of[2], (C,), jnp.float32), 0.1, 1.9),
        "ln_bias": scatter_about(key_of[3], (C,), 0.5, 3.0, jnp.float32),
        "qkv_weight": draw_qkv_weight(jax.random.fold_in(key_of[6], 71), 0),
        "proj_weight": scatter_about(key_of[5], (C, C), C ** -0.5, 0.4375),
    }


def window_rows(volume):
    size_x, size_y, size_z, features = volume.shape
    shaped = volume.reshape(size_x // WIN, WIN, size_y // WIN, WIN, size_z // WIN, WIN, features)
    return shaped.transpose(0, 2, 4, 1, 3, 5, 6).reshape(-1, WIN ** 3, features)

def volume_of(token_rows, size_x, size_y, size_z):
    features = token_rows.shape[-1]
    shaped = token_rows.reshape(size_x // WIN, size_y // WIN, size_z // WIN, WIN, WIN, WIN, features)
    return shaped.transpose(0, 3, 1, 4, 2, 5, 6).reshape(size_x, size_y, size_z, features)

def segment_ids(coord_x, coord_y, coord_z, volume_y, volume_z):
    segment_x = (coord_x + SHIFT) // WIN
    segment_y = (coord_y + SHIFT) // WIN
    segment_z = (coord_z + SHIFT) // WIN
    joined = (segment_x[:, None, None] * (volume_y // WIN + 1) + segment_y[None, :, None]) * (volume_z // WIN + 1)
    return (joined + segment_z[None, None, :]).astype(jnp.int32)

def layer_stats(token_float):
    row_mean = lax.optimization_barrier(jnp.mean(token_float, axis=-1, keepdims=True))
    centered = token_float - row_mean
    variance = lax.optimization_barrier(jnp.mean(centered * centered, axis=-1, keepdims=True))
    inverse_std = lax.rsqrt(variance + 1e-05)
    return (centered * inverse_std, inverse_std)

def attend_window(operands):
    projected, grad_mixed, window_ids = operands
    channels = projected.shape[-1] // 3
    head_dim = channels // HEADS
    score_scale = head_dim ** (-0.5)
    queries = projected[:, :channels].reshape(-1, HEADS, head_dim).astype(jnp.float32)
    key_rows = projected[:, channels:2 * channels].reshape(-1, HEADS, head_dim).astype(jnp.float32)
    value_rows = projected[:, 2 * channels:].reshape(-1, HEADS, head_dim).astype(jnp.float32)
    scores = jnp.einsum('qhd,khd->hqk', queries, key_rows) * score_scale
    same_segment = window_ids[:, None] == window_ids[None, :]
    scores = jnp.where(same_segment[None], scores, -1e+30)
    row_top = lax.optimization_barrier(jnp.max(scores, axis=-1, keepdims=True))
    expd = jnp.exp(scores - row_top)
    attention = expd / lax.optimization_barrier(jnp.sum(expd, axis=-1, keepdims=True))
    attention_b = lax.optimization_barrier(attention.astype(jnp.bfloat16)).astype(jnp.float32)
    mixed_rows = jnp.einsum('hqk,khd->qhd', attention_b, value_rows).astype(jnp.bfloat16).reshape(-1, channels)
    grad_out = grad_mixed.reshape(-1, HEADS, head_dim).astype(jnp.float32)
    grad_values = jnp.einsum('hqk,qhd->khd', attention_b, grad_out).astype(jnp.bfloat16)
    grad_attention = jnp.einsum('qhd,khd->hqk', grad_out, value_rows)
    inner_sum = lax.optimization_barrier(jnp.sum(attention * grad_attention, axis=-1, keepdims=True))
    grad_scores = (attention * (grad_attention - inner_sum) * score_scale).astype(jnp.bfloat16)
    grad_scores = lax.optimization_barrier(grad_scores).astype(jnp.float32)
    grad_queries = jnp.einsum('hqk,khd->qhd', grad_scores, key_rows).astype(jnp.bfloat16)
    grad_keys = jnp.einsum('hqk,qhd->khd', grad_scores, queries).astype(jnp.bfloat16)
    grad_projected = jnp.concatenate([grad_queries.reshape(-1, channels), grad_keys.reshape(-1, channels), grad_values.reshape(-1, channels)], axis=-1)
    return (mixed_rows, grad_projected)

def reference(tokens, cotangent, ln_gain, ln_bias, qkv_weight, proj_weight):
    rolled_x = jnp.roll(tokens, (-SHIFT, -SHIFT, -SHIFT), axis=(0, 1, 2))
    rolled_g = jnp.roll(cotangent, (-SHIFT, -SHIFT, -SHIFT), axis=(0, 1, 2))
    x_rows = window_rows(rolled_x).reshape(-1, C)
    g_rows = window_rows(rolled_g).reshape(-1, C)
    coord_x = (jnp.arange(NX, dtype=jnp.int32) + SHIFT) % NX
    coord_y = (jnp.arange(NY, dtype=jnp.int32) + SHIFT) % NY
    coord_z = (jnp.arange(NZ, dtype=jnp.int32) + SHIFT) % NZ
    window_count = NX * NY * NZ // WIN ** 3
    all_ids = window_rows(segment_ids(coord_x, coord_y, coord_z, NY, NZ)[..., None]).reshape(window_count, WIN ** 3)
    token_float = x_rows.astype(jnp.float32)
    standard, inverse_std = layer_stats(token_float)
    normed = (standard * ln_gain + ln_bias).astype(jnp.bfloat16)
    projected = jnp.dot(normed, qkv_weight, preferred_element_type=jnp.float32).astype(jnp.bfloat16)
    grad_mixed = jnp.dot(g_rows, proj_weight.T, preferred_element_type=jnp.float32).astype(jnp.bfloat16)
    mixed_rows, grad_projected = lax.map(attend_window, (projected.reshape(window_count, WIN ** 3, 3 * C), grad_mixed.reshape(window_count, WIN ** 3, C), all_ids))
    mixed_rows = mixed_rows.reshape(-1, C)
    grad_projected = grad_projected.reshape(-1, 3 * C)
    block_rows = (token_float + jnp.dot(mixed_rows, proj_weight, preferred_element_type=jnp.float32)).astype(jnp.bfloat16)
    grad_normed = jnp.dot(grad_projected, qkv_weight.T, preferred_element_type=jnp.float32)
    scaled = grad_normed * ln_gain
    grad_x = inverse_std * (scaled - lax.optimization_barrier(jnp.mean(scaled, axis=-1, keepdims=True)) - standard * lax.optimization_barrier(jnp.mean(scaled * standard, axis=-1, keepdims=True)))
    grad_rows = (g_rows.astype(jnp.float32) + grad_x).astype(jnp.bfloat16)
    factor = 1.0 / math.sqrt(NX * NY * NZ)
    grad_qkv = jnp.dot(normed.T, grad_projected, preferred_element_type=jnp.float32) * factor
    grad_proj = jnp.dot(mixed_rows.T, g_rows, preferred_element_type=jnp.float32) * factor
    grad_gain = lax.optimization_barrier(jnp.sum(grad_normed * standard, axis=0)) * factor
    grad_bias = lax.optimization_barrier(jnp.sum(grad_normed, axis=0)) * factor
    block_out = jnp.roll(volume_of(block_rows, NX, NY, NZ), (SHIFT, SHIFT, SHIFT), axis=(0, 1, 2))
    d_tokens = jnp.roll(volume_of(grad_rows, NX, NY, NZ), (SHIFT, SHIFT, SHIFT), axis=(0, 1, 2))
    return (block_out, d_tokens, grad_qkv, grad_proj, grad_gain, grad_bias)
```

```python
import functools
import math

import jax
import jax.numpy as jnp
from jax import lax
from jax.experimental import pallas as pl
from jax.experimental.pallas import tpu as pltpu
from jax.sharding import PartitionSpec as P

HEADS = 12
WIN = 8
SHIFT = 4
F32 = jnp.float32
BF16 = jnp.bfloat16
LOG2E = math.log2(math.e)
MASKED = 2.0**100

NT = (((1,), (1,)), ((), ()))
TN = (((0,), (0,)), ((), ()))


def dot(a, b):
    return jnp.dot(a, b, preferred_element_type=F32)


def attend_kernel(
    groups,
    x_ref,
    kf_ref,
    qf_ref,
    gain_ref,
    bias_ref,
    wqkv_t_ref,
    wqkv_ref,
    proj_ref,
    proj_t_ref,
    y_ref,
    dw_ref,
    dp_ref,
    dgb_ref,
    qkv_s,
    gm_s,
    mix_s,
    gqkv_s,
):
    channels = x_ref.shape[1]
    hd = channels // HEADS
    xf = x_ref[0].astype(F32)
    mean = jnp.mean(xf, axis=0, keepdims=True)
    centered = xf - mean
    var = jnp.mean(centered * centered, axis=0, keepdims=True)
    inv = lax.rsqrt(var + 1e-5)
    std = centered * inv
    gain = gain_ref[...]
    normed = (std * gain + bias_ref[...]).astype(BF16)
    qkv_s[...] = dot(wqkv_t_ref[...], normed).astype(BF16)
    g = x_ref[1]
    gm_s[...] = dot(proj_ref[...], g).astype(BF16)
    for start, size in groups:
        cols = slice(start, start + size)

        def head(h, carry):
            def rows(base):
                return pl.ds(pl.multiple_of(base + h * hd, hd), hd)

            q = qkv_s[rows(0), cols]
            k = qkv_s[rows(channels), cols]
            v = qkv_s[rows(2 * channels), cols]
            gm = gm_s[rows(0), cols]
            qf = q.astype(F32) * (hd**-0.5 * LOG2E)
            q_hi = qf.astype(BF16)
            q_lo = (qf - q_hi.astype(F32)).astype(BF16)
            ka = jnp.concatenate([k, k, kf_ref[:, cols]], axis=0)
            qa = jnp.concatenate([q_hi, q_lo, qf_ref[:, cols]], axis=0)
            s = lax.dot_general(ka, qa, TN, preferred_element_type=F32)
            e = jnp.exp2(s - jnp.max(s, axis=0, keepdims=True))
            p = e * (1.0 / jnp.sum(e, axis=0, keepdims=True))
            pb = p.astype(BF16)
            o = dot(v, pb)
            mix_s[rows(0), cols] = o.astype(BF16)
            dp = lax.dot_general(v, gm, TN, preferred_element_type=F32)
            inner = jnp.sum(p * dp, axis=0, keepdims=True)
            ds = (p * (dp - inner)).astype(BF16)
            gv = lax.dot_general(gm, pb, NT, preferred_element_type=F32)
            gq = dot(k, ds) * hd**-0.5
            gk = lax.dot_general(q, ds, NT, preferred_element_type=F32) * hd**-0.5
            gqkv_s[rows(0), cols] = gq.astype(BF16)
            gqkv_s[rows(channels), cols] = gk.astype(BF16)
            gqkv_s[rows(2 * channels), cols] = gv.astype(BF16)
            return carry

        lax.fori_loop(0, HEADS, head, 0, unroll=2)
    mixed = mix_s[...]
    y_ref[0] = (xf + dot(proj_t_ref[...], mixed)).astype(BF16)
    gqkv = gqkv_s[...]
    gn = dot(wqkv_ref[...], gqkv)
    scaled = gn * gain
    gx = inv * (
        scaled
        - jnp.mean(scaled, axis=0, keepdims=True)
        - std * jnp.mean(scaled * std, axis=0, keepdims=True)
    )
    y_ref[1] = (g.astype(F32) + gx).astype(BF16)
    dw_ref[...] = lax.dot_general(normed, gqkv, NT, preferred_element_type=F32)
    dp_ref[...] = lax.dot_general(mixed, g, NT, preferred_element_type=F32)
    dgb_ref[:, 0:1] = jnp.sum(gn * std, axis=1, keepdims=True)
    dgb_ref[:, 1:2] = jnp.sum(gn, axis=1, keepdims=True)


def attend(x, kf, qf, gain, bias, wqkv_t, wqkv, proj, proj_t, groups):
    _, channels, cells = x.shape
    vmem = pl.BlockSpec(memory_space=pltpu.VMEM)
    return pl.pallas_call(
        functools.partial(attend_kernel, groups),
        out_shape=(
            jax.ShapeDtypeStruct((2, channels, cells), BF16),
            jax.ShapeDtypeStruct((channels, 3 * channels), F32),
            jax.ShapeDtypeStruct((channels, channels), F32),
            jax.ShapeDtypeStruct((channels, 2), F32),
        ),
        in_specs=[vmem] * 9,
        out_specs=(vmem,) * 4,
        scratch_shapes=[
            pltpu.VMEM((3 * channels, cells), BF16),
            pltpu.VMEM((channels, cells), BF16),
            pltpu.VMEM((channels, cells), BF16),
            pltpu.VMEM((3 * channels, cells), BF16),
        ],
        compiler_params=pltpu.CompilerParams(vmem_limit_bytes=40 * 2**20),
        cost_estimate=pl.CostEstimate(
            flops=12 * 12 * 512 * 512 * 256, bytes_accessed=4 * 2**20, transcendentals=12 * 512 * 512
        ),
        name="attend",
    )(x, kf, qf, gain, bias, wqkv_t, wqkv, proj, proj_t)


def moved(block, step_x, step_y):
    nx, ny = lax.axis_size("gx"), lax.axis_size("gy")
    route = []
    for i in range(nx):
        for j in range(ny):
            to = ((i + step_x) % nx) * ny + (j + step_y) % ny
            route.append((i * ny + j, to))
    return lax.ppermute(block, ("gx", "gy"), route)


def summed(flat):
    nx, ny = lax.axis_size("gx"), lax.axis_size("gy")
    pieces = flat.reshape(ny, -1, flat.shape[-1])
    mine = jnp.sum(lax.all_to_all(pieces, "gy", 0, 0), axis=0)
    spread = jnp.broadcast_to(mine[None], (nx, *mine.shape))
    total = jnp.sum(lax.all_to_all(spread, "gx", 0, 0), axis=0)
    spread = jnp.broadcast_to(total[None], (ny, *total.shape))
    return lax.all_to_all(spread, "gy", 0, 0).reshape(flat.shape)


def shards(tokens, cotangent, ln_gain, ln_bias, qkv_weight, proj_weight):
    tile_x, tile_y, depth, channels = tokens.shape
    nx, ny = lax.axis_size("gx"), lax.axis_size("gy")
    windows = depth // WIN
    half = WIN // 2
    quarter = SHIFT * SHIFT * half
    both = jnp.roll(jnp.stack([tokens, cotangent]), -SHIFT, axis=3)
    both = both.reshape(2, 2, SHIFT, 2, SHIFT, windows, 2, half, channels)
    packed = both.transpose(5, 1, 3, 0, 8, 6, 2, 4, 7)
    packed = packed.reshape(windows, 2, 2, 2, channels, 2, quarter)

    lane = jnp.arange(4 * 2 * quarter, dtype=jnp.int32)
    quad = (lane // quarter) % 4
    far_x = jnp.where((quad % 2 == 1) & (lax.axis_index("gx") == nx - 1), 1.0, 0.0)
    far_y = jnp.where((quad // 2 == 1) & (lax.axis_index("gy") == ny - 1), 1.0, 0.0)
    zero = jnp.zeros_like(far_x)
    kf = jnp.stack([far_x, 1 - far_x, far_y, 1 - far_y] + [zero] * 12).astype(BF16)
    qf = jnp.stack([far_x - 1, -far_x, far_y - 1, -far_y] + [zero] * 12) * MASKED
    qf = qf.astype(BF16)

    gain, bias = ln_gain[:, None], ln_bias[:, None]
    wqkv_t, proj_t = qkv_weight.T, proj_weight.T

    inputs = []
    for w in range(windows):
        quads = [
            packed[w, 1, 1],
            moved(packed[w, 0, 1], -1, 0),
            moved(packed[w, 1, 0], 0, -1),
            moved(packed[w, 0, 0], -1, -1),
        ]
        inputs.append(jnp.stack(quads, axis=3).reshape(2, channels, -1))
    outs = []
    sums = None
    for w in range(windows):
        cells = inputs[w].shape[-1]
        groups = ((0, cells),) if w < windows - 1 else ((0, cells // 2), (cells // 2, cells // 2))
        y, *partial = attend(
            inputs[w], kf, qf, gain, bias, wqkv_t, qkv_weight, proj_weight, proj_t, groups
        )
        sums = partial if sums is None else [a + b for a, b in zip(sums, partial)]
        y = y.reshape(2, channels, 2, 4, quarter)
        own = y[:, :, :, 0]
        from_x = moved(y[:, :, :, 1], 1, 0)
        from_y = moved(y[:, :, :, 2], 0, 1)
        from_xy = moved(y[:, :, :, 3], 1, 1)
        outs.append(jnp.stack([jnp.stack([from_xy, from_x]), jnp.stack([from_y, own])]))
    out = jnp.stack(outs).reshape(windows, 2, 2, 2, channels, 2, SHIFT, SHIFT, half)
    out = out.transpose(3, 1, 6, 2, 7, 0, 5, 8, 4).reshape(2, tile_x, tile_y, depth, channels)
    out = jnp.roll(out, SHIFT, axis=3)

    flat = jnp.concatenate([s.reshape(-1) for s in sums])
    count = flat.shape[0]
    unit = 128 * ny
    flat = jnp.pad(flat, (0, -count % unit)).reshape(-1, 128)
    total = summed(flat).reshape(-1)[:count]
    factor = 1.0 / math.sqrt(tile_x * nx * tile_y * ny * depth)
    total = total * factor
    n1 = 3 * channels * channels
    n2 = n1 + channels * channels
    grads = total[n2:].reshape(channels, 2)
    return (
        out[0],
        out[1],
        total[:n1].reshape(channels, 3 * channels),
        total[n1:n2].reshape(channels, channels),
        grads[:, 0],
        grads[:, 1],
    )


def solution(mesh):
    placed = (P("gx", "gy", None, None), P("gx", "gy", None, None), P(), P(), P(), P())
    return jax.shard_map(
        shards,
        mesh=mesh,
        in_specs=placed,
        out_specs=(P("gx", "gy", None, None), P("gx", "gy", None, None), P(), P(), P(), P()),
        check_vma=False,
    )
```

```python
import functools
import math

import jax
import jax.numpy as jnp
from jax import lax
from jax.experimental import pallas as pl
from jax.experimental.pallas import tpu as pltpu
from jax.sharding import PartitionSpec as P

HEADS = 12
WIN = 8
SHIFT = 4
F32 = jnp.float32
BF16 = jnp.bfloat16
LOG2E = math.log2(math.e)
MASKED = 2.0**100
LANES = 128
VMEM = pl.BlockSpec(memory_space=pltpu.VMEM)

NT = (((1,), (1,)), ((), ()))
TN = (((0,), (0,)), ((), ()))


def dot(a, b):
    return jnp.dot(a, b, preferred_element_type=F32)


def pieces_of(block):
    channels = block.shape[-1]
    pieces = {}
    for xh in range(2):
        for yh in range(2):
            quad = block[xh * 4 : xh * 4 + 4, yh * 4 : yh * 4 + 4].reshape(16, 24, channels)
            first = quad[:, 4:12].reshape(LANES, channels)
            second = quad[:, 12:20].reshape(LANES, channels)
            pairs = quad.reshape(8, 2, 24, channels)
            high = jnp.concatenate([pairs[:, 0, 20:24], pairs[:, 1, 20:24]], axis=1)
            low = jnp.concatenate([pairs[:, 0, 0:4], pairs[:, 1, 0:4]], axis=1)
            last = jnp.concatenate([high.reshape(64, channels), low.reshape(64, channels)], axis=0)
            pieces[xh, yh] = [piece.T.astype(BF16) for piece in (first, second, last)]
    return pieces


def quadrant_of(first, second, last):
    channels = first.shape[0]
    first = first.astype(F32).T.reshape(16, 8, channels)
    second = second.astype(F32).T.reshape(16, 8, channels)
    last = last.astype(F32).T
    high = last[:64].reshape(8, 8, channels)
    low = last[64:].reshape(8, 8, channels)
    even = jnp.concatenate([low[:, 0:4]], axis=1)
    odd = low[:, 4:8]
    low = jnp.stack([even, odd], axis=1).reshape(16, 4, channels)
    high = jnp.stack([high[:, 0:4], high[:, 4:8]], axis=1).reshape(16, 4, channels)
    whole = jnp.concatenate([low, first, second, high], axis=1)
    return whole.reshape(4, 4, 24, channels).astype(BF16)


def pack_kernel(
    tokens_ref, cot_ref, gain_ref, bias_ref, wqkv_ref, proj_ref,
    *outs,
):
    piece_refs, (gain_out, bias_out, wqkv_t_out, proj_t_out, kf_out, qf_out) = outs[:12], outs[12:]
    for which, ref in enumerate((tokens_ref, cot_ref)):
        pieces = pieces_of(ref[...].astype(F32))
        for xh in range(2):
            for yh in range(2):
                for w in range(3):
                    piece_refs[w * 4 + xh * 2 + yh][which] = pieces[xh, yh][w]
    gain_out[...] = gain_ref[...].T
    bias_out[...] = bias_ref[...].T
    wqkv_t_out[...] = wqkv_ref[...].astype(F32).T.astype(BF16)
    proj_t_out[...] = proj_ref[...].astype(F32).T.astype(BF16)
    edge_x = lax.axis_index("gx") == lax.axis_size("gx") - 1
    edge_y = lax.axis_index("gy") == lax.axis_size("gy") - 1
    shape = kf_out.shape[1:]
    row = lax.broadcasted_iota(jnp.int32, shape, 0)
    lane = lax.broadcasted_iota(jnp.int32, shape, 1)
    for layout, span in enumerate((LANES, LANES // 2)):
        quad = (lane // span) % 4
        far_x = jnp.where(jnp.logical_and(quad // 2 == 0, edge_x), 1.0, 0.0)
        far_y = jnp.where(jnp.logical_and(quad % 2 == 0, edge_y), 1.0, 0.0)
        key = jnp.where(row == 0, far_x, jnp.where(row == 1, 1 - far_x, jnp.where(row == 2, far_y, 1 - far_y)))
        query = jnp.where(row == 0, 1 - far_x, jnp.where(row == 1, far_x, jnp.where(row == 2, 1 - far_y, far_y)))
        kf_out[layout] = jnp.where(row < 4, key, 0.0).astype(BF16)
        qf_out[layout] = jnp.where(row < 4, query * -MASKED, 0.0).astype(BF16)


def packed(tokens, cotangent, gain, bias, wqkv, proj):
    channels = tokens.shape[-1]
    cells = 4 * LANES
    S = jax.ShapeDtypeStruct
    return pl.pallas_call(
        pack_kernel,
        out_shape=(S((2, channels, LANES), BF16),) * 12
        + (
            S((channels, 1), F32),
            S((channels, 1), F32),
            S((3 * channels, channels), BF16),
            S((channels, channels), BF16),
            S((2, 16, cells), BF16),
            S((2, 16, cells), BF16),
        ),
        in_specs=[VMEM] * 6,
        out_specs=(VMEM,) * 18,
        compiler_params=pltpu.CompilerParams(vmem_limit_bytes=40 * 2**20),
        name="pack",
    )(tokens, cotangent, gain[None], bias[None], wqkv, proj)


def unpack_kernel(*refs):
    pieces, outs = refs[:12], refs[12:]
    for which, out in enumerate(outs):
        for xh in range(2):
            for yh in range(2):
                quad = quadrant_of(*(pieces[w * 4 + xh * 2 + yh][which] for w in range(3)))
                out[xh * 4 : xh * 4 + 4, yh * 4 : yh * 4 + 4] = quad


def unpacked(pieces, shape):
    return pl.pallas_call(
        unpack_kernel,
        out_shape=(jax.ShapeDtypeStruct(shape, BF16),) * 2,
        in_specs=[VMEM] * 12,
        out_specs=(VMEM,) * 2,
        compiler_params=pltpu.CompilerParams(vmem_limit_bytes=40 * 2**20),
        name="unpack",
    )(*pieces)


def attend_kernel(
    halves, last,
    q00_ref, q01_ref, q10_ref, q11_ref,
    kf_ref, qf_ref, gain_ref, bias_ref, wqkv_t_ref, wqkv_ref, proj_ref, proj_t_ref, sums_ref,
    y00_ref, y01_ref, y10_ref, y11_ref, grads_ref,
    qkv_s, gm_s, mix_s, gqkv_s,
):
    quads = (q00_ref, q01_ref, q10_ref, q11_ref)
    channels = q00_ref.shape[1]
    hd = channels // HEADS
    cells = 4 * LANES
    half = LANES // 2

    def whole(which):
        if halves:
            parts = [q[which].astype(F32) for q in quads]
            return jnp.concatenate(
                [p[:, :half] for p in parts] + [p[:, half:] for p in parts], axis=1
            )
        return jnp.concatenate([q[which].astype(F32) for q in quads], axis=1)

    xf = whole(0)
    gf = whole(1)
    g = gf.astype(BF16)
    mean = jnp.mean(xf, axis=0, keepdims=True)
    centered = xf - mean
    var = jnp.mean(centered * centered, axis=0, keepdims=True)
    inv = lax.rsqrt(var + 1e-5)
    std = centered * inv
    gain = gain_ref[...]
    normed = (std * gain + bias_ref[...]).astype(BF16)
    qkv_s[...] = dot(wqkv_t_ref[...], normed).astype(BF16)
    gm_s[...] = dot(proj_ref[...], g).astype(BF16)
    size = cells // 2 if halves else cells
    for start in range(0, cells, size):
        cols = slice(start, start + size)
        layout = 1 if halves else 0

        def head(h, carry):
            def rows(base):
                return pl.ds(pl.multiple_of(base + h * hd, hd), hd)

            q = qkv_s[rows(0), cols]
            k = qkv_s[rows(channels), cols]
            v = qkv_s[rows(2 * channels), cols]
            gm = gm_s[rows(0), cols]
            qf = q.astype(F32) * (hd**-0.5 * LOG2E)
            q_hi = qf.astype(BF16)
            q_lo = (qf - q_hi.astype(F32)).astype(BF16)
            ka = jnp.concatenate([k, k, kf_ref[layout, :, cols]], axis=0)
            qa = jnp.concatenate([q_hi, q_lo, qf_ref[layout, :, cols]], axis=0)
            s = lax.dot_general(ka, qa, TN, preferred_element_type=F32)
            e = jnp.exp2(s - jnp.max(s, axis=0, keepdims=True))
            p = e * (1.0 / jnp.sum(e, axis=0, keepdims=True))
            pb = p.astype(BF16)
            o = dot(v, pb)
            mix_s[rows(0), cols] = o.astype(BF16)
            dp = lax.dot_general(v, gm, TN, preferred_element_type=F32)
            inner = jnp.sum(p * dp, axis=0, keepdims=True)
            ds = (p * (dp - inner)).astype(BF16)
            gv = lax.dot_general(gm, pb, NT, preferred_element_type=F32)
            gq = dot(k, ds) * hd**-0.5
            gk = lax.dot_general(q, ds, NT, preferred_element_type=F32) * hd**-0.5
            gqkv_s[rows(0), cols] = gq.astype(BF16)
            gqkv_s[rows(channels), cols] = gk.astype(BF16)
            gqkv_s[rows(2 * channels), cols] = gv.astype(BF16)
            return carry

        lax.fori_loop(0, HEADS, head, 0, unroll=2)
    mixed = mix_s[...]
    block_out = xf + dot(proj_t_ref[...], mixed)
    gqkv = gqkv_s[...]
    gn = dot(wqkv_ref[...], gqkv)
    scaled = gn * gain
    gx = inv * (
        scaled
        - jnp.mean(scaled, axis=0, keepdims=True)
        - std * jnp.mean(scaled * std, axis=0, keepdims=True)
    )
    d_tokens = gf + gx
    for which, y in enumerate((block_out, d_tokens)):
        for i, ref in enumerate((y00_ref, y01_ref, y10_ref, y11_ref)):
            if halves:
                lo = y[:, i * half : (i + 1) * half]
                hi = y[:, cells // 2 + i * half : cells // 2 + (i + 1) * half]
                part = jnp.concatenate([lo, hi], axis=1)
            else:
                part = y[:, i * LANES : (i + 1) * LANES]
            ref[which] = part.astype(BF16)

    dw = lax.dot_general(normed, gqkv, NT, preferred_element_type=F32)
    dproj = lax.dot_general(mixed, g, NT, preferred_element_type=F32)
    dgain = jnp.sum(gn * std, axis=1, keepdims=True)
    dbias = jnp.sum(gn, axis=1, keepdims=True)
    joined = jnp.concatenate([dw, dproj], axis=1)
    blocks = [joined[:, i * LANES : (i + 1) * LANES] for i in range(joined.shape[1] // LANES)]
    lane = lax.broadcasted_iota(jnp.int32, (channels, LANES), 1)
    tail = jnp.where(lane == 0, dgain, jnp.where(lane == 1, dbias, 0.0)).T[:8]
    used = len(blocks) * channels
    grads = jnp.concatenate(blocks, axis=0) + sums_ref[:used]
    extra = jnp.concatenate(
        [tail[:, :LANES], jnp.pad(tail[:, LANES:], ((0, 0), (0, 2 * LANES - channels)))], axis=0
    ) + sums_ref[used : used + 16]
    grads_ref[:used] = grads.astype(grads_ref.dtype)
    grads_ref[used : used + 16] = extra.astype(grads_ref.dtype)
    grads_ref[used + 16 :] = jnp.zeros(
        (grads_ref.shape[0] - used - 16, LANES), grads_ref.dtype
    )


GRAD_ROWS = 1280


def attend(quads, features, gain, bias, wqkv_t, wqkv, proj, proj_t, sums, halves, last):
    channels = quads[0].shape[1]
    cells = 4 * LANES
    S = jax.ShapeDtypeStruct
    return pl.pallas_call(
        functools.partial(attend_kernel, halves, last),
        out_shape=(S((2, channels, LANES), BF16),) * 4
        + (S((GRAD_ROWS, LANES), BF16 if last else F32),),
        in_specs=[VMEM] * 13,
        out_specs=(VMEM,) * 5,
        scratch_shapes=[
            pltpu.VMEM((3 * channels, cells), BF16),
            pltpu.VMEM((channels, cells), BF16),
            pltpu.VMEM((channels, cells), BF16),
            pltpu.VMEM((3 * channels, cells), BF16),
        ],
        compiler_params=pltpu.CompilerParams(vmem_limit_bytes=40 * 2**20),
        cost_estimate=pl.CostEstimate(
            flops=12 * 12 * 512 * 512 * 256, bytes_accessed=4 * 2**20, transcendentals=12 * 512 * 512
        ),
        name="attend",
    )(*quads, *features, gain, bias, wqkv_t, wqkv, proj, proj_t, sums)


def moved(block, step_x, step_y):
    nx, ny = lax.axis_size("gx"), lax.axis_size("gy")
    route = []
    for i in range(nx):
        for j in range(ny):
            to = ((i + step_x) % nx) * ny + (j + step_y) % ny
            route.append((i * ny + j, to))
    return lax.ppermute(block, ("gx", "gy"), route)


def summed(rows):
    nx, ny = lax.axis_size("gx"), lax.axis_size("gy")
    pieces = rows.reshape(ny, -1, LANES)
    got = lax.all_to_all(pieces, "gy", 0, 0)
    mine = jnp.sum(got.astype(F32), axis=0)
    got = lax.all_to_all(jnp.broadcast_to(mine[None], (nx, *mine.shape)), "gx", 0, 0)
    total = jnp.sum(got, axis=0)
    got = lax.all_to_all(jnp.broadcast_to(total[None], (ny, *total.shape)), "gy", 0, 0)
    return got.reshape(rows.shape)


def grads_kernel(factor, rows_ref, dw_ref, dproj_ref, gain_ref, bias_ref):
    channels = dw_ref.shape[0]
    blocks = 4 * channels // LANES
    joined = jnp.concatenate(
        [rows_ref[i * channels : (i + 1) * channels] for i in range(blocks)], axis=1
    ) * factor
    dw_ref[...] = joined[:, : 3 * channels]
    dproj_ref[...] = joined[:, 3 * channels :]
    used = blocks * channels
    tail = rows_ref[used : used + 16] * factor
    tail = jnp.concatenate([tail[:8], tail[8:]], axis=1)[:, :channels]
    gain_ref[...] = tail[0:1]
    bias_ref[...] = tail[1:2]


def grads_of(rows, channels, factor):
    S = jax.ShapeDtypeStruct
    return pl.pallas_call(
        functools.partial(grads_kernel, factor),
        out_shape=(
            S((channels, 3 * channels), F32),
            S((channels, channels), F32),
            S((1, channels), F32),
            S((1, channels), F32),
        ),
        in_specs=[VMEM],
        out_specs=(VMEM,) * 4,
        name="unpack_grads",
    )(rows)


def shards(tokens, cotangent, ln_gain, ln_bias, qkv_weight, proj_weight):
    tile_x, tile_y, depth, channels = tokens.shape
    nx, ny = lax.axis_size("gx"), lax.axis_size("gy")
    windows = depth // WIN
    *pieces, gain, bias, wqkv_t, proj_t, kf, qf = packed(
        tokens, cotangent, ln_gain, ln_bias, qkv_weight, proj_weight
    )
    inputs = []
    for w in range(windows):
        p00, p01, p10, p11 = pieces[w * 4 : w * 4 + 4]
        inputs.append([moved(p00, -1, -1), moved(p01, -1, 0), moved(p10, 0, -1), p11])
    back = []
    sums = jnp.zeros((GRAD_ROWS, LANES), F32)
    for w in range(windows):
        last = w == windows - 1
        if w >= 2:
            inputs[w], back[w - 2] = lax.optimization_barrier((inputs[w], back[w - 2]))
        *ys, sums = attend(
            inputs[w], (kf, qf), gain, bias, wqkv_t, qkv_weight, proj_weight, proj_t, sums,
            halves=last, last=last,
        )
        back.append([moved(ys[0], 1, 1), moved(ys[1], 1, 0), moved(ys[2], 0, 1), ys[3]])
    sums, back[1] = lax.optimization_barrier((sums, back[1]))
    total = summed(sums)
    block_out, d_tokens = unpacked([piece for quads in back for piece in quads], tokens.shape)
    factor = 1.0 / math.sqrt(tile_x * nx * tile_y * ny * depth)
    dw, dproj, dgain, dbias = grads_of(total, channels, factor)
    return block_out, d_tokens, dw, dproj, dgain[0], dbias[0]


def solution(mesh):
    placed = (P("gx", "gy", None, None), P("gx", "gy", None, None), P(), P(), P(), P())
    return jax.shard_map(
        shards,
        mesh=mesh,
        in_specs=placed,
        out_specs=(P("gx", "gy", None, None), P("gx", "gy", None, None), P(), P(), P(), P()),
        check_vma=False,
    )
```

```python
import functools
import math

import jax
import jax.numpy as jnp
from jax import lax
from jax.experimental import pallas as pl
from jax.experimental.pallas import tpu as pltpu
from jax.sharding import PartitionSpec as P

HEADS = 12
WIN = 8
SHIFT = 4
F32 = jnp.float32
BF16 = jnp.bfloat16
LOG2E = math.log2(math.e)
MASKED = 2.0**100
LANES = 128
VMEM = pl.BlockSpec(memory_space=pltpu.VMEM)

NT = (((1,), (1,)), ((), ()))
TN = (((0,), (0,)), ((), ()))


def dot(a, b):
    return jnp.dot(a, b, preferred_element_type=F32)


def pieces_of(block):
    channels = block.shape[-1]
    pieces = {}
    for xh in range(2):
        for yh in range(2):
            quad = block[xh * 4 : xh * 4 + 4, yh * 4 : yh * 4 + 4].reshape(16, 24, channels)
            first = quad[:, 4:12].reshape(LANES, channels)
            second = quad[:, 12:20].reshape(LANES, channels)
            pairs = quad.reshape(8, 2, 24, channels)
            high = jnp.concatenate([pairs[:, 0, 20:24], pairs[:, 1, 20:24]], axis=1)
            low = jnp.concatenate([pairs[:, 0, 0:4], pairs[:, 1, 0:4]], axis=1)
            last = jnp.concatenate([high.reshape(64, channels), low.reshape(64, channels)], axis=0)
            pieces[xh, yh] = [piece.T.astype(BF16) for piece in (first, second, last)]
    return pieces


def quadrant_of(first, second, last):
    channels = first.shape[0]
    first = first.astype(F32).T.reshape(16, 8, channels)
    second = second.astype(F32).T.reshape(16, 8, channels)
    last = last.astype(F32).T
    high = last[:64].reshape(8, 8, channels)
    low = last[64:].reshape(8, 8, channels)
    even = jnp.concatenate([low[:, 0:4]], axis=1)
    odd = low[:, 4:8]
    low = jnp.stack([even, odd], axis=1).reshape(16, 4, channels)
    high = jnp.stack([high[:, 0:4], high[:, 4:8]], axis=1).reshape(16, 4, channels)
    whole = jnp.concatenate([low, first, second, high], axis=1)
    return whole.reshape(4, 4, 24, channels).astype(BF16)


def pack_kernel(
    tokens_ref, cot_ref, gain_ref, bias_ref, wqkv_ref, proj_ref,
    *outs,
):
    piece_refs, (gain_out, bias_out, wqkv_t_out, proj_t_out, kf_out, qf_out) = outs[:12], outs[12:]
    for which, ref in enumerate((tokens_ref, cot_ref)):
        pieces = pieces_of(ref[...].astype(F32))
        for xh in range(2):
            for yh in range(2):
                for w in range(3):
                    piece_refs[w * 4 + xh * 2 + yh][which] = pieces[xh, yh][w]
    gain_out[...] = gain_ref[...].T
    bias_out[...] = bias_ref[...].T
    wqkv_t_out[...] = wqkv_ref[...].astype(F32).T.astype(BF16)
    proj_t_out[...] = proj_ref[...].astype(F32).T.astype(BF16)
    edge_x = lax.axis_index("gx") == lax.axis_size("gx") - 1
    edge_y = lax.axis_index("gy") == lax.axis_size("gy") - 1
    shape = kf_out.shape[1:]
    row = lax.broadcasted_iota(jnp.int32, shape, 0)
    lane = lax.broadcasted_iota(jnp.int32, shape, 1)
    for layout, span in enumerate((LANES, LANES // 2)):
        quad = (lane // span) % 4
        far_x = jnp.where(jnp.logical_and(quad // 2 == 0, edge_x), 1.0, 0.0)
        far_y = jnp.where(jnp.logical_and(quad % 2 == 0, edge_y), 1.0, 0.0)
        key = jnp.where(row == 0, far_x, jnp.where(row == 1, 1 - far_x, jnp.where(row == 2, far_y, 1 - far_y)))
        query = jnp.where(row == 0, 1 - far_x, jnp.where(row == 1, far_x, jnp.where(row == 2, 1 - far_y, far_y)))
        kf_out[layout] = jnp.where(row < 4, key, 0.0).astype(BF16)
        qf_out[layout] = jnp.where(row < 4, query * -MASKED, 0.0).astype(BF16)


def packed(tokens, cotangent, gain, bias, wqkv, proj):
    channels = tokens.shape[-1]
    cells = 4 * LANES
    S = jax.ShapeDtypeStruct
    return pl.pallas_call(
        pack_kernel,
        out_shape=(S((2, channels, LANES), BF16),) * 12
        + (
            S((channels, 1), F32),
            S((channels, 1), F32),
            S((3 * channels, channels), BF16),
            S((channels, channels), BF16),
            S((2, 16, cells), BF16),
            S((2, 16, cells), BF16),
        ),
        in_specs=[VMEM] * 6,
        out_specs=(VMEM,) * 18,
        compiler_params=pltpu.CompilerParams(vmem_limit_bytes=40 * 2**20),
        name="pack",
    )(tokens, cotangent, gain[None], bias[None], wqkv, proj)


def unpack_kernel(*refs):
    pieces, outs = refs[:12], refs[12:]
    for which, out in enumerate(outs):
        for xh in range(2):
            for yh in range(2):
                quad = quadrant_of(*(pieces[w * 4 + xh * 2 + yh][which] for w in range(3)))
                out[xh * 4 : xh * 4 + 4, yh * 4 : yh * 4 + 4] = quad


def unpacked(pieces, shape):
    return pl.pallas_call(
        unpack_kernel,
        out_shape=(jax.ShapeDtypeStruct(shape, BF16),) * 2,
        in_specs=[VMEM] * 12,
        out_specs=(VMEM,) * 2,
        compiler_params=pltpu.CompilerParams(vmem_limit_bytes=40 * 2**20),
        name="unpack",
    )(*pieces)


def attend_kernel(
    halves, last,
    q00_ref, q01_ref, q10_ref, q11_ref,
    kf_ref, qf_ref, gain_ref, bias_ref, wqkv_t_ref, wqkv_ref, proj_ref, proj_t_ref, sums_ref,
    y00_ref, y01_ref, y10_ref, y11_ref, grads_ref,
    qkv_s, gm_s, mix_s, gqkv_s, kv_s, qa_s, ga_s, e_s, pb_s, dp_s, ds_s, r_s, d_s,
):
    quads = (q00_ref, q01_ref, q10_ref, q11_ref)
    channels = q00_ref.shape[1]
    hd = channels // HEADS
    cells = 4 * LANES
    half = LANES // 2

    def whole(which):
        if halves:
            parts = [q[which].astype(F32) for q in quads]
            return jnp.concatenate(
                [p[:, :half] for p in parts] + [p[:, half:] for p in parts], axis=1
            )
        return jnp.concatenate([q[which].astype(F32) for q in quads], axis=1)

    xf = whole(0)
    gf = whole(1)
    g = gf.astype(BF16)
    mean = jnp.mean(xf, axis=0, keepdims=True)
    centered = xf - mean
    var = jnp.mean(centered * centered, axis=0, keepdims=True)
    inv = lax.rsqrt(var + 1e-5)
    std = centered * inv
    gain = gain_ref[...]
    normed = (std * gain + bias_ref[...]).astype(BF16)
    qkv = dot(wqkv_t_ref[...], normed).astype(BF16)
    qkv_s[...] = qkv
    gm_s[...] = dot(proj_ref[...], g).astype(BF16)

    layout = 1 if halves else 0
    size = cells // 2 if halves else cells
    groups = [slice(start, start + size) for start in range(0, cells, size)]
    step_rows = 64 * (cells // size)
    chunks = [
        (gi, slice(c, c + step_rows), group)
        for gi, group in enumerate(groups)
        for c in range(group.start, group.stop, step_rows)
    ]
    scale = hd**-0.5

    def head_rows(base, h):
        if isinstance(h, int):
            return slice(base + h * hd, base + (h + 1) * hd)
        return pl.ds(pl.multiple_of(base + h * hd, hd), hd)

    def q_rows(h):
        return head_rows(0, h)

    def k_rows(h):
        return head_rows(channels, h)

    def v_rows(h):
        return head_rows(2 * channels, h)

    def folded(x):
        return jnp.sum(x.reshape(-1, 8, x.shape[-1]), axis=0)

    def added(total, gi, x):
        total[gi] = x if total[gi] is None else total[gi] + x

    def prepare(h, slot):
        k = qkv_s[k_rows(h)]
        qf = qkv_s[q_rows(h)].astype(F32) * (scale * LOG2E)
        q_hi = qf.astype(BF16)
        q_lo = (qf - q_hi.astype(F32)).astype(BF16)
        none = jnp.zeros_like(k)
        kv_s[slot] = jnp.concatenate([k, k, kf_ref[layout], qkv_s[v_rows(h)]], axis=0).T
        qa_s[slot] = jnp.concatenate([q_hi, q_lo, qf_ref[layout], none], axis=0)
        ga_s[slot] = jnp.concatenate([none, none, none, gm_s[q_rows(h)]], axis=0)

    def exponentials(slot, chunk, total):
        gi, rows, cols = chunk
        e = jnp.exp2(dot(kv_s[slot, rows], qa_s[slot, :, cols]))
        e_s[slot, rows] = e
        added(total, gi, folded(e))

    def attention(slot, chunk, total):
        gi, rows, cols = chunk
        p = e_s[slot, rows] * r_s[slot, 0:1, cols]
        e_s[slot, rows] = p
        pb_s[rows] = p.astype(BF16)
        dp = dot(kv_s[slot, rows], ga_s[slot, :, cols])
        dp_s[rows] = dp
        added(total, gi, folded(p * dp))

    def grad_scores(slot, chunk):
        _, rows, cols = chunk
        ds_s[slot, rows] = (e_s[slot, rows] * (dp_s[rows] - d_s[0:1, cols])).astype(BF16)

    def mixed_of(h):
        for cols in groups:
            mix_s[q_rows(h), cols] = dot(qkv_s[v_rows(h), cols], pb_s[cols]).astype(BF16)

    def grad_values_of(h):
        for cols in groups:
            gv = lax.dot_general(gm_s[q_rows(h), cols], pb_s[cols], NT, preferred_element_type=F32)
            gqkv_s[v_rows(h), cols] = gv.astype(BF16)

    def grad_queries_of(h, slot):
        for cols in groups:
            gq = dot(qkv_s[k_rows(h), cols], ds_s[slot, cols]) * scale
            gqkv_s[q_rows(h), cols] = gq.astype(BF16)

    def grad_keys_of(h, slot):
        for cols in groups:
            gk = lax.dot_general(
                qkv_s[q_rows(h), cols], ds_s[slot, cols], NT, preferred_element_type=F32
            )
            gqkv_s[k_rows(h), cols] = (gk * scale).astype(BF16)

    def keep_inverse(slot, total):
        for gi, cols in enumerate(groups):
            r_s[slot, 0:1, cols] = 1.0 / jnp.sum(total[gi], axis=0, keepdims=True)

    def step(i, slot, first=True, final=True, ahead=True):
        sums = [None] * len(groups)
        inner = [None] * len(groups)
        count = len(chunks)
        for c, chunk in enumerate(chunks):
            if first:
                exponentials(slot, chunk, sums)
            attention(1 - slot, chunk, inner)
            if final and c == count // 4:
                grad_queries_of(i - 2, slot)
            if final and c == 3 * count // 4:
                grad_keys_of(i - 2, slot)
        if first:
            keep_inverse(slot, sums)
        for gi, cols in enumerate(groups):
            d_s[0:1, cols] = jnp.sum(inner[gi], axis=0, keepdims=True)
        for c, chunk in enumerate(chunks):
            grad_scores(1 - slot, chunk)
            if c == 0:
                mixed_of(i - 1)
            if c == count // 2:
                grad_values_of(i - 1)
        if ahead:
            prepare(i + 1, 1 - slot)

    squares = jnp.square(qkv[: 2 * channels].astype(F32)).reshape(2 * HEADS, hd, cells)
    longest = jnp.max(jnp.sum(squares, axis=1), axis=1, keepdims=True)
    bound = jnp.max(longest[:HEADS] * longest[HEADS:]) * (scale * LOG2E) ** 2
    in_range = bound <= 110.0**2

    @pl.when(in_range)
    def _():
        prepare(0, 0)
        prepare(1, 1)
        sums = [None] * len(groups)
        for chunk in chunks:
            exponentials(0, chunk, sums)
        keep_inverse(0, sums)
        step(1, 1, final=False)

        def two_steps(j, carry):
            step(2 + 2 * j, 0)
            step(3 + 2 * j, 1)
            return carry

        lax.fori_loop(0, (HEADS - 4) // 2, two_steps, 0)
        step(HEADS - 2, 0)
        step(HEADS - 1, 1, ahead=False)
        step(HEADS, 0, first=False, ahead=False)
        grad_queries_of(HEADS - 1, 1)
        grad_keys_of(HEADS - 1, 1)

    @pl.when(jnp.logical_not(in_range))
    def _():
        def head(h, carry):
            prepare(h, 0)
            for cols in groups:
                s = dot(kv_s[0, cols], qa_s[0, :, cols])
                e = jnp.exp2(s - jnp.max(s, axis=0, keepdims=True))
                p = e * (1.0 / jnp.sum(e, axis=0, keepdims=True))
                pb_s[cols] = p.astype(BF16)
                dp = dot(kv_s[0, cols], ga_s[0, :, cols])
                inner = jnp.sum(p * dp, axis=0, keepdims=True)
                ds_s[0, cols] = (p * (dp - inner)).astype(BF16)
            mixed_of(h)
            grad_values_of(h)
            grad_queries_of(h, 0)
            grad_keys_of(h, 0)
            return carry

        lax.fori_loop(0, HEADS, head, 0)

    mixed = mix_s[...]
    block_out = xf + dot(proj_t_ref[...], mixed)
    gqkv = gqkv_s[...]
    gn = dot(wqkv_ref[...], gqkv)
    scaled = gn * gain
    gx = inv * (
        scaled
        - jnp.mean(scaled, axis=0, keepdims=True)
        - std * jnp.mean(scaled * std, axis=0, keepdims=True)
    )
    d_tokens = gf + gx
    for which, y in enumerate((block_out, d_tokens)):
        for i, ref in enumerate((y00_ref, y01_ref, y10_ref, y11_ref)):
            if halves:
                lo = y[:, i * half : (i + 1) * half]
                hi = y[:, cells // 2 + i * half : cells // 2 + (i + 1) * half]
                part = jnp.concatenate([lo, hi], axis=1)
            else:
                part = y[:, i * LANES : (i + 1) * LANES]
            ref[which] = part.astype(BF16)

    dw = lax.dot_general(normed, gqkv, NT, preferred_element_type=F32)
    dproj = lax.dot_general(mixed, g, NT, preferred_element_type=F32)
    dgain = jnp.sum(gn * std, axis=1, keepdims=True)
    dbias = jnp.sum(gn, axis=1, keepdims=True)
    joined = jnp.concatenate([dw, dproj], axis=1)
    blocks = [joined[:, i * LANES : (i + 1) * LANES] for i in range(joined.shape[1] // LANES)]
    lane = lax.broadcasted_iota(jnp.int32, (channels, LANES), 1)
    tail = jnp.where(lane == 0, dgain, jnp.where(lane == 1, dbias, 0.0)).T[:8]
    used = len(blocks) * channels
    grads = jnp.concatenate(blocks, axis=0) + sums_ref[:used]
    extra = jnp.concatenate(
        [tail[:, :LANES], jnp.pad(tail[:, LANES:], ((0, 0), (0, 2 * LANES - channels)))], axis=0
    ) + sums_ref[used : used + 16]
    grads_ref[:used] = grads.astype(grads_ref.dtype)
    grads_ref[used : used + 16] = extra.astype(grads_ref.dtype)
    grads_ref[used + 16 :] = jnp.zeros(
        (grads_ref.shape[0] - used - 16, LANES), grads_ref.dtype
    )


GRAD_ROWS = 1280


def attend(quads, features, gain, bias, wqkv_t, wqkv, proj, proj_t, sums, halves, last):
    channels = quads[0].shape[1]
    cells = 4 * LANES
    width = cells // 2 if halves else cells
    S = jax.ShapeDtypeStruct
    return pl.pallas_call(
        functools.partial(attend_kernel, halves, last),
        out_shape=(S((2, channels, LANES), BF16),) * 4
        + (S((GRAD_ROWS, LANES), BF16 if last else F32),),
        in_specs=[VMEM] * 13,
        out_specs=(VMEM,) * 5,
        scratch_shapes=[
            pltpu.VMEM((3 * channels, cells), BF16),
            pltpu.VMEM((channels, cells), BF16),
            pltpu.VMEM((channels, cells), BF16),
            pltpu.VMEM((3 * channels, cells), BF16),
            pltpu.VMEM((2, cells, 64), BF16),
            pltpu.VMEM((2, 64, cells), BF16),
            pltpu.VMEM((2, 64, cells), BF16),
            pltpu.VMEM((2, cells, width), F32),
            pltpu.VMEM((cells, width), BF16),
            pltpu.VMEM((cells, width), F32),
            pltpu.VMEM((2, cells, width), BF16),
            pltpu.VMEM((2, 8, cells), F32),
            pltpu.VMEM((8, cells), F32),
        ],
        compiler_params=pltpu.CompilerParams(vmem_limit_bytes=40 * 2**20),
        cost_estimate=pl.CostEstimate(
            flops=12 * 12 * 512 * 512 * 256, bytes_accessed=4 * 2**20, transcendentals=12 * 512 * 512
        ),
        name="attend",
    )(*quads, *features, gain, bias, wqkv_t, wqkv, proj, proj_t, sums)


def moved(block, step_x, step_y):
    nx, ny = lax.axis_size("gx"), lax.axis_size("gy")
    route = []
    for i in range(nx):
        for j in range(ny):
            to = ((i + step_x) % nx) * ny + (j + step_y) % ny
            route.append((i * ny + j, to))
    return lax.ppermute(block, ("gx", "gy"), route)


def summed(rows, beside):
    nx, ny = lax.axis_size("gx"), lax.axis_size("gy")
    near = 2 * ny
    planes = [[near * i + j for j in range(near)] for i in range(nx // 2)]
    across = [list(ids) for ids in zip(*planes)]

    def exchanged(pieces, groups):
        return lax.all_to_all(pieces, ("gx", "gy"), 0, 0, axis_index_groups=groups)

    def copies(piece, count):
        return jnp.broadcast_to(piece[None], (count, *piece.shape))

    got = exchanged(rows.reshape(near, -1, LANES), planes)
    got, beside = lax.optimization_barrier((got, beside))
    mine = jnp.sum(got.astype(F32), axis=0).astype(BF16)
    got = exchanged(copies(mine, nx // 2), across)
    total = jnp.sum(got.astype(F32), axis=0).astype(BF16)
    return exchanged(copies(total, near), planes).reshape(rows.shape), beside


def grads_kernel(factor, rows_ref, dw_ref, dproj_ref, gain_ref, bias_ref):
    channels = dw_ref.shape[0]
    blocks = 4 * channels // LANES
    joined = jnp.concatenate(
        [rows_ref[i * channels : (i + 1) * channels].astype(F32) for i in range(blocks)], axis=1
    ) * factor
    dw_ref[...] = joined[:, : 3 * channels]
    dproj_ref[...] = joined[:, 3 * channels :]
    used = blocks * channels
    tail = rows_ref[used : used + 16].astype(F32) * factor
    tail = jnp.concatenate([tail[:8], tail[8:]], axis=1)[:, :channels]
    gain_ref[...] = tail[0:1]
    bias_ref[...] = tail[1:2]


def grads_of(rows, channels, factor):
    S = jax.ShapeDtypeStruct
    return pl.pallas_call(
        functools.partial(grads_kernel, factor),
        out_shape=(
            S((channels, 3 * channels), F32),
            S((channels, channels), F32),
            S((1, channels), F32),
            S((1, channels), F32),
        ),
        in_specs=[VMEM],
        out_specs=(VMEM,) * 4,
        name="unpack_grads",
    )(rows)


def shards(tokens, cotangent, ln_gain, ln_bias, qkv_weight, proj_weight):
    tile_x, tile_y, depth, channels = tokens.shape
    nx, ny = lax.axis_size("gx"), lax.axis_size("gy")
    windows = depth // WIN
    *pieces, gain, bias, wqkv_t, proj_t, kf, qf = packed(
        tokens, cotangent, ln_gain, ln_bias, qkv_weight, proj_weight
    )
    inputs = []
    for w in range(windows):
        p00, p01, p10, p11 = pieces[w * 4 : w * 4 + 4]
        inputs.append([moved(p00, -1, -1), moved(p01, -1, 0), moved(p10, 0, -1), p11])
    back = []
    sums = jnp.zeros((GRAD_ROWS, LANES), F32)
    for w in range(windows):
        last = w == windows - 1
        if w >= 2:
            inputs[w], back[w - 2] = lax.optimization_barrier((inputs[w], back[w - 2]))
        *ys, sums = attend(
            inputs[w], (kf, qf), gain, bias, wqkv_t, qkv_weight, proj_weight, proj_t, sums,
            halves=last, last=last,
        )
        back.append([moved(ys[0], 1, 1), moved(ys[1], 1, 0), moved(ys[2], 0, 1), ys[3]])
    sums, back[1] = lax.optimization_barrier((sums, back[1]))
    total, back = summed(sums, back)
    block_out, d_tokens = unpacked([piece for quads in back for piece in quads], tokens.shape)
    factor = 1.0 / math.sqrt(tile_x * nx * tile_y * ny * depth)
    dw, dproj, dgain, dbias = grads_of(total, channels, factor)
    return block_out, d_tokens, dw, dproj, dgain[0], dbias[0]


def solution(mesh):
    placed = (P("gx", "gy", None, None), P("gx", "gy", None, None), P(), P(), P(), P())
    return jax.shard_map(
        shards,
        mesh=mesh,
        in_specs=placed,
        out_specs=(P("gx", "gy", None, None), P("gx", "gy", None, None), P(), P(), P(), P()),
        check_vma=False,
    )
```

```python
import functools
import math

import jax
import jax.numpy as jnp
from jax import lax
from jax.experimental import pallas as pl
from jax.experimental.pallas import tpu as pltpu
from jax.sharding import PartitionSpec as P

HEADS = 12
WIN = 8
SHIFT = 4
F32 = jnp.float32
BF16 = jnp.bfloat16
LOG2E = math.log2(math.e)
MASKED = 2.0**100
LANES = 128
VMEM = pl.BlockSpec(memory_space=pltpu.VMEM)

NT = (((1,), (1,)), ((), ()))
TN = (((0,), (0,)), ((), ()))


def dot(a, b):
    return jnp.dot(a, b, preferred_element_type=F32)


def pieces_of(block):
    channels = block.shape[-1]
    pieces = {}
    for xh in range(2):
        for yh in range(2):
            quad = block[xh * 4 : xh * 4 + 4, yh * 4 : yh * 4 + 4].reshape(16, 24, channels)
            first = quad[:, 4:12].reshape(LANES, channels)
            second = quad[:, 12:20].reshape(LANES, channels)
            pairs = quad.reshape(8, 2, 24, channels)
            high = jnp.concatenate([pairs[:, 0, 20:24], pairs[:, 1, 20:24]], axis=1)
            low = jnp.concatenate([pairs[:, 0, 0:4], pairs[:, 1, 0:4]], axis=1)
            last = jnp.concatenate([high.reshape(64, channels), low.reshape(64, channels)], axis=0)
            pieces[xh, yh] = [piece.T.astype(BF16) for piece in (first, second, last)]
    return pieces


def quadrant_of(first, second, last):
    channels = first.shape[0]
    first = first.astype(F32).T.reshape(16, 8, channels)
    second = second.astype(F32).T.reshape(16, 8, channels)
    last = last.astype(F32).T
    high = last[:64].reshape(8, 8, channels)
    low = last[64:].reshape(8, 8, channels)
    even = jnp.concatenate([low[:, 0:4]], axis=1)
    odd = low[:, 4:8]
    low = jnp.stack([even, odd], axis=1).reshape(16, 4, channels)
    high = jnp.stack([high[:, 0:4], high[:, 4:8]], axis=1).reshape(16, 4, channels)
    whole = jnp.concatenate([low, first, second, high], axis=1)
    return whole.reshape(4, 4, 24, channels).astype(BF16)


def pack_kernel(tokens_ref, cot_ref, *refs):
    first_refs, rest_refs, (buffer, sems) = refs[:4], refs[4:8], refs[8:]
    sources = (tokens_ref, cot_ref)

    def copy(which, x):
        return pltpu.make_async_copy(
            sources[which].at[pl.ds(2 * x, 2)], buffer.at[which, pl.ds(2 * x, 2)], sems.at[which, x]
        )

    for which in range(2):
        for x in range(4):
            copy(which, x).start()
    for which in range(2):
        for x in range(4):
            copy(which, x).wait()
    for which in range(2):
        pieces = pieces_of(buffer[which].astype(F32))
        for xh in range(2):
            for yh in range(2):
                first, second, last = pieces[xh, yh]
                first_refs[xh * 2 + yh][which] = first
                rest_refs[xh * 2 + yh][0, which] = last
                rest_refs[xh * 2 + yh][1, which] = second


def packed(tokens, cotangent):
    channels = tokens.shape[-1]
    S = jax.ShapeDtypeStruct
    outs = pl.pallas_call(
        pack_kernel,
        out_shape=(S((2, channels, LANES), BF16),) * 4 + (S((2, 2, channels, LANES), BF16),) * 4,
        in_specs=[pl.BlockSpec(memory_space=pltpu.HBM)] * 2,
        out_specs=(VMEM,) * 8,
        scratch_shapes=[pltpu.VMEM((2, *tokens.shape), BF16), pltpu.SemaphoreType.DMA((2, 4))],
        compiler_params=pltpu.CompilerParams(vmem_limit_bytes=40 * 2**20),
        name="pack",
    )(tokens, cotangent)
    return outs[:4], outs[4:]


def prepare_kernel(
    gain_ref, bias_ref, wqkv_ref, proj_ref,
    gain_out, bias_out, wqkv_t_out, proj_t_out, kf_out, qf_out,
):
    gain_out[...] = gain_ref[...].T
    bias_out[...] = bias_ref[...].T
    wqkv_t_out[...] = wqkv_ref[...].astype(F32).T.astype(BF16)
    proj_t_out[...] = proj_ref[...].astype(F32).T.astype(BF16)
    edge_x = lax.axis_index("gx") == lax.axis_size("gx") - 1
    edge_y = lax.axis_index("gy") == lax.axis_size("gy") - 1
    shape = kf_out.shape[1:]
    row = lax.broadcasted_iota(jnp.int32, shape, 0)
    lane = lax.broadcasted_iota(jnp.int32, shape, 1)
    for layout, span in enumerate((LANES, LANES // 2)):
        quad = (lane // span) % 4
        far_x = jnp.where(jnp.logical_and(quad // 2 == 0, edge_x), 1.0, 0.0)
        far_y = jnp.where(jnp.logical_and(quad % 2 == 0, edge_y), 1.0, 0.0)
        key = jnp.where(row == 0, far_x, jnp.where(row == 1, 1 - far_x, jnp.where(row == 2, far_y, 1 - far_y)))
        query = jnp.where(row == 0, 1 - far_x, jnp.where(row == 1, far_x, jnp.where(row == 2, 1 - far_y, far_y)))
        kf_out[layout] = jnp.where(row < 4, key, 0.0).astype(BF16)
        qf_out[layout] = jnp.where(row < 4, query * -MASKED, 0.0).astype(BF16)


def prepared(gain, bias, wqkv, proj):
    channels = gain.shape[0]
    cells = 4 * LANES
    S = jax.ShapeDtypeStruct
    return pl.pallas_call(
        prepare_kernel,
        out_shape=(
            S((channels, 1), F32),
            S((channels, 1), F32),
            S((3 * channels, channels), BF16),
            S((channels, channels), BF16),
            S((2, 16, cells), BF16),
            S((2, 16, cells), BF16),
        ),
        in_specs=[VMEM] * 4,
        out_specs=(VMEM,) * 6,
        compiler_params=pltpu.CompilerParams(vmem_limit_bytes=40 * 2**20),
        name="prepare",
    )(gain[None], bias[None], wqkv, proj)


def unpack_kernel(*refs):
    paired, middle, outs = refs[:4], refs[4:8], refs[8:]
    for which, out in enumerate(outs):
        for xh in range(2):
            for yh in range(2):
                i = xh * 2 + yh
                quad = quadrant_of(paired[i][0, which], middle[i][which], paired[i][1, which])
                out[xh * 4 : xh * 4 + 4, yh * 4 : yh * 4 + 4] = quad


def unpacked(paired, middle, shape):
    return pl.pallas_call(
        unpack_kernel,
        out_shape=(jax.ShapeDtypeStruct(shape, BF16),) * 2,
        in_specs=[VMEM] * 8,
        out_specs=(VMEM,) * 2,
        compiler_params=pltpu.CompilerParams(vmem_limit_bytes=40 * 2**20),
        name="unpack",
    )(*paired, *middle)


def attend_kernel(
    turn,
    q00_ref, q01_ref, q10_ref, q11_ref,
    kf_ref, qf_ref, gain_ref, bias_ref, wqkv_t_ref, wqkv_ref, proj_ref, proj_t_ref,
    *refs,
):
    halves = turn == 1
    given = (0, 5, 1)[turn]
    earlier_refs, refs = refs[:given], refs[given:]
    y_refs, grads_ref, scratch = refs[:4], refs[4], refs[5:]
    (qkv_s, gm_s, mix_s, gqkv_s, kv_s, qa_s, ga_s, e_s, pb_s, dp_s, ds_s, r_s, d_s) = scratch
    quads = (q00_ref, q01_ref, q10_ref, q11_ref)
    if turn:
        quads = [quad.at[turn - 1] for quad in quads]
    channels = q00_ref.shape[-2]
    hd = channels // HEADS
    cells = 4 * LANES
    half = LANES // 2

    def whole(which):
        if halves:
            parts = [q[which].astype(F32) for q in quads]
            return jnp.concatenate(
                [p[:, :half] for p in parts] + [p[:, half:] for p in parts], axis=1
            )
        return jnp.concatenate([q[which].astype(F32) for q in quads], axis=1)

    xf = whole(0)
    gf = whole(1)
    g = gf.astype(BF16)
    mean = jnp.mean(xf, axis=0, keepdims=True)
    centered = xf - mean
    var = jnp.mean(centered * centered, axis=0, keepdims=True)
    inv = lax.rsqrt(var + 1e-5)
    std = centered * inv
    gain = gain_ref[...]
    normed = (std * gain + bias_ref[...]).astype(BF16)
    qkv = dot(wqkv_t_ref[...], normed).astype(BF16)
    qkv_s[...] = qkv
    gm_s[...] = dot(proj_ref[...], g).astype(BF16)

    layout = 1 if halves else 0
    size = cells // 2 if halves else cells
    groups = [slice(start, start + size) for start in range(0, cells, size)]
    step_rows = 64 * (cells // size)
    chunks = [
        (gi, slice(c, c + step_rows), group)
        for gi, group in enumerate(groups)
        for c in range(group.start, group.stop, step_rows)
    ]
    scale = hd**-0.5

    def head_rows(base, h):
        if isinstance(h, int):
            return slice(base + h * hd, base + (h + 1) * hd)
        return pl.ds(pl.multiple_of(base + h * hd, hd), hd)

    def q_rows(h):
        return head_rows(0, h)

    def k_rows(h):
        return head_rows(channels, h)

    def v_rows(h):
        return head_rows(2 * channels, h)

    def folded(x):
        return jnp.sum(x.reshape(-1, 8, x.shape[-1]), axis=0)

    def added(total, gi, x):
        total[gi] = x if total[gi] is None else total[gi] + x

    def prepare(h, slot):
        k = qkv_s[k_rows(h)]
        qf = qkv_s[q_rows(h)].astype(F32) * (scale * LOG2E)
        q_hi = qf.astype(BF16)
        q_lo = (qf - q_hi.astype(F32)).astype(BF16)
        none = jnp.zeros_like(k)
        kv_s[slot] = jnp.concatenate([k, k, kf_ref[layout], qkv_s[v_rows(h)]], axis=0).T
        qa_s[slot] = jnp.concatenate([q_hi, q_lo, qf_ref[layout], none], axis=0)
        ga_s[slot] = jnp.concatenate([none, none, none, gm_s[q_rows(h)]], axis=0)

    def exponentials(slot, chunk, total):
        gi, rows, cols = chunk
        e = jnp.exp2(dot(kv_s[slot, rows], qa_s[slot, :, cols]))
        e_s[slot, rows] = e
        added(total, gi, folded(e))

    def attention(slot, chunk, total):
        gi, rows, cols = chunk
        p = e_s[slot, rows] * r_s[slot, 0:1, cols]
        e_s[slot, rows] = p
        pb_s[rows] = p.astype(BF16)
        dp = dot(kv_s[slot, rows], ga_s[slot, :, cols])
        dp_s[rows] = dp
        added(total, gi, folded(p * dp))

    def grad_scores(slot, chunk):
        _, rows, cols = chunk
        ds_s[slot, rows] = (e_s[slot, rows] * (dp_s[rows] - d_s[0:1, cols])).astype(BF16)

    def mixed_of(h):
        for cols in groups:
            mix_s[q_rows(h), cols] = dot(qkv_s[v_rows(h), cols], pb_s[cols]).astype(BF16)

    def grad_values_of(h):
        for cols in groups:
            gv = lax.dot_general(gm_s[q_rows(h), cols], pb_s[cols], NT, preferred_element_type=F32)
            gqkv_s[v_rows(h), cols] = gv.astype(BF16)

    def grad_queries_of(h, slot):
        for cols in groups:
            gq = dot(qkv_s[k_rows(h), cols], ds_s[slot, cols]) * scale
            gqkv_s[q_rows(h), cols] = gq.astype(BF16)

    def grad_keys_of(h, slot):
        for cols in groups:
            gk = lax.dot_general(
                qkv_s[q_rows(h), cols], ds_s[slot, cols], NT, preferred_element_type=F32
            )
            gqkv_s[k_rows(h), cols] = (gk * scale).astype(BF16)

    def keep_inverse(slot, total):
        for gi, cols in enumerate(groups):
            r_s[slot, 0:1, cols] = 1.0 / jnp.sum(total[gi], axis=0, keepdims=True)

    def step(i, slot, first=True, final=True, ahead=True):
        sums = [None] * len(groups)
        inner = [None] * len(groups)
        count = len(chunks)
        for c, chunk in enumerate(chunks):
            if first:
                exponentials(slot, chunk, sums)
            attention(1 - slot, chunk, inner)
            if final and c == count // 4:
                grad_queries_of(i - 2, slot)
            if final and c == 3 * count // 4:
                grad_keys_of(i - 2, slot)
        if first:
            keep_inverse(slot, sums)
        for gi, cols in enumerate(groups):
            d_s[0:1, cols] = jnp.sum(inner[gi], axis=0, keepdims=True)
        for c, chunk in enumerate(chunks):
            grad_scores(1 - slot, chunk)
            if c == 0:
                mixed_of(i - 1)
            if c == count // 2:
                grad_values_of(i - 1)
        if ahead:
            prepare(i + 1, 1 - slot)

    squares = jnp.square(qkv[: 2 * channels].astype(F32)).reshape(2 * HEADS, hd, cells)
    longest = jnp.max(jnp.sum(squares, axis=1), axis=1, keepdims=True)
    bound = jnp.max(longest[:HEADS] * longest[HEADS:]) * (scale * LOG2E) ** 2
    in_range = bound <= 110.0**2

    @pl.when(in_range)
    def _():
        prepare(0, 0)
        prepare(1, 1)
        sums = [None] * len(groups)
        for chunk in chunks:
            exponentials(0, chunk, sums)
        keep_inverse(0, sums)
        step(1, 1, final=False)

        def two_steps(j, carry):
            step(2 + 2 * j, 0)
            step(3 + 2 * j, 1)
            return carry

        lax.fori_loop(0, (HEADS - 4) // 2, two_steps, 0)
        step(HEADS - 2, 0)
        step(HEADS - 1, 1, ahead=False)
        step(HEADS, 0, first=False, ahead=False)
        grad_queries_of(HEADS - 1, 1)
        grad_keys_of(HEADS - 1, 1)

    @pl.when(jnp.logical_not(in_range))
    def _():
        def head(h, carry):
            prepare(h, 0)
            for cols in groups:
                s = dot(kv_s[0, cols], qa_s[0, :, cols])
                e = jnp.exp2(s - jnp.max(s, axis=0, keepdims=True))
                p = e * (1.0 / jnp.sum(e, axis=0, keepdims=True))
                pb_s[cols] = p.astype(BF16)
                dp = dot(kv_s[0, cols], ga_s[0, :, cols])
                inner = jnp.sum(p * dp, axis=0, keepdims=True)
                ds_s[0, cols] = (p * (dp - inner)).astype(BF16)
            mixed_of(h)
            grad_values_of(h)
            grad_queries_of(h, 0)
            grad_keys_of(h, 0)
            return carry

        lax.fori_loop(0, HEADS, head, 0)

    mixed = mix_s[...]
    block_out = xf + dot(proj_t_ref[...], mixed)
    gqkv = gqkv_s[...]
    gn = dot(wqkv_ref[...], gqkv)
    scaled = gn * gain
    gx = inv * (
        scaled
        - jnp.mean(scaled, axis=0, keepdims=True)
        - std * jnp.mean(scaled * std, axis=0, keepdims=True)
    )
    d_tokens = gf + gx
    for which, y in enumerate((block_out, d_tokens)):
        for i, ref in enumerate(y_refs):
            if halves:
                lo = y[:, i * half : (i + 1) * half]
                hi = y[:, cells // 2 + i * half : cells // 2 + (i + 1) * half]
                part = jnp.concatenate([lo, hi], axis=1)
            else:
                part = y[:, i * LANES : (i + 1) * LANES]
            if turn == 1:
                ref[0, which] = earlier_refs[i][which]
                ref[1, which] = part.astype(BF16)
            else:
                ref[which] = part.astype(BF16)

    dw = lax.dot_general(normed, gqkv, NT, preferred_element_type=F32)
    dproj = lax.dot_general(mixed, g, NT, preferred_element_type=F32)
    dgain = jnp.sum(gn * std, axis=1, keepdims=True)
    dbias = jnp.sum(gn, axis=1, keepdims=True)
    joined = jnp.concatenate([dw, dproj], axis=1)
    blocks = [joined[:, i * LANES : (i + 1) * LANES] for i in range(joined.shape[1] // LANES)]
    lane = lax.broadcasted_iota(jnp.int32, (channels, LANES), 1)
    tail = jnp.where(lane == 0, dgain, jnp.where(lane == 1, dbias, 0.0)).T[:8]
    used = len(blocks) * channels
    grads = jnp.concatenate(blocks, axis=0)
    pad = jnp.zeros((8, 2 * LANES - channels), F32)
    extra = jnp.concatenate(
        [tail[:, :LANES], jnp.concatenate([tail[:, LANES:], pad], axis=1)], axis=0
    )
    if turn:
        grads = grads + earlier_refs[-1][:used]
        extra = extra + earlier_refs[-1][used : used + 16]
    grads_ref[:used] = grads.astype(grads_ref.dtype)
    grads_ref[used : used + 16] = extra.astype(grads_ref.dtype)
    grads_ref[used + 16 :] = jnp.zeros(
        (grads_ref.shape[0] - used - 16, LANES), grads_ref.dtype
    )


GRAD_ROWS = 1280


def attend(turn, quads, features, weights, earlier):
    channels = quads[0].shape[-2]
    cells = 4 * LANES
    width = cells // 2 if turn == 1 else cells
    S = jax.ShapeDtypeStruct
    piece = (2, channels, LANES)
    return pl.pallas_call(
        functools.partial(attend_kernel, turn),
        out_shape=(S((2, *piece) if turn == 1 else piece, BF16),) * 4
        + (S((GRAD_ROWS, LANES), BF16 if turn == 2 else F32),),
        in_specs=[VMEM] * (12 + len(earlier)),
        out_specs=(VMEM,) * 5,
        scratch_shapes=[
            pltpu.VMEM((3 * channels, cells), BF16),
            pltpu.VMEM((channels, cells), BF16),
            pltpu.VMEM((channels, cells), BF16),
            pltpu.VMEM((3 * channels, cells), BF16),
            pltpu.VMEM((2, cells, 64), BF16),
            pltpu.VMEM((2, 64, cells), BF16),
            pltpu.VMEM((2, 64, cells), BF16),
            pltpu.VMEM((2, cells, width), F32),
            pltpu.VMEM((cells, width), BF16),
            pltpu.VMEM((cells, width), F32),
            pltpu.VMEM((2, cells, width), BF16),
            pltpu.VMEM((2, 8, cells), F32),
            pltpu.VMEM((8, cells), F32),
        ],
        compiler_params=pltpu.CompilerParams(vmem_limit_bytes=40 * 2**20),
        cost_estimate=pl.CostEstimate(
            flops=12 * 12 * 512 * 512 * 256, bytes_accessed=4 * 2**20, transcendentals=12 * 512 * 512
        ),
        name="attend",
    )(*quads, *features, *weights, *earlier)


def moved(block, step_x, step_y):
    nx, ny = lax.axis_size("gx"), lax.axis_size("gy")
    route = []
    for i in range(nx):
        for j in range(ny):
            to = ((i + step_x) % nx) * ny + (j + step_y) % ny
            route.append((i * ny + j, to))
    return lax.ppermute(block, ("gx", "gy"), route)


def summed(rows, beside):
    nx, ny = lax.axis_size("gx"), lax.axis_size("gy")
    near = 2 * ny
    planes = [[near * i + j for j in range(near)] for i in range(nx // 2)]
    across = [list(ids) for ids in zip(*planes)]

    def exchanged(pieces, groups):
        return lax.all_to_all(pieces, ("gx", "gy"), 0, 0, axis_index_groups=groups)

    def copies(piece, count):
        return jnp.broadcast_to(piece[None], (count, *piece.shape))

    got = exchanged(rows.reshape(near, -1, LANES), planes)
    mine = jnp.sum(got.astype(F32), axis=0).astype(BF16)
    got = exchanged(copies(mine, nx // 2), across)
    got, beside = lax.optimization_barrier((got, beside))
    total = jnp.sum(got.astype(F32), axis=0).astype(BF16)
    return exchanged(copies(total, near), planes).reshape(rows.shape), beside


def grads_kernel(
    factor, rows_ref, dw_ref, dproj_ref, gain_ref, bias_ref, rows_s, dw_s, dproj_s, ends_s, in_sems, out_sems
):
    channels = dw_s.shape[0]
    blocks = 4 * channels // LANES
    used = blocks * channels
    spans = [(i * channels, channels) for i in range(blocks)] + [(used, 16)]
    incoming = [
        pltpu.make_async_copy(
            rows_ref.at[pl.ds(start, size)], rows_s.at[pl.ds(start, size)], in_sems.at[i]
        )
        for i, (start, size) in enumerate(spans)
    ]
    for copy in incoming:
        copy.start()
    outgoing = []

    def send(src, dst):
        copy = pltpu.make_async_copy(src, dst, out_sems.at[len(outgoing)])
        copy.start()
        outgoing.append(copy)

    def block(i):
        incoming[i].wait()
        return rows_s[i * channels : (i + 1) * channels].astype(F32) * factor

    whole = 3 * channels // LANES
    for i in range(whole):
        dw_s[:, i * LANES : (i + 1) * LANES] = block(i)
        if i % 2:
            cols = pl.ds((i - 1) * LANES, 2 * LANES)
            send(dw_s.at[:, cols], dw_ref.at[:, cols])
    rest = jnp.concatenate([block(i) for i in range(whole, blocks)], axis=1)
    edge = 3 * channels - whole * LANES
    dw_s[:, whole * LANES :] = rest[:, :edge]
    send(dw_s.at[:, pl.ds(whole * LANES, edge)], dw_ref.at[:, pl.ds(whole * LANES, edge)])
    dproj_s[...] = rest[:, edge:]
    send(dproj_s, dproj_ref)
    incoming[blocks].wait()
    tail = rows_s[used : used + 16].astype(F32) * factor
    ends_s[...] = jnp.concatenate([tail[:8], tail[8:]], axis=1)[:, :channels]
    gain_ref[...] = ends_s[0:1]
    bias_ref[...] = ends_s[1:2]
    for copy in outgoing:
        copy.wait()


def grads_of(rows, channels, factor):
    S = jax.ShapeDtypeStruct
    anywhere = pl.BlockSpec(memory_space=pltpu.HBM)
    return pl.pallas_call(
        functools.partial(grads_kernel, factor),
        out_shape=(
            S((channels, 3 * channels), F32),
            S((channels, channels), F32),
            S((1, channels), F32),
            S((1, channels), F32),
        ),
        in_specs=[anywhere],
        out_specs=(anywhere, anywhere, VMEM, VMEM),
        scratch_shapes=[
            pltpu.VMEM((GRAD_ROWS, LANES), BF16),
            pltpu.VMEM((channels, 3 * channels), F32),
            pltpu.VMEM((channels, channels), F32),
            pltpu.VMEM((8, channels), F32),
            pltpu.SemaphoreType.DMA((4 * channels // LANES + 1,)),
            pltpu.SemaphoreType.DMA((4,)),
        ],
        name="unpack_grads",
    )(rows)


def shards(tokens, cotangent, ln_gain, ln_bias, qkv_weight, proj_weight):
    tile_x, tile_y, depth, channels = tokens.shape
    nx, ny = lax.axis_size("gx"), lax.axis_size("gy")
    first, rest = packed(tokens, cotangent)
    first, ln_gain, ln_bias, qkv_weight, proj_weight = lax.optimization_barrier(
        (first, ln_gain, ln_bias, qkv_weight, proj_weight)
    )
    gain, bias, wqkv_t, proj_t, *features = prepared(ln_gain, ln_bias, qkv_weight, proj_weight)
    weights = (gain, bias, wqkv_t, qkv_weight, proj_weight, proj_t)

    steps = ((1, 1), (1, 0), (0, 1))

    def gathered(quads):
        return [moved(quad, -x, -y) for quad, (x, y) in zip(quads, steps)] + [quads[3]]

    def returned(quads):
        return [moved(quad, x, y) for quad, (x, y) in zip(quads, steps)] + [quads[3]]

    first, rest = gathered(first), gathered(rest)
    *y, sums = attend(0, first, features, weights, ())
    *y, sums = attend(1, rest, features, weights, (*y, sums))
    paired = returned(y)
    *y, sums = attend(2, rest, features, weights, (sums,))
    middle = returned(y)
    sums, paired = lax.optimization_barrier((sums, paired))
    total, (paired, middle) = summed(sums, (paired, middle))
    block_out, d_tokens = unpacked(paired, middle, tokens.shape)
    factor = 1.0 / math.sqrt(tile_x * nx * tile_y * ny * depth)
    dw, dproj, dgain, dbias = grads_of(total, channels, factor)
    return block_out, d_tokens, dw, dproj, dgain[0], dbias[0]


def solution(mesh):
    placed = (P("gx", "gy", None, None), P("gx", "gy", None, None), P(), P(), P(), P())
    return jax.shard_map(
        shards,
        mesh=mesh,
        in_specs=placed,
        out_specs=(P("gx", "gy", None, None), P("gx", "gy", None, None), P(), P(), P(), P()),
        check_vma=False,
    )
```

```python
import functools
import math

import jax
import jax.numpy as jnp
from jax import lax
from jax.experimental import pallas as pl
from jax.experimental.pallas import tpu as pltpu
from jax.sharding import PartitionSpec as P

HEADS = 12
WIN = 8
SHIFT = 4
F32 = jnp.float32
BF16 = jnp.bfloat16
LOG2E = math.log2(math.e)
MASKED = 2.0**100
LANES = 128
VMEM = pl.BlockSpec(memory_space=pltpu.VMEM)

NT = (((1,), (1,)), ((), ()))
TN = (((0,), (0,)), ((), ()))


def dot(a, b):
    return jnp.dot(a, b, preferred_element_type=F32)


def pieces_of(block):
    channels = block.shape[-1]
    pieces = {}
    for xh in range(2):
        for yh in range(2):
            quad = block[xh * 4 : xh * 4 + 4, yh * 4 : yh * 4 + 4].reshape(16, 24, channels)
            first = quad[:, 4:12].reshape(LANES, channels)
            second = quad[:, 12:20].reshape(LANES, channels)
            pairs = quad.reshape(8, 2, 24, channels)
            high = jnp.concatenate([pairs[:, 0, 20:24], pairs[:, 1, 20:24]], axis=1)
            low = jnp.concatenate([pairs[:, 0, 0:4], pairs[:, 1, 0:4]], axis=1)
            last = jnp.concatenate([high.reshape(64, channels), low.reshape(64, channels)], axis=0)
            pieces[xh, yh] = [piece.T.astype(BF16) for piece in (first, second, last)]
    return pieces


def quadrant_of(first, second, last):
    channels = first.shape[0]
    first = first.astype(F32).T.reshape(16, 8, channels)
    second = second.astype(F32).T.reshape(16, 8, channels)
    last = last.astype(F32).T
    high = last[:64].reshape(8, 8, channels)
    low = last[64:].reshape(8, 8, channels)
    even = jnp.concatenate([low[:, 0:4]], axis=1)
    odd = low[:, 4:8]
    low = jnp.stack([even, odd], axis=1).reshape(16, 4, channels)
    high = jnp.stack([high[:, 0:4], high[:, 4:8]], axis=1).reshape(16, 4, channels)
    whole = jnp.concatenate([low, first, second, high], axis=1)
    return whole.reshape(4, 4, 24, channels).astype(BF16)


def pack_kernel(tokens_ref, cot_ref, *refs):
    first_refs, rest_refs, (buffer, sems) = refs[:4], refs[4:8], refs[8:]
    sources = (tokens_ref, cot_ref)

    def copy(which, x):
        return pltpu.make_async_copy(
            sources[which].at[pl.ds(2 * x, 2)], buffer.at[which, pl.ds(2 * x, 2)], sems.at[which, x]
        )

    for which in range(2):
        for x in range(4):
            copy(which, x).start()
    for which in range(2):
        for x in range(4):
            copy(which, x).wait()
    for which in range(2):
        pieces = pieces_of(buffer[which].astype(F32))
        for xh in range(2):
            for yh in range(2):
                first, second, last = pieces[xh, yh]
                first_refs[xh * 2 + yh][which] = first
                rest_refs[xh * 2 + yh][0, which] = last
                rest_refs[xh * 2 + yh][1, which] = second


def packed(tokens, cotangent):
    channels = tokens.shape[-1]
    S = jax.ShapeDtypeStruct
    outs = pl.pallas_call(
        pack_kernel,
        out_shape=(S((2, channels, LANES), BF16),) * 4 + (S((2, 2, channels, LANES), BF16),) * 4,
        in_specs=[pl.BlockSpec(memory_space=pltpu.HBM)] * 2,
        out_specs=(VMEM,) * 8,
        scratch_shapes=[pltpu.VMEM((2, *tokens.shape), BF16), pltpu.SemaphoreType.DMA((2, 4))],
        compiler_params=pltpu.CompilerParams(vmem_limit_bytes=62 * 2**20),
        name="pack",
    )(tokens, cotangent)
    return outs[:4], outs[4:]


def prepare_kernel(
    gain_ref, bias_ref, wqkv_ref, proj_ref,
    gain_out, bias_out, wqkv_t_out, proj_t_out, kf_out, qf_out,
):
    gain_out[...] = gain_ref[...].T
    bias_out[...] = bias_ref[...].T
    wqkv_t_out[...] = wqkv_ref[...].astype(F32).T.astype(BF16)
    proj_t_out[...] = proj_ref[...].astype(F32).T.astype(BF16)
    edge_x = lax.axis_index("gx") == lax.axis_size("gx") - 1
    edge_y = lax.axis_index("gy") == lax.axis_size("gy") - 1
    shape = kf_out.shape[1:]
    row = lax.broadcasted_iota(jnp.int32, shape, 0)
    lane = lax.broadcasted_iota(jnp.int32, shape, 1)
    for layout, span in enumerate((LANES, LANES // 2)):
        quad = (lane // span) % 4
        far_x = jnp.where(jnp.logical_and(quad // 2 == 0, edge_x), 1.0, 0.0)
        far_y = jnp.where(jnp.logical_and(quad % 2 == 0, edge_y), 1.0, 0.0)
        key = jnp.where(row == 0, far_x, jnp.where(row == 1, 1 - far_x, jnp.where(row == 2, far_y, 1 - far_y)))
        query = jnp.where(row == 0, 1 - far_x, jnp.where(row == 1, far_x, jnp.where(row == 2, 1 - far_y, far_y)))
        kf_out[layout] = jnp.where(row < 4, key, 0.0).astype(BF16)
        qf_out[layout] = jnp.where(row < 4, query * -MASKED, 0.0).astype(BF16)


def prepared(gain, bias, wqkv, proj):
    channels = gain.shape[0]
    cells = 4 * LANES
    S = jax.ShapeDtypeStruct
    return pl.pallas_call(
        prepare_kernel,
        out_shape=(
            S((channels, 1), F32),
            S((channels, 1), F32),
            S((3 * channels, channels), BF16),
            S((channels, channels), BF16),
            S((2, 16, cells), BF16),
            S((2, 16, cells), BF16),
        ),
        in_specs=[VMEM] * 4,
        out_specs=(VMEM,) * 6,
        compiler_params=pltpu.CompilerParams(vmem_limit_bytes=40 * 2**20),
        name="prepare",
    )(gain[None], bias[None], wqkv, proj)


def unpack_kernel(*refs):
    paired, middle, outs = refs[:4], refs[4:8], refs[8:]
    for which, out in enumerate(outs):
        for xh in range(2):
            for yh in range(2):
                i = xh * 2 + yh
                quad = quadrant_of(paired[i][0, which], middle[i][which], paired[i][1, which])
                out[xh * 4 : xh * 4 + 4, yh * 4 : yh * 4 + 4] = quad


def unpacked(paired, middle, shape):
    return pl.pallas_call(
        unpack_kernel,
        out_shape=(jax.ShapeDtypeStruct(shape, BF16),) * 2,
        in_specs=[VMEM] * 8,
        out_specs=(VMEM,) * 2,
        compiler_params=pltpu.CompilerParams(vmem_limit_bytes=40 * 2**20),
        name="unpack",
    )(*paired, *middle)


def attend_kernel(
    turn,
    q00_ref, q01_ref, q10_ref, q11_ref,
    kf_ref, qf_ref, gain_ref, bias_ref, wqkv_t_ref, wqkv_ref, proj_ref, proj_t_ref,
    *refs,
):
    halves = turn == 1
    given = (0, 5, 1)[turn]
    earlier_refs, refs = refs[:given], refs[given:]
    y_refs, grads_ref, scratch = refs[:4], refs[4], refs[5:]
    (qkv_s, gm_s, mix_s, gqkv_s, kv_s, qa_s, ga_s, e_s, pb_s, dp_s, ds_s, r_s, d_s) = scratch
    quads = (q00_ref, q01_ref, q10_ref, q11_ref)
    if turn:
        quads = [quad.at[turn - 1] for quad in quads]
    channels = q00_ref.shape[-2]
    hd = channels // HEADS
    cells = 4 * LANES
    half = LANES // 2

    def whole(which):
        if halves:
            parts = [q[which].astype(F32) for q in quads]
            return jnp.concatenate(
                [p[:, :half] for p in parts] + [p[:, half:] for p in parts], axis=1
            )
        return jnp.concatenate([q[which].astype(F32) for q in quads], axis=1)

    xf = whole(0)
    gf = whole(1)
    g = gf.astype(BF16)
    mean = jnp.mean(xf, axis=0, keepdims=True)
    centered = xf - mean
    var = jnp.mean(centered * centered, axis=0, keepdims=True)
    inv = lax.rsqrt(var + 1e-5)
    std = centered * inv
    gain = gain_ref[...]
    normed = (std * gain + bias_ref[...]).astype(BF16)
    qkv = dot(wqkv_t_ref[...], normed).astype(BF16)
    qkv_s[...] = qkv
    gm_s[...] = dot(proj_ref[...], g).astype(BF16)

    layout = 1 if halves else 0
    size = cells // 2 if halves else cells
    groups = [slice(start, start + size) for start in range(0, cells, size)]
    step_rows = 64 * (cells // size)
    chunks = [
        (gi, slice(c, c + step_rows), group)
        for gi, group in enumerate(groups)
        for c in range(group.start, group.stop, step_rows)
    ]
    scale = hd**-0.5

    def head_rows(base, h):
        if isinstance(h, int):
            return slice(base + h * hd, base + (h + 1) * hd)
        return pl.ds(pl.multiple_of(base + h * hd, hd), hd)

    def q_rows(h):
        return head_rows(0, h)

    def k_rows(h):
        return head_rows(channels, h)

    def v_rows(h):
        return head_rows(2 * channels, h)

    def folded(x):
        return jnp.sum(x.reshape(-1, 8, x.shape[-1]), axis=0)

    def added(total, gi, x):
        total[gi] = x if total[gi] is None else total[gi] + x

    def prepare(h, slot):
        k = qkv_s[k_rows(h)]
        qf = qkv_s[q_rows(h)].astype(F32) * (scale * LOG2E)
        q_hi = qf.astype(BF16)
        q_lo = (qf - q_hi.astype(F32)).astype(BF16)
        none = jnp.zeros_like(k)
        kv_s[slot] = jnp.concatenate([k, k, kf_ref[layout], qkv_s[v_rows(h)]], axis=0).T
        qa_s[slot] = jnp.concatenate([q_hi, q_lo, qf_ref[layout], none], axis=0)
        ga_s[slot] = jnp.concatenate([none, none, none, gm_s[q_rows(h)]], axis=0)

    def exponentials(slot, chunk, total):
        gi, rows, cols = chunk
        e = jnp.exp2(dot(kv_s[slot, rows], qa_s[slot, :, cols]))
        e_s[slot, rows] = e
        added(total, gi, folded(e))

    def attention(slot, chunk, total):
        gi, rows, cols = chunk
        p = e_s[slot, rows] * r_s[slot, 0:1, cols]
        e_s[slot, rows] = p
        pb_s[rows] = p.astype(BF16)
        dp = dot(kv_s[slot, rows], ga_s[slot, :, cols])
        dp_s[rows] = dp
        added(total, gi, folded(p * dp))

    def grad_scores(slot, chunk):
        _, rows, cols = chunk
        ds_s[slot, rows] = (e_s[slot, rows] * (dp_s[rows] - d_s[0:1, cols])).astype(BF16)

    def mixed_of(h):
        for cols in groups:
            mix_s[q_rows(h), cols] = dot(qkv_s[v_rows(h), cols], pb_s[cols]).astype(BF16)

    def grad_values_of(h):
        for cols in groups:
            gv = lax.dot_general(gm_s[q_rows(h), cols], pb_s[cols], NT, preferred_element_type=F32)
            gqkv_s[v_rows(h), cols] = gv.astype(BF16)

    def grad_queries_of(h, slot):
        for cols in groups:
            gq = dot(qkv_s[k_rows(h), cols], ds_s[slot, cols]) * scale
            gqkv_s[q_rows(h), cols] = gq.astype(BF16)

    def grad_keys_of(h, slot):
        for cols in groups:
            gk = lax.dot_general(
                qkv_s[q_rows(h), cols], ds_s[slot, cols], NT, preferred_element_type=F32
            )
            gqkv_s[k_rows(h), cols] = (gk * scale).astype(BF16)

    def keep_inverse(slot, total):
        for gi, cols in enumerate(groups):
            r_s[slot, 0:1, cols] = 1.0 / jnp.sum(total[gi], axis=0, keepdims=True)

    def step(i, slot, first=True, final=True, ahead=True):
        sums = [None] * len(groups)
        inner = [None] * len(groups)
        count = len(chunks)
        for c, chunk in enumerate(chunks):
            if first:
                exponentials(slot, chunk, sums)
            attention(1 - slot, chunk, inner)
            if final and c == count // 4:
                grad_queries_of(i - 2, slot)
            if final and c == 3 * count // 4:
                grad_keys_of(i - 2, slot)
        if first:
            keep_inverse(slot, sums)
        for gi, cols in enumerate(groups):
            d_s[0:1, cols] = jnp.sum(inner[gi], axis=0, keepdims=True)
        for c, chunk in enumerate(chunks):
            grad_scores(1 - slot, chunk)
            if c == 0:
                mixed_of(i - 1)
            if c == count // 2:
                grad_values_of(i - 1)
        if ahead:
            prepare(i + 1, 1 - slot)

    squares = jnp.square(qkv[: 2 * channels].astype(F32)).reshape(2 * HEADS, hd, cells)
    longest = jnp.max(jnp.sum(squares, axis=1), axis=1, keepdims=True)
    bound = jnp.max(longest[:HEADS] * longest[HEADS:]) * (scale * LOG2E) ** 2
    in_range = bound <= 110.0**2

    @pl.when(in_range)
    def _():
        prepare(0, 0)
        prepare(1, 1)
        sums = [None] * len(groups)
        for chunk in chunks:
            exponentials(0, chunk, sums)
        keep_inverse(0, sums)
        step(1, 1, final=False)

        def two_steps(j, carry):
            step(2 + 2 * j, 0)
            step(3 + 2 * j, 1)
            return carry

        lax.fori_loop(0, (HEADS - 4) // 2, two_steps, 0)
        step(HEADS - 2, 0)
        step(HEADS - 1, 1, ahead=False)
        step(HEADS, 0, first=False, ahead=False)
        grad_queries_of(HEADS - 1, 1)
        grad_keys_of(HEADS - 1, 1)

    @pl.when(jnp.logical_not(in_range))
    def _():
        def head(h, carry):
            prepare(h, 0)
            for cols in groups:
                s = dot(kv_s[0, cols], qa_s[0, :, cols])
                e = jnp.exp2(s - jnp.max(s, axis=0, keepdims=True))
                p = e * (1.0 / jnp.sum(e, axis=0, keepdims=True))
                pb_s[cols] = p.astype(BF16)
                dp = dot(kv_s[0, cols], ga_s[0, :, cols])
                inner = jnp.sum(p * dp, axis=0, keepdims=True)
                ds_s[0, cols] = (p * (dp - inner)).astype(BF16)
            mixed_of(h)
            grad_values_of(h)
            grad_queries_of(h, 0)
            grad_keys_of(h, 0)
            return carry

        lax.fori_loop(0, HEADS, head, 0)

    mixed = mix_s[...]
    block_out = xf + dot(proj_t_ref[...], mixed)
    gqkv = gqkv_s[...]
    gn = dot(wqkv_ref[...], gqkv)
    scaled = gn * gain
    gx = inv * (
        scaled
        - jnp.mean(scaled, axis=0, keepdims=True)
        - std * jnp.mean(scaled * std, axis=0, keepdims=True)
    )
    d_tokens = gf + gx
    for which, y in enumerate((block_out, d_tokens)):
        for i, ref in enumerate(y_refs):
            if halves:
                lo = y[:, i * half : (i + 1) * half]
                hi = y[:, cells // 2 + i * half : cells // 2 + (i + 1) * half]
                part = jnp.concatenate([lo, hi], axis=1)
            else:
                part = y[:, i * LANES : (i + 1) * LANES]
            if turn == 1:
                ref[0, which] = earlier_refs[i][which]
                ref[1, which] = part.astype(BF16)
            else:
                ref[which] = part.astype(BF16)

    dw = lax.dot_general(normed, gqkv, NT, preferred_element_type=F32)
    dproj = lax.dot_general(mixed, g, NT, preferred_element_type=F32)
    dgain = jnp.sum(gn * std, axis=1, keepdims=True)
    dbias = jnp.sum(gn, axis=1, keepdims=True)
    joined = jnp.concatenate([dw, dproj], axis=1)
    blocks = [joined[:, i * LANES : (i + 1) * LANES] for i in range(joined.shape[1] // LANES)]
    lane = lax.broadcasted_iota(jnp.int32, (channels, LANES), 1)
    tail = jnp.where(lane == 0, dgain, jnp.where(lane == 1, dbias, 0.0)).T[:8]
    used = len(blocks) * channels
    grads = jnp.concatenate(blocks, axis=0)
    pad = jnp.zeros((8, 2 * LANES - channels), F32)
    extra = jnp.concatenate(
        [tail[:, :LANES], jnp.concatenate([tail[:, LANES:], pad], axis=1)], axis=0
    )
    if turn:
        grads = grads + earlier_refs[-1][:used]
        extra = extra + earlier_refs[-1][used : used + 16]
    grads_ref[:used] = grads.astype(grads_ref.dtype)
    grads_ref[used : used + 16] = extra.astype(grads_ref.dtype)
    grads_ref[used + 16 :] = jnp.zeros(
        (grads_ref.shape[0] - used - 16, LANES), grads_ref.dtype
    )


GRAD_ROWS = 1280


def attend(turn, quads, features, weights, earlier):
    channels = quads[0].shape[-2]
    cells = 4 * LANES
    width = cells // 2 if turn == 1 else cells
    S = jax.ShapeDtypeStruct
    piece = (2, channels, LANES)
    return pl.pallas_call(
        functools.partial(attend_kernel, turn),
        out_shape=(S((2, *piece) if turn == 1 else piece, BF16),) * 4
        + (S((GRAD_ROWS, LANES), BF16 if turn == 2 else F32),),
        in_specs=[VMEM] * (12 + len(earlier)),
        out_specs=(VMEM,) * 5,
        scratch_shapes=[
            pltpu.VMEM((3 * channels, cells), BF16),
            pltpu.VMEM((channels, cells), BF16),
            pltpu.VMEM((channels, cells), BF16),
            pltpu.VMEM((3 * channels, cells), BF16),
            pltpu.VMEM((2, cells, 64), BF16),
            pltpu.VMEM((2, 64, cells), BF16),
            pltpu.VMEM((2, 64, cells), BF16),
            pltpu.VMEM((2, cells, width), F32),
            pltpu.VMEM((cells, width), BF16),
            pltpu.VMEM((cells, width), F32),
            pltpu.VMEM((2, cells, width), BF16),
            pltpu.VMEM((2, 8, cells), F32),
            pltpu.VMEM((8, cells), F32),
        ],
        compiler_params=pltpu.CompilerParams(vmem_limit_bytes=40 * 2**20),
        cost_estimate=pl.CostEstimate(
            flops=12 * 12 * 512 * 512 * 256, bytes_accessed=4 * 2**20, transcendentals=12 * 512 * 512
        ),
        name="attend",
    )(*quads, *features, *weights, *earlier)


def moved(block, step_x, step_y):
    nx, ny = lax.axis_size("gx"), lax.axis_size("gy")
    route = []
    for i in range(nx):
        for j in range(ny):
            to = ((i + step_x) % nx) * ny + (j + step_y) % ny
            route.append((i * ny + j, to))
    return lax.ppermute(block, ("gx", "gy"), route)


def summed(rows):
    nx, ny = lax.axis_size("gx"), lax.axis_size("gy")
    near = 2 * ny
    planes = [[near * i + j for j in range(near)] for i in range(nx // 2)]
    across = [list(ids) for ids in zip(*planes)]

    def exchanged(pieces, groups):
        return lax.all_to_all(pieces, ("gx", "gy"), 0, 0, axis_index_groups=groups)

    def copies(piece, count):
        return jnp.broadcast_to(piece[None], (count, *piece.shape))

    got = exchanged(rows.reshape(near, -1, LANES), planes)
    mine = jnp.sum(got.astype(F32), axis=0).astype(BF16)
    got = exchanged(copies(mine, nx // 2), across)
    total = jnp.sum(got.astype(F32), axis=0).astype(BF16)
    return exchanged(copies(total, near), planes).reshape(rows.shape)


def grads_kernel(
    factor, rows_ref, dw_ref, dproj_ref, gain_ref, bias_ref, dw_s, dproj_s, ends_s, out_sems
):
    channels = dw_s.shape[0]
    blocks = 4 * channels // LANES
    used = blocks * channels
    outgoing = []

    def send(src, dst):
        copy = pltpu.make_async_copy(src, dst, out_sems.at[len(outgoing)])
        copy.start()
        outgoing.append(copy)

    def block(i):
        return rows_ref[i * channels : (i + 1) * channels].astype(F32) * factor

    whole = 3 * channels // LANES
    for i in range(whole):
        dw_s[:, i * LANES : (i + 1) * LANES] = block(i)
        if i % 2:
            cols = pl.ds((i - 1) * LANES, 2 * LANES)
            send(dw_s.at[:, cols], dw_ref.at[:, cols])
    rest = jnp.concatenate([block(i) for i in range(whole, blocks)], axis=1)
    edge = 3 * channels - whole * LANES
    dw_s[:, whole * LANES :] = rest[:, :edge]
    send(dw_s.at[:, pl.ds(whole * LANES, edge)], dw_ref.at[:, pl.ds(whole * LANES, edge)])
    dproj_s[...] = rest[:, edge:]
    send(dproj_s, dproj_ref)
    tail = rows_ref[used : used + 16].astype(F32) * factor
    ends_s[...] = jnp.concatenate([tail[:8], tail[8:]], axis=1)[:, :channels]
    gain_ref[...] = ends_s[0:1]
    bias_ref[...] = ends_s[1:2]
    for copy in outgoing:
        copy.wait()


def grads_of(rows, channels, factor):
    S = jax.ShapeDtypeStruct
    anywhere = pl.BlockSpec(memory_space=pltpu.HBM)
    return pl.pallas_call(
        functools.partial(grads_kernel, factor),
        out_shape=(
            S((channels, 3 * channels), F32),
            S((channels, channels), F32),
            S((1, channels), F32),
            S((1, channels), F32),
        ),
        in_specs=[VMEM],
        out_specs=(anywhere, anywhere, VMEM, VMEM),
        scratch_shapes=[
            pltpu.VMEM((channels, 3 * channels), F32),
            pltpu.VMEM((channels, channels), F32),
            pltpu.VMEM((8, channels), F32),
            pltpu.SemaphoreType.DMA((4,)),
        ],
        name="unpack_grads",
    )(rows)


def shards(tokens, cotangent, ln_gain, ln_bias, qkv_weight, proj_weight):
    tile_x, tile_y, depth, channels = tokens.shape
    nx, ny = lax.axis_size("gx"), lax.axis_size("gy")
    first, rest = packed(tokens, cotangent)
    first, ln_gain, ln_bias, qkv_weight, proj_weight = lax.optimization_barrier(
        (first, ln_gain, ln_bias, qkv_weight, proj_weight)
    )
    gain, bias, wqkv_t, proj_t, *features = prepared(ln_gain, ln_bias, qkv_weight, proj_weight)
    weights = (gain, bias, wqkv_t, qkv_weight, proj_weight, proj_t)

    steps = ((1, 1), (1, 0), (0, 1))

    def gathered(quads):
        return [moved(quad, -x, -y) for quad, (x, y) in zip(quads, steps)] + [quads[3]]

    def returned(quads):
        return [moved(quad, x, y) for quad, (x, y) in zip(quads, steps)] + [quads[3]]

    first, rest = gathered(first), gathered(rest)
    *y, sums = attend(0, first, features, weights, ())
    *y, sums = attend(1, rest, features, weights, (*y, sums))
    paired = returned(y)
    *y, sums = attend(2, rest, features, weights, (sums,))
    middle = returned(y)
    sums, paired = lax.optimization_barrier((sums, paired))
    total = summed(sums)
    block_out, d_tokens = unpacked(paired, middle, tokens.shape)
    factor = 1.0 / math.sqrt(tile_x * nx * tile_y * ny * depth)
    dw, dproj, dgain, dbias = grads_of(total, channels, factor)
    return block_out, d_tokens, dw, dproj, dgain[0], dbias[0]


def solution(mesh):
    placed = (P("gx", "gy", None, None), P("gx", "gy", None, None), P(), P(), P(), P())
    return jax.shard_map(
        shards,
        mesh=mesh,
        in_specs=placed,
        out_specs=(P("gx", "gy", None, None), P("gx", "gy", None, None), P(), P(), P(), P()),
        check_vma=False,
    )
```

```python
import functools
import math

import jax
import jax.numpy as jnp
from jax import lax
from jax.experimental import pallas as pl
from jax.experimental.pallas import tpu as pltpu
from jax.sharding import PartitionSpec as P

HEADS = 12
WIN = 8
SHIFT = 4
F32 = jnp.float32
BF16 = jnp.bfloat16
LOG2E = math.log2(math.e)
MASKED = 2.0**100
LANES = 128
VMEM = pl.BlockSpec(memory_space=pltpu.VMEM)

NT = (((1,), (1,)), ((), ()))
TN = (((0,), (0,)), ((), ()))


def dot(a, b):
    return jnp.dot(a, b, preferred_element_type=F32)


def quadrants(block):
    shape = (16, *block.shape[2:])
    return [
        block[x : x + 4, y : y + 4].reshape(shape) for x in (0, 4) for y in (0, 4)
    ]


def piece_of(cells):
    return cells.reshape(LANES, cells.shape[-1]).T.astype(BF16)


def last_piece_of(quad):
    channels = quad.shape[-1]
    pairs = quad.reshape(8, 2, *quad.shape[1:])
    high = jnp.concatenate([pairs[:, 0, 20:24], pairs[:, 1, 20:24]], axis=1)
    low = jnp.concatenate([pairs[:, 0, 0:4], pairs[:, 1, 0:4]], axis=1)
    return piece_of(jnp.concatenate([high.reshape(64, channels), low.reshape(64, channels)], axis=0))


def quadrant_of(first, second, last):
    channels = first.shape[0]
    first = first.astype(F32).T.reshape(16, 8, channels)
    second = second.astype(F32).T.reshape(16, 8, channels)
    last = last.astype(F32).T
    high = last[:64].reshape(8, 8, channels)
    low = last[64:].reshape(8, 8, channels)
    even = jnp.concatenate([low[:, 0:4]], axis=1)
    odd = low[:, 4:8]
    low = jnp.stack([even, odd], axis=1).reshape(16, 4, channels)
    high = jnp.stack([high[:, 0:4], high[:, 4:8]], axis=1).reshape(16, 4, channels)
    whole = jnp.concatenate([low, first, second, high], axis=1)
    return whole.reshape(4, 4, 24, channels).astype(BF16)


def read_block(sources, buffer, sems, depth):
    copies = [
        pltpu.make_async_copy(
            source.at[pl.ds(2 * x, 2), :, pl.ds(0, depth)],
            buffer.at[which, pl.ds(2 * x, 2)],
            sems.at[which, x],
        )
        for which, source in enumerate(sources)
        for x in range(4)
    ]
    for copy in copies:
        copy.start()
    return copies


def pack_first_kernel(tokens_ref, cot_ref, *refs):
    outs, (buffer, sems) = refs[:4], refs[4:]
    copies = read_block((tokens_ref, cot_ref), buffer, sems, buffer.shape[3])
    for which in range(2):
        for copy in copies[4 * which : 4 * which + 4]:
            copy.wait()
        for i, quad in enumerate(quadrants(buffer[which].astype(F32))):
            outs[i][which] = piece_of(quad[:, 4:12])


def pack_rest_kernel(tokens_ref, cot_ref, *refs):
    outs, (buffer, sems) = refs[:4], refs[4:]
    copies = read_block((tokens_ref, cot_ref), buffer, sems, buffer.shape[3])
    for which in range(2):
        for copy in copies[4 * which : 4 * which + 4]:
            copy.wait()
        for i, quad in enumerate(quadrants(buffer[which].astype(F32))):
            outs[i][0, which] = last_piece_of(quad)
            outs[i][1, which] = piece_of(quad[:, 12:20])


def packed(tokens, cotangent, first):
    tile_x, tile_y, depth, channels = tokens.shape
    piece = (2, channels, LANES)
    shape = piece if first else (2, *piece)
    held = 2 * WIN if first else depth
    return pl.pallas_call(
        pack_first_kernel if first else pack_rest_kernel,
        out_shape=(jax.ShapeDtypeStruct(shape, BF16),) * 4,
        in_specs=[pl.BlockSpec(memory_space=pltpu.HBM)] * 2,
        out_specs=(VMEM,) * 4,
        scratch_shapes=[
            pltpu.VMEM((2, tile_x, tile_y, held, channels), BF16),
            pltpu.SemaphoreType.DMA((2, 4)),
        ],
        compiler_params=pltpu.CompilerParams(vmem_limit_bytes=62 * 2**20),
        name="pack_first" if first else "pack_rest",
    )(tokens, cotangent)


def prepare_kernel(
    gain_ref, bias_ref, wqkv_ref, proj_ref,
    gain_out, bias_out, wqkv_t_out, proj_t_out, kf_out, qf_out,
):
    gain_out[...] = gain_ref[...].T
    bias_out[...] = bias_ref[...].T
    wqkv_t_out[...] = wqkv_ref[...].astype(F32).T.astype(BF16)
    proj_t_out[...] = proj_ref[...].astype(F32).T.astype(BF16)
    edge_x = lax.axis_index("gx") == lax.axis_size("gx") - 1
    edge_y = lax.axis_index("gy") == lax.axis_size("gy") - 1
    shape = kf_out.shape[1:]
    row = lax.broadcasted_iota(jnp.int32, shape, 0)
    lane = lax.broadcasted_iota(jnp.int32, shape, 1)
    for layout, span in enumerate((LANES, LANES // 2)):
        quad = (lane // span) % 4
        far_x = jnp.where(jnp.logical_and(quad // 2 == 0, edge_x), 1.0, 0.0)
        far_y = jnp.where(jnp.logical_and(quad % 2 == 0, edge_y), 1.0, 0.0)
        key = jnp.where(row == 0, far_x, jnp.where(row == 1, 1 - far_x, jnp.where(row == 2, far_y, 1 - far_y)))
        query = jnp.where(row == 0, 1 - far_x, jnp.where(row == 1, far_x, jnp.where(row == 2, 1 - far_y, far_y)))
        kf_out[layout] = jnp.where(row < 4, key, 0.0).astype(BF16)
        qf_out[layout] = jnp.where(row < 4, query * -MASKED, 0.0).astype(BF16)


def prepared(gain, bias, wqkv, proj):
    channels = gain.shape[0]
    cells = 4 * LANES
    S = jax.ShapeDtypeStruct
    return pl.pallas_call(
        prepare_kernel,
        out_shape=(
            S((channels, 1), F32),
            S((channels, 1), F32),
            S((3 * channels, channels), BF16),
            S((channels, channels), BF16),
            S((2, 16, cells), BF16),
            S((2, 16, cells), BF16),
        ),
        in_specs=[VMEM] * 4,
        out_specs=(VMEM,) * 6,
        compiler_params=pltpu.CompilerParams(vmem_limit_bytes=40 * 2**20),
        name="prepare",
    )(gain[None], bias[None], wqkv, proj)


def unpack_kernel(*refs):
    paired, middle, outs = refs[:4], refs[4:8], refs[8:]
    for which, out in enumerate(outs):
        for xh in range(2):
            for yh in range(2):
                i = xh * 2 + yh
                quad = quadrant_of(paired[i][0, which], middle[i][which], paired[i][1, which])
                out[xh * 4 : xh * 4 + 4, yh * 4 : yh * 4 + 4] = quad


def unpacked(paired, middle, shape):
    return pl.pallas_call(
        unpack_kernel,
        out_shape=(jax.ShapeDtypeStruct(shape, BF16),) * 2,
        in_specs=[VMEM] * 8,
        out_specs=(VMEM,) * 2,
        compiler_params=pltpu.CompilerParams(vmem_limit_bytes=40 * 2**20),
        name="unpack",
    )(*paired, *middle)


def attend_kernel(
    turn,
    q00_ref, q01_ref, q10_ref, q11_ref,
    kf_ref, qf_ref, gain_ref, bias_ref, wqkv_t_ref, wqkv_ref, proj_ref, proj_t_ref,
    *refs,
):
    halves = turn == 1
    given = (0, 5, 1)[turn]
    earlier_refs, refs = refs[:given], refs[given:]
    y_refs, grads_ref, scratch = refs[:4], refs[4], refs[5:]
    (qkv_s, gm_s, mix_s, gqkv_s, k_s, q_s, v_s, g_s, e_s, p_s, pb_s, dp_s, ds_s, dst_s, r_s, d_s) = scratch
    quads = (q00_ref, q01_ref, q10_ref, q11_ref)
    if turn:
        quads = [quad.at[turn - 1] for quad in quads]
    channels = q00_ref.shape[-2]
    hd = channels // HEADS
    cells = 4 * LANES
    half = LANES // 2

    def whole(which):
        if halves:
            parts = [q[which].astype(F32) for q in quads]
            return jnp.concatenate(
                [p[:, :half] for p in parts] + [p[:, half:] for p in parts], axis=1
            )
        return jnp.concatenate([q[which].astype(F32) for q in quads], axis=1)

    xf = whole(0)
    gf = whole(1)
    g = gf.astype(BF16)
    mean = jnp.mean(xf, axis=0, keepdims=True)
    centered = xf - mean
    var = jnp.mean(centered * centered, axis=0, keepdims=True)
    inv = lax.rsqrt(var + 1e-5)
    std = centered * inv
    gain = gain_ref[...]
    normed = (std * gain + bias_ref[...]).astype(BF16)
    qkv = dot(wqkv_t_ref[...], normed).astype(BF16)
    qkv_s[...] = qkv
    gm_s[...] = dot(proj_ref[...], g).astype(BF16)

    layout = 1 if halves else 0
    size = cells // 2 if halves else cells
    groups = [slice(start, start + size) for start in range(0, cells, size)]
    chunks = [
        (gi, slice(c, c + LANES), slice(c - group.start, c - group.start + LANES), group)
        for gi, group in enumerate(groups)
        for c in range(group.start, group.stop, LANES)
    ]
    part = cells // 2
    parts = [
        (groups[min(i, len(groups) - 1)], slice(i * part, (i + 1) * part),
         slice(i * part % size, i * part % size + part))
        for i in range(2)
    ]
    scale = hd**-0.5

    def head_rows(base, h):
        if isinstance(h, int):
            return slice(base + h * hd, base + (h + 1) * hd)
        return pl.ds(pl.multiple_of(base + h * hd, hd), hd)

    def q_rows(h):
        return head_rows(0, h)

    def k_rows(h):
        return head_rows(channels, h)

    def v_rows(h):
        return head_rows(2 * channels, h)

    def folded(x):
        return jnp.sum(x.reshape(-1, 8, x.shape[-1]), axis=0)

    def added(total, gi, x):
        total[gi] = x if total[gi] is None else total[gi] + x

    def prepare(h, slot):
        k = qkv_s[k_rows(h)]
        qf = qkv_s[q_rows(h)].astype(F32) * (scale * LOG2E)
        q_hi = qf.astype(BF16)
        q_lo = (qf - q_hi.astype(F32)).astype(BF16)
        k_s[slot] = jnp.concatenate([k, k, kf_ref[layout]], axis=0).T
        q_s[slot] = jnp.concatenate([q_hi, q_lo, qf_ref[layout]], axis=0)
        v_s[slot] = qkv_s[v_rows(h)].T
        g_s[slot] = gm_s[q_rows(h)]

    def exponentials(slot, chunk, total):
        gi, rows, _, cols = chunk
        e = jnp.exp2(dot(k_s[slot, rows], q_s[slot, :, cols]))
        e_s[slot, rows] = e
        added(total, gi, folded(e))

    def attention(slot, chunk, total):
        gi, rows, _, cols = chunk
        p = e_s[slot, rows] * r_s[slot, 0:1, cols]
        p_s[slot, rows] = p
        pb_s[slot, rows] = p.astype(BF16)
        dp = dot(v_s[slot, rows], g_s[slot, :, cols])
        dp_s[slot, rows] = dp
        added(total, gi, folded(p * dp))

    def grad_scores(slot, chunk):
        _, rows, place, cols = chunk
        ds = (p_s[slot, rows] * (dp_s[slot, rows] - d_s[slot, 0:1, cols])).astype(BF16)
        ds_s[slot, rows] = ds
        dst_s[slot, cols, place] = ds.T

    def mixed_part(h, slot, i):
        over, out, place = parts[i]
        mix_s[q_rows(h), out] = dot(qkv_s[v_rows(h), over], pb_s[slot, over, place]).astype(BF16)

    def grad_values_part(h, slot, i):
        over, out, _ = parts[i]
        gv = lax.dot_general(
            gm_s[q_rows(h), over], pb_s[slot, out], NT, preferred_element_type=F32
        )
        gqkv_s[v_rows(h), out] = gv.astype(BF16)

    def grad_queries_part(h, slot, i):
        over, out, place = parts[i]
        gq = dot(qkv_s[k_rows(h), over], ds_s[slot, over, place]) * scale
        gqkv_s[q_rows(h), out] = gq.astype(BF16)

    def grad_keys_part(h, slot, i):
        over, out, place = parts[i]
        gk = dot(qkv_s[q_rows(h), over], dst_s[slot, over, place]) * scale
        gqkv_s[k_rows(h), out] = gk.astype(BF16)

    def kept(ref, slot, total, of):
        for gi, cols in enumerate(groups):
            ref[slot, 0:1, cols] = of(jnp.sum(total[gi], axis=0, keepdims=True))

    def step(i, slot, one=True, two=True, three=True, four=True, ahead=True):
        sums = [None] * len(groups)
        inner = [None] * len(groups)
        for c, chunk in enumerate(chunks):
            if c % 2 == 0 and three:
                mixed_part(i - 2, slot, c // 2)
                grad_values_part(i - 2, slot, c // 2)
            if c % 2 == 1 and four:
                grad_queries_part(i - 3, 1 - slot, c // 2)
                grad_keys_part(i - 3, 1 - slot, c // 2)
            if one:
                exponentials(slot, chunk, sums)
            if two:
                attention(1 - slot, chunk, inner)
            if three:
                grad_scores(slot, chunk)
        if one:
            kept(r_s, slot, sums, lambda total: 1.0 / total)
        if two:
            kept(d_s, 1 - slot, inner, lambda total: total)
        if ahead:
            prepare(i + 1, 1 - slot)

    squares = jnp.square(qkv[: 2 * channels].astype(F32)).reshape(2 * HEADS, hd, cells)
    longest = jnp.max(jnp.sum(squares, axis=1), axis=1, keepdims=True)
    bound = jnp.max(longest[:HEADS] * longest[HEADS:]) * (scale * LOG2E) ** 2
    in_range = bound <= 110.0**2

    @pl.when(in_range)
    def _():
        prepare(0, 0)
        step(0, 0, two=False, three=False, four=False)
        step(1, 1, three=False, four=False)
        step(2, 0, four=False)

        def two_steps(j, carry):
            step(3 + 2 * j, 1)
            step(4 + 2 * j, 0)
            return carry

        lax.fori_loop(0, (HEADS - 4) // 2, two_steps, 0)
        step(HEADS - 1, 1, ahead=False)
        step(HEADS, 0, one=False, ahead=False)
        step(HEADS + 1, 1, one=False, two=False, ahead=False)
        step(HEADS + 2, 0, one=False, two=False, three=False, ahead=False)

    @pl.when(jnp.logical_not(in_range))
    def _():
        def head(h, carry):
            prepare(h, 0)
            for cols in groups:
                s = dot(k_s[0, cols], q_s[0, :, cols])
                e = jnp.exp2(s - jnp.max(s, axis=0, keepdims=True))
                p = e * (1.0 / jnp.sum(e, axis=0, keepdims=True))
                pb_s[0, cols] = p.astype(BF16)
                dp = dot(v_s[0, cols], g_s[0, :, cols])
                inner = jnp.sum(p * dp, axis=0, keepdims=True)
                ds = (p * (dp - inner)).astype(BF16)
                ds_s[0, cols] = ds
                dst_s[0, cols] = ds.T
            for i in range(2):
                mixed_part(h, 0, i)
                grad_values_part(h, 0, i)
                grad_queries_part(h, 0, i)
                grad_keys_part(h, 0, i)
            return carry

        lax.fori_loop(0, HEADS, head, 0)

    mixed = mix_s[...]
    block_out = xf + dot(proj_t_ref[...], mixed)
    gqkv = gqkv_s[...]
    gn = dot(wqkv_ref[...], gqkv)
    scaled = gn * gain
    gx = inv * (
        scaled
        - jnp.mean(scaled, axis=0, keepdims=True)
        - std * jnp.mean(scaled * std, axis=0, keepdims=True)
    )
    d_tokens = gf + gx
    for which, y in enumerate((block_out, d_tokens)):
        for i, ref in enumerate(y_refs):
            if halves:
                lo = y[:, i * half : (i + 1) * half]
                hi = y[:, cells // 2 + i * half : cells // 2 + (i + 1) * half]
                part = jnp.concatenate([lo, hi], axis=1)
            else:
                part = y[:, i * LANES : (i + 1) * LANES]
            if turn == 1:
                ref[0, which] = earlier_refs[i][which]
                ref[1, which] = part.astype(BF16)
            else:
                ref[which] = part.astype(BF16)

    dw = lax.dot_general(normed, gqkv, NT, preferred_element_type=F32)
    dproj = lax.dot_general(mixed, g, NT, preferred_element_type=F32)
    dgain = jnp.sum(gn * std, axis=1, keepdims=True)
    dbias = jnp.sum(gn, axis=1, keepdims=True)
    joined = jnp.concatenate([dw, dproj], axis=1)
    blocks = [joined[:, i * LANES : (i + 1) * LANES] for i in range(joined.shape[1] // LANES)]
    lane = lax.broadcasted_iota(jnp.int32, (channels, LANES), 1)
    tail = jnp.where(lane == 0, dgain, jnp.where(lane == 1, dbias, 0.0)).T[:8]
    used = len(blocks) * channels
    grads = jnp.concatenate(blocks, axis=0)
    pad = jnp.zeros((8, 2 * LANES - channels), F32)
    extra = jnp.concatenate(
        [tail[:, :LANES], jnp.concatenate([tail[:, LANES:], pad], axis=1)], axis=0
    )
    if turn:
        grads = grads + earlier_refs[-1][:used]
        extra = extra + earlier_refs[-1][used : used + 16]
    grads_ref[:used] = grads.astype(grads_ref.dtype)
    grads_ref[used : used + 16] = extra.astype(grads_ref.dtype)
    grads_ref[used + 16 :] = jnp.zeros(
        (grads_ref.shape[0] - used - 16, LANES), grads_ref.dtype
    )


GRAD_ROWS = 1280


def attend(turn, quads, features, weights, earlier):
    channels = quads[0].shape[-2]
    cells = 4 * LANES
    width = cells // 2 if turn == 1 else cells
    S = jax.ShapeDtypeStruct
    piece = (2, channels, LANES)
    return pl.pallas_call(
        functools.partial(attend_kernel, turn),
        out_shape=(S((2, *piece) if turn == 1 else piece, BF16),) * 4
        + (S((GRAD_ROWS, LANES), BF16 if turn == 2 else F32),),
        in_specs=[VMEM] * (12 + len(earlier)),
        out_specs=(VMEM,) * 5,
        scratch_shapes=[
            pltpu.VMEM((3 * channels, cells), BF16),
            pltpu.VMEM((channels, cells), BF16),
            pltpu.VMEM((channels, cells), BF16),
            pltpu.VMEM((3 * channels, cells), BF16),
            pltpu.VMEM((2, cells, 48), BF16),
            pltpu.VMEM((2, 48, cells), BF16),
            pltpu.VMEM((2, cells, 16), BF16),
            pltpu.VMEM((2, 16, cells), BF16),
            pltpu.VMEM((2, cells, width), F32),
            pltpu.VMEM((2, cells, width), F32),
            pltpu.VMEM((2, cells, width), BF16),
            pltpu.VMEM((2, cells, width), F32),
            pltpu.VMEM((2, cells, width), BF16),
            pltpu.VMEM((2, cells, width), BF16),
            pltpu.VMEM((2, 8, cells), F32),
            pltpu.VMEM((2, 8, cells), F32),
        ],
        compiler_params=pltpu.CompilerParams(vmem_limit_bytes=40 * 2**20),
        cost_estimate=pl.CostEstimate(
            flops=12 * 12 * 512 * 512 * 256, bytes_accessed=4 * 2**20, transcendentals=12 * 512 * 512
        ),
        name="attend",
    )(*quads, *features, *weights, *earlier)


def moved(block, step_x, step_y):
    nx, ny = lax.axis_size("gx"), lax.axis_size("gy")
    route = []
    for i in range(nx):
        for j in range(ny):
            to = ((i + step_x) % nx) * ny + (j + step_y) % ny
            route.append((i * ny + j, to))
    return lax.ppermute(block, ("gx", "gy"), route)


def summed(rows, beside):
    nx, ny = lax.axis_size("gx"), lax.axis_size("gy")
    near = 2 * ny
    planes = [[near * i + j for j in range(near)] for i in range(nx // 2)]
    across = [list(ids) for ids in zip(*planes)]
    beside = list(beside)

    def exchanged(pieces, groups, turn):
        got = lax.all_to_all(pieces, ("gx", "gy"), 0, 0, axis_index_groups=groups)
        if turn < 2:
            got, beside[turn] = lax.optimization_barrier((got, beside[turn]))
        return got

    def copies(piece, count):
        return jnp.broadcast_to(piece[None], (count, *piece.shape))

    got = exchanged(rows.reshape(near, -1, LANES), planes, 0)
    mine = jnp.sum(got.astype(F32), axis=0).astype(BF16)
    got = exchanged(copies(mine, nx // 2), across, 1)
    total = jnp.sum(got.astype(F32), axis=0).astype(BF16)
    return exchanged(copies(total, near), planes, 2).reshape(rows.shape), beside


def grads_kernel(factor, rows_ref, dw_ref, dproj_ref, gain_ref, bias_ref):
    channels = dw_ref.shape[0]
    blocks = 4 * channels // LANES
    joined = jnp.concatenate(
        [rows_ref[i * channels : (i + 1) * channels].astype(F32) for i in range(blocks)], axis=1
    ) * factor
    dw_ref[...] = joined[:, : 3 * channels]
    dproj_ref[...] = joined[:, 3 * channels :]
    used = blocks * channels
    tail = rows_ref[used : used + 16].astype(F32) * factor
    tail = jnp.concatenate([tail[:8], tail[8:]], axis=1)[:, :channels]
    gain_ref[...] = tail[0:1]
    bias_ref[...] = tail[1:2]


def grads_of(rows, channels, factor):
    S = jax.ShapeDtypeStruct
    return pl.pallas_call(
        functools.partial(grads_kernel, factor),
        out_shape=(
            S((channels, 3 * channels), F32),
            S((channels, channels), F32),
            S((1, channels), F32),
            S((1, channels), F32),
        ),
        in_specs=[VMEM],
        out_specs=(VMEM,) * 4,
        name="unpack_grads",
    )(rows)


def shards(tokens, cotangent, ln_gain, ln_bias, qkv_weight, proj_weight):
    tile_x, tile_y, depth, channels = tokens.shape
    nx, ny = lax.axis_size("gx"), lax.axis_size("gy")
    first = packed(tokens, cotangent, True)
    first, tokens, cotangent, ln_gain, ln_bias, qkv_weight, proj_weight = lax.optimization_barrier(
        (first, tokens, cotangent, ln_gain, ln_bias, qkv_weight, proj_weight)
    )
    rest = packed(tokens, cotangent, False)
    gain, bias, wqkv_t, proj_t, *features = prepared(ln_gain, ln_bias, qkv_weight, proj_weight)
    weights = (gain, bias, wqkv_t, qkv_weight, proj_weight, proj_t)

    steps = ((1, 1), (1, 0), (0, 1))

    def gathered(quads):
        return [moved(quad, -x, -y) for quad, (x, y) in zip(quads, steps)] + [quads[3]]

    def returned(quads):
        return [moved(quad, x, y) for quad, (x, y) in zip(quads, steps)] + [quads[3]]

    first, rest = gathered(first), gathered(rest)
    *y, sums = attend(0, first, features, weights, ())
    *y, sums = attend(1, rest, features, weights, (*y, sums))
    paired = returned(y)
    *y, sums = attend(2, rest, features, weights, (sums,))
    middle = returned(y)
    sums, paired = lax.optimization_barrier((sums, paired))
    total, middle[:3] = summed(sums, middle[:3])
    block_out, d_tokens = unpacked(paired, middle, tokens.shape)
    factor = 1.0 / math.sqrt(tile_x * nx * tile_y * ny * depth)
    dw, dproj, dgain, dbias = grads_of(total, channels, factor)
    return block_out, d_tokens, dw, dproj, dgain[0], dbias[0]


def solution(mesh):
    placed = (P("gx", "gy", None, None), P("gx", "gy", None, None), P(), P(), P(), P())
    return jax.shard_map(
        shards,
        mesh=mesh,
        in_specs=placed,
        out_specs=(P("gx", "gy", None, None), P("gx", "gy", None, None), P(), P(), P(), P()),
        check_vma=False,
    )
```

```python
import functools
import math

import jax
import jax.numpy as jnp
from jax import lax
from jax.experimental import pallas as pl
from jax.experimental.pallas import tpu as pltpu
from jax.sharding import PartitionSpec as P

HEADS = 12
WIN = 8
SHIFT = 4
F32 = jnp.float32
BF16 = jnp.bfloat16
LOG2E = math.log2(math.e)
MASKED = 2.0**100
LANES = 128
VMEM = pl.BlockSpec(memory_space=pltpu.VMEM)

NT = (((1,), (1,)), ((), ()))
TN = (((0,), (0,)), ((), ()))


def dot(a, b):
    return jnp.dot(a, b, preferred_element_type=F32)


def quadrants(block):
    shape = (16, *block.shape[2:])
    return [
        block[x : x + 4, y : y + 4].reshape(shape) for x in (0, 4) for y in (0, 4)
    ]


def piece_of(cells):
    return cells.reshape(LANES, cells.shape[-1]).T.astype(BF16)


def last_piece_of(quad):
    channels = quad.shape[-1]
    pairs = quad.reshape(8, 2, *quad.shape[1:])
    high = jnp.concatenate([pairs[:, 0, 20:24], pairs[:, 1, 20:24]], axis=1)
    low = jnp.concatenate([pairs[:, 0, 0:4], pairs[:, 1, 0:4]], axis=1)
    return piece_of(jnp.concatenate([high.reshape(64, channels), low.reshape(64, channels)], axis=0))


def quadrant_of(first, second, last):
    channels = first.shape[0]
    first = first.astype(F32).T.reshape(16, 8, channels)
    second = second.astype(F32).T.reshape(16, 8, channels)
    last = last.astype(F32).T
    high = last[:64].reshape(8, 8, channels)
    low = last[64:].reshape(8, 8, channels)
    even = jnp.concatenate([low[:, 0:4]], axis=1)
    odd = low[:, 4:8]
    low = jnp.stack([even, odd], axis=1).reshape(16, 4, channels)
    high = jnp.stack([high[:, 0:4], high[:, 4:8]], axis=1).reshape(16, 4, channels)
    whole = jnp.concatenate([low, first, second, high], axis=1)
    return whole.reshape(4, 4, 24, channels).astype(BF16)


def read_block(sources, buffer, sems, depth):
    copies = [
        pltpu.make_async_copy(
            source.at[pl.ds(2 * x, 2), :, pl.ds(0, depth)],
            buffer.at[which, pl.ds(2 * x, 2)],
            sems.at[which, x],
        )
        for which, source in enumerate(sources)
        for x in range(4)
    ]
    for copy in copies:
        copy.start()
    return copies


def pack_first_kernel(tokens_ref, cot_ref, *refs):
    outs, (buffer, sems) = refs[:4], refs[4:]
    copies = read_block((tokens_ref, cot_ref), buffer, sems, buffer.shape[3])
    for which in range(2):
        for copy in copies[4 * which : 4 * which + 4]:
            copy.wait()
        for i, quad in enumerate(quadrants(buffer[which].astype(F32))):
            outs[i][which] = piece_of(quad[:, 4:12])


def pack_rest_kernel(tokens_ref, cot_ref, *refs):
    outs, (buffer, sems) = refs[:4], refs[4:]
    copies = read_block((tokens_ref, cot_ref), buffer, sems, buffer.shape[3])
    for which in range(2):
        for copy in copies[4 * which : 4 * which + 4]:
            copy.wait()
        for i, quad in enumerate(quadrants(buffer[which].astype(F32))):
            outs[i][0, which] = last_piece_of(quad)
            outs[i][1, which] = piece_of(quad[:, 12:20])


def packed(tokens, cotangent, first):
    tile_x, tile_y, depth, channels = tokens.shape
    piece = (2, channels, LANES)
    shape = piece if first else (2, *piece)
    held = 2 * WIN if first else depth
    return pl.pallas_call(
        pack_first_kernel if first else pack_rest_kernel,
        out_shape=(jax.ShapeDtypeStruct(shape, BF16),) * 4,
        in_specs=[pl.BlockSpec(memory_space=pltpu.HBM)] * 2,
        out_specs=(VMEM,) * 4,
        scratch_shapes=[
            pltpu.VMEM((2, tile_x, tile_y, held, channels), BF16),
            pltpu.SemaphoreType.DMA((2, 4)),
        ],
        compiler_params=pltpu.CompilerParams(vmem_limit_bytes=62 * 2**20),
        name="pack_first" if first else "pack_rest",
    )(tokens, cotangent)


def prepare_kernel(
    gain_ref, bias_ref, wqkv_ref, proj_ref,
    gain_out, bias_out, wqkv_t_out, proj_t_out, kf_out, qf_out,
):
    gain_out[...] = gain_ref[...].T
    bias_out[...] = bias_ref[...].T
    wqkv_t_out[...] = wqkv_ref[...].astype(F32).T.astype(BF16)
    proj_t_out[...] = proj_ref[...].astype(F32).T.astype(BF16)
    edge_x = lax.axis_index("gx") == lax.axis_size("gx") - 1
    edge_y = lax.axis_index("gy") == lax.axis_size("gy") - 1
    shape = kf_out.shape[1:]
    row = lax.broadcasted_iota(jnp.int32, shape, 0)
    lane = lax.broadcasted_iota(jnp.int32, shape, 1)
    for layout, span in enumerate((LANES, LANES // 2)):
        quad = (lane // span) % 4
        far_x = jnp.where(jnp.logical_and(quad // 2 == 0, edge_x), 1.0, 0.0)
        far_y = jnp.where(jnp.logical_and(quad % 2 == 0, edge_y), 1.0, 0.0)
        key = jnp.where(row == 0, far_x, jnp.where(row == 1, 1 - far_x, jnp.where(row == 2, far_y, 1 - far_y)))
        query = jnp.where(row == 0, 1 - far_x, jnp.where(row == 1, far_x, jnp.where(row == 2, 1 - far_y, far_y)))
        kf_out[layout] = jnp.where(row < 4, key, 0.0).astype(BF16)
        qf_out[layout] = jnp.where(row < 4, query * -MASKED, 0.0).astype(BF16)


def prepared(gain, bias, wqkv, proj):
    channels = gain.shape[0]
    cells = 4 * LANES
    S = jax.ShapeDtypeStruct
    return pl.pallas_call(
        prepare_kernel,
        out_shape=(
            S((channels, 1), F32),
            S((channels, 1), F32),
            S((3 * channels, channels), BF16),
            S((channels, channels), BF16),
            S((2, 16, cells), BF16),
            S((2, 16, cells), BF16),
        ),
        in_specs=[VMEM] * 4,
        out_specs=(VMEM,) * 6,
        compiler_params=pltpu.CompilerParams(vmem_limit_bytes=40 * 2**20),
        name="prepare",
    )(gain[None], bias[None], wqkv, proj)


def unpack_kernel(low_y_ref, paired_low, paired_high, middle_low, middle_high, *outs):
    for which, out in enumerate(outs):
        for xh, (paired, middle) in enumerate(
            ((paired_low, middle_low), (paired_high, middle_high))
        ):
            for yh in range(2):
                if yh:
                    first, last = paired[1, 0, which], paired[1, 1, which]
                    second = middle[1, which]
                else:
                    first, last = low_y_ref[2 * xh, which], low_y_ref[2 * xh + 1, which]
                    second = low_y_ref[4 + xh, which]
                quad = quadrant_of(first, second, last)
                out[xh * 4 : xh * 4 + 4, yh * 4 : yh * 4 + 4] = quad


def unpacked(low_y, paired, middle, shape):
    return pl.pallas_call(
        unpack_kernel,
        out_shape=(jax.ShapeDtypeStruct(shape, BF16),) * 2,
        in_specs=[VMEM] * 5,
        out_specs=(VMEM,) * 2,
        compiler_params=pltpu.CompilerParams(vmem_limit_bytes=40 * 2**20),
        name="unpack",
    )(low_y, *paired, *middle)


def attend_kernel(
    turn,
    q00_ref, q01_ref, q10_ref, q11_ref,
    kf_ref, qf_ref, gain_ref, bias_ref, wqkv_t_ref, wqkv_ref, proj_ref, proj_t_ref,
    *refs,
):
    halves = turn == 1
    given = (0, 3, 1)[turn]
    earlier_refs, refs = refs[:given], refs[given:]
    y_refs, grads_ref, scratch = refs[:2], refs[2], refs[3:]
    (qkv_s, gm_s, mix_s, gqkv_s, k_s, q_s, v_s, g_s, e_s, p_s, pb_s, dp_s, ds_s, dst_s, r_s, d_s) = scratch
    quads = (q00_ref, q01_ref, q10_ref, q11_ref)
    if turn:
        quads = [quad.at[turn - 1] for quad in quads]
    channels = q00_ref.shape[-2]
    hd = channels // HEADS
    cells = 4 * LANES
    half = LANES // 2

    def whole(which):
        if halves:
            parts = [q[which].astype(F32) for q in quads]
            return jnp.concatenate(
                [p[:, :half] for p in parts] + [p[:, half:] for p in parts], axis=1
            )
        return jnp.concatenate([q[which].astype(F32) for q in quads], axis=1)

    xf = whole(0)
    gf = whole(1)
    g = gf.astype(BF16)
    mean = jnp.mean(xf, axis=0, keepdims=True)
    centered = xf - mean
    var = jnp.mean(centered * centered, axis=0, keepdims=True)
    inv = lax.rsqrt(var + 1e-5)
    std = centered * inv
    gain = gain_ref[...]
    normed = (std * gain + bias_ref[...]).astype(BF16)
    qkv = dot(wqkv_t_ref[...], normed).astype(BF16)
    qkv_s[...] = qkv
    gm_s[...] = dot(proj_ref[...], g).astype(BF16)

    layout = 1 if halves else 0
    size = cells // 2 if halves else cells
    groups = [slice(start, start + size) for start in range(0, cells, size)]
    chunks = [
        (gi, slice(c, c + LANES), slice(c - group.start, c - group.start + LANES), group)
        for gi, group in enumerate(groups)
        for c in range(group.start, group.stop, LANES)
    ]
    part = cells // 2
    parts = [
        (groups[min(i, len(groups) - 1)], slice(i * part, (i + 1) * part),
         slice(i * part % size, i * part % size + part))
        for i in range(2)
    ]
    scale = hd**-0.5

    def head_rows(base, h):
        if isinstance(h, int):
            return slice(base + h * hd, base + (h + 1) * hd)
        return pl.ds(pl.multiple_of(base + h * hd, hd), hd)

    def q_rows(h):
        return head_rows(0, h)

    def k_rows(h):
        return head_rows(channels, h)

    def v_rows(h):
        return head_rows(2 * channels, h)

    def folded(x):
        return jnp.sum(x.reshape(-1, 8, x.shape[-1]), axis=0)

    def added(total, gi, x):
        total[gi] = x if total[gi] is None else total[gi] + x

    def prepare(h, slot):
        k = qkv_s[k_rows(h)]
        qf = qkv_s[q_rows(h)].astype(F32) * (scale * LOG2E)
        q_hi = qf.astype(BF16)
        q_lo = (qf - q_hi.astype(F32)).astype(BF16)
        k_s[slot] = jnp.concatenate([k, k, kf_ref[layout]], axis=0).T
        q_s[slot] = jnp.concatenate([q_hi, q_lo, qf_ref[layout]], axis=0)
        v_s[slot] = qkv_s[v_rows(h)].T
        g_s[slot] = gm_s[q_rows(h)]

    def exponentials(slot, chunk, total):
        gi, rows, _, cols = chunk
        e = jnp.exp2(dot(k_s[slot, rows], q_s[slot, :, cols]))
        e_s[slot, rows] = e
        added(total, gi, folded(e))

    def attention(slot, chunk, total):
        gi, rows, _, cols = chunk
        p = e_s[slot, rows] * r_s[slot, 0:1, cols]
        p_s[slot, rows] = p
        pb_s[slot, rows] = p.astype(BF16)
        dp = dot(v_s[slot, rows], g_s[slot, :, cols])
        dp_s[slot, rows] = dp
        added(total, gi, folded(p * dp))

    def grad_scores(slot, chunk):
        _, rows, place, cols = chunk
        ds = (p_s[slot, rows] * (dp_s[slot, rows] - d_s[slot, 0:1, cols])).astype(BF16)
        ds_s[slot, rows] = ds
        dst_s[slot, cols, place] = ds.T

    def mixed_part(h, slot, i):
        over, out, place = parts[i]
        mix_s[q_rows(h), out] = dot(qkv_s[v_rows(h), over], pb_s[slot, over, place]).astype(BF16)

    def grad_values_part(h, slot, i):
        over, out, _ = parts[i]
        gv = lax.dot_general(
            gm_s[q_rows(h), over], pb_s[slot, out], NT, preferred_element_type=F32
        )
        gqkv_s[v_rows(h), out] = gv.astype(BF16)

    def grad_queries_part(h, slot, i):
        over, out, place = parts[i]
        gq = dot(qkv_s[k_rows(h), over], ds_s[slot, over, place]) * scale
        gqkv_s[q_rows(h), out] = gq.astype(BF16)

    def grad_keys_part(h, slot, i):
        over, out, place = parts[i]
        gk = dot(qkv_s[q_rows(h), over], dst_s[slot, over, place]) * scale
        gqkv_s[k_rows(h), out] = gk.astype(BF16)

    def kept(ref, slot, total, of):
        for gi, cols in enumerate(groups):
            ref[slot, 0:1, cols] = of(jnp.sum(total[gi], axis=0, keepdims=True))

    def step(i, slot, one=True, two=True, three=True, four=True, ahead=True):
        sums = [None] * len(groups)
        inner = [None] * len(groups)
        for c, chunk in enumerate(chunks):
            if c % 2 == 0 and three:
                mixed_part(i - 2, slot, c // 2)
                grad_values_part(i - 2, slot, c // 2)
            if c % 2 == 1 and four:
                grad_queries_part(i - 3, 1 - slot, c // 2)
                grad_keys_part(i - 3, 1 - slot, c // 2)
            if one:
                exponentials(slot, chunk, sums)
            if two:
                attention(1 - slot, chunk, inner)
            if three:
                grad_scores(slot, chunk)
        if one:
            kept(r_s, slot, sums, lambda total: 1.0 / total)
        if two:
            kept(d_s, 1 - slot, inner, lambda total: total)
        if ahead:
            prepare(i + 1, 1 - slot)

    squares = jnp.square(qkv[: 2 * channels].astype(F32)).reshape(2 * HEADS, hd, cells)
    longest = jnp.max(jnp.sum(squares, axis=1), axis=1, keepdims=True)
    bound = jnp.max(longest[:HEADS] * longest[HEADS:]) * (scale * LOG2E) ** 2
    in_range = bound <= 110.0**2

    @pl.when(in_range)
    def _():
        prepare(0, 0)
        step(0, 0, two=False, three=False, four=False)
        step(1, 1, three=False, four=False)
        step(2, 0, four=False)

        def two_steps(j, carry):
            step(3 + 2 * j, 1)
            step(4 + 2 * j, 0)
            return carry

        lax.fori_loop(0, (HEADS - 4) // 2, two_steps, 0)
        step(HEADS - 1, 1, ahead=False)
        step(HEADS, 0, one=False, ahead=False)
        step(HEADS + 1, 1, one=False, two=False, ahead=False)
        step(HEADS + 2, 0, one=False, two=False, three=False, ahead=False)

    @pl.when(jnp.logical_not(in_range))
    def _():
        def head(h, carry):
            prepare(h, 0)
            for cols in groups:
                s = dot(k_s[0, cols], q_s[0, :, cols])
                e = jnp.exp2(s - jnp.max(s, axis=0, keepdims=True))
                p = e * (1.0 / jnp.sum(e, axis=0, keepdims=True))
                pb_s[0, cols] = p.astype(BF16)
                dp = dot(v_s[0, cols], g_s[0, :, cols])
                inner = jnp.sum(p * dp, axis=0, keepdims=True)
                ds = (p * (dp - inner)).astype(BF16)
                ds_s[0, cols] = ds
                dst_s[0, cols] = ds.T
            for i in range(2):
                mixed_part(h, 0, i)
                grad_values_part(h, 0, i)
                grad_queries_part(h, 0, i)
                grad_keys_part(h, 0, i)
            return carry

        lax.fori_loop(0, HEADS, head, 0)

    mixed = mix_s[...]
    block_out = xf + dot(proj_t_ref[...], mixed)
    gqkv = gqkv_s[...]
    gn = dot(wqkv_ref[...], gqkv)
    scaled = gn * gain
    gx = inv * (
        scaled
        - jnp.mean(scaled, axis=0, keepdims=True)
        - std * jnp.mean(scaled * std, axis=0, keepdims=True)
    )
    d_tokens = gf + gx
    for which, y in enumerate((block_out, d_tokens)):
        for i in range(4):
            ref, yh = y_refs[i // 2], i % 2
            if halves:
                lo = y[:, i * half : (i + 1) * half]
                hi = y[:, cells // 2 + i * half : cells // 2 + (i + 1) * half]
                part = jnp.concatenate([lo, hi], axis=1)
                ref[yh, 0, which] = earlier_refs[i // 2][yh, which]
                ref[yh, 1, which] = part.astype(BF16)
            else:
                ref[yh, which] = y[:, i * LANES : (i + 1) * LANES].astype(BF16)

    dw = lax.dot_general(normed, gqkv, NT, preferred_element_type=F32)
    dproj = lax.dot_general(mixed, g, NT, preferred_element_type=F32)
    dgain = jnp.sum(gn * std, axis=1, keepdims=True)
    dbias = jnp.sum(gn, axis=1, keepdims=True)
    joined = jnp.concatenate([dw, dproj], axis=1)
    blocks = [joined[:, i * LANES : (i + 1) * LANES] for i in range(joined.shape[1] // LANES)]
    lane = lax.broadcasted_iota(jnp.int32, (channels, LANES), 1)
    tail = jnp.where(lane == 0, dgain, jnp.where(lane == 1, dbias, 0.0)).T[:8]
    used = len(blocks) * channels
    grads = jnp.concatenate(blocks, axis=0)
    pad = jnp.zeros((8, 2 * LANES - channels), F32)
    extra = jnp.concatenate(
        [tail[:, :LANES], jnp.concatenate([tail[:, LANES:], pad], axis=1)], axis=0
    )
    if turn:
        grads = grads + earlier_refs[-1][:used]
        extra = extra + earlier_refs[-1][used : used + 16]
    grads_ref[:used] = grads.astype(grads_ref.dtype)
    grads_ref[used : used + 16] = extra.astype(grads_ref.dtype)
    grads_ref[used + 16 :] = jnp.zeros(
        (grads_ref.shape[0] - used - 16, LANES), grads_ref.dtype
    )


GRAD_ROWS = 1280


def attend(turn, quads, features, weights, earlier):
    channels = quads[0].shape[-2]
    cells = 4 * LANES
    width = cells // 2 if turn == 1 else cells
    S = jax.ShapeDtypeStruct
    piece = (2, channels, LANES)
    return pl.pallas_call(
        functools.partial(attend_kernel, turn),
        out_shape=(S((2, 2, *piece) if turn == 1 else (2, *piece), BF16),) * 2
        + (S((GRAD_ROWS, LANES), BF16 if turn == 2 else F32),),
        in_specs=[VMEM] * (12 + len(earlier)),
        out_specs=(VMEM,) * 3,
        scratch_shapes=[
            pltpu.VMEM((3 * channels, cells), BF16),
            pltpu.VMEM((channels, cells), BF16),
            pltpu.VMEM((channels, cells), BF16),
            pltpu.VMEM((3 * channels, cells), BF16),
            pltpu.VMEM((2, cells, 48), BF16),
            pltpu.VMEM((2, 48, cells), BF16),
            pltpu.VMEM((2, cells, 16), BF16),
            pltpu.VMEM((2, 16, cells), BF16),
            pltpu.VMEM((2, cells, width), F32),
            pltpu.VMEM((2, cells, width), F32),
            pltpu.VMEM((2, cells, width), BF16),
            pltpu.VMEM((2, cells, width), F32),
            pltpu.VMEM((2, cells, width), BF16),
            pltpu.VMEM((2, cells, width), BF16),
            pltpu.VMEM((2, 8, cells), F32),
            pltpu.VMEM((2, 8, cells), F32),
        ],
        compiler_params=pltpu.CompilerParams(vmem_limit_bytes=40 * 2**20),
        cost_estimate=pl.CostEstimate(
            flops=12 * 12 * 512 * 512 * 256, bytes_accessed=4 * 2**20, transcendentals=12 * 512 * 512
        ),
        name="attend",
    )(*quads, *features, *weights, *earlier)


def moved(block, step_x, step_y):
    nx, ny = lax.axis_size("gx"), lax.axis_size("gy")
    route = []
    for i in range(nx):
        for j in range(ny):
            to = ((i + step_x) % nx) * ny + (j + step_y) % ny
            route.append((i * ny + j, to))
    return lax.ppermute(block, ("gx", "gy"), route)


def summed(rows, paired, middle):
    nx, ny = lax.axis_size("gx"), lax.axis_size("gy")
    near = 2 * ny
    planes = [[near * i + j for j in range(near)] for i in range(nx // 2)]
    across = [list(ids) for ids in zip(*planes)]

    def exchanged(pieces, groups):
        return lax.all_to_all(pieces, ("gx", "gy"), 0, 0, axis_index_groups=groups)

    def copies(piece, count):
        return jnp.broadcast_to(piece[None], (count, *piece.shape))

    got = exchanged(rows.reshape(near, -1, LANES), planes)
    middle = (moved(middle[0], 1, 0), middle[1])
    got, middle = lax.optimization_barrier((got, middle))
    mine = jnp.sum(got.astype(F32), axis=0).astype(BF16)
    got = exchanged(copies(mine, nx // 2), across)
    low_y = moved(jnp.concatenate([paired[0][0], paired[1][0], middle[0][:1], middle[1][:1]]), 0, 1)
    got, low_y = lax.optimization_barrier((got, low_y))
    total = jnp.sum(got.astype(F32), axis=0).astype(BF16)
    return exchanged(copies(total, near), planes).reshape(rows.shape), low_y, middle


def grads_kernel(factor, rows_ref, dw_ref, dproj_ref, gain_ref, bias_ref):
    channels = dw_ref.shape[0]
    blocks = 4 * channels // LANES
    joined = jnp.concatenate(
        [rows_ref[i * channels : (i + 1) * channels].astype(F32) for i in range(blocks)], axis=1
    ) * factor
    dw_ref[...] = joined[:, : 3 * channels]
    dproj_ref[...] = joined[:, 3 * channels :]
    used = blocks * channels
    tail = rows_ref[used : used + 16].astype(F32) * factor
    tail = jnp.concatenate([tail[:8], tail[8:]], axis=1)[:, :channels]
    gain_ref[...] = tail[0:1]
    bias_ref[...] = tail[1:2]


def grads_of(rows, channels, factor):
    S = jax.ShapeDtypeStruct
    return pl.pallas_call(
        functools.partial(grads_kernel, factor),
        out_shape=(
            S((channels, 3 * channels), F32),
            S((channels, channels), F32),
            S((1, channels), F32),
            S((1, channels), F32),
        ),
        in_specs=[VMEM],
        out_specs=(VMEM,) * 4,
        name="unpack_grads",
    )(rows)


def shards(tokens, cotangent, ln_gain, ln_bias, qkv_weight, proj_weight):
    tile_x, tile_y, depth, channels = tokens.shape
    nx, ny = lax.axis_size("gx"), lax.axis_size("gy")
    first = packed(tokens, cotangent, True)
    first, tokens, cotangent, ln_gain, ln_bias, qkv_weight, proj_weight = lax.optimization_barrier(
        (first, tokens, cotangent, ln_gain, ln_bias, qkv_weight, proj_weight)
    )
    rest = packed(tokens, cotangent, False)
    gain, bias, wqkv_t, proj_t, *features = prepared(ln_gain, ln_bias, qkv_weight, proj_weight)
    weights = (gain, bias, wqkv_t, qkv_weight, proj_weight, proj_t)

    steps = ((1, 1), (1, 0), (0, 1))

    def gathered(quads):
        return [moved(quad, -x, -y) for quad, (x, y) in zip(quads, steps)] + [quads[3]]

    first, rest = gathered(first), gathered(rest)
    low, high, sums = attend(0, first, features, weights, ())
    low, high, sums = attend(1, rest, features, weights, (low, high, sums))
    paired = (moved(low, 1, 0), high)
    *middle, sums = attend(2, rest, features, weights, (sums,))
    sums, paired = lax.optimization_barrier((sums, paired))
    total, low_y, middle = summed(sums, paired, middle)
    block_out, d_tokens = unpacked(low_y, paired, middle, tokens.shape)
    factor = 1.0 / math.sqrt(tile_x * nx * tile_y * ny * depth)
    dw, dproj, dgain, dbias = grads_of(total, channels, factor)
    return block_out, d_tokens, dw, dproj, dgain[0], dbias[0]


def solution(mesh):
    placed = (P("gx", "gy", None, None), P("gx", "gy", None, None), P(), P(), P(), P())
    return jax.shard_map(
        shards,
        mesh=mesh,
        in_specs=placed,
        out_specs=(P("gx", "gy", None, None), P("gx", "gy", None, None), P(), P(), P(), P()),
        check_vma=False,
    )
```

```python
import functools
import math

import jax
import jax.numpy as jnp
from jax import lax
from jax.experimental import pallas as pl
from jax.experimental.pallas import tpu as pltpu
from jax.sharding import PartitionSpec as P

HEADS = 12
WIN = 8
SHIFT = 4
F32 = jnp.float32
BF16 = jnp.bfloat16
LOG2E = math.log2(math.e)
MASKED = 2.0**100
LANES = 128
VMEM = pl.BlockSpec(memory_space=pltpu.VMEM)

NT = (((1,), (1,)), ((), ()))
TN = (((0,), (0,)), ((), ()))


def dot(a, b):
    return jnp.dot(a, b, preferred_element_type=F32)


def quadrants(block):
    shape = (16, *block.shape[2:])
    return [
        block[x : x + 4, y : y + 4].reshape(shape) for x in (0, 4) for y in (0, 4)
    ]


def piece_of(cells):
    return cells.reshape(LANES, cells.shape[-1]).T.astype(BF16)


def last_piece_of(quad):
    channels = quad.shape[-1]
    pairs = quad.reshape(8, 2, *quad.shape[1:])
    high = jnp.concatenate([pairs[:, 0, 20:24], pairs[:, 1, 20:24]], axis=1)
    low = jnp.concatenate([pairs[:, 0, 0:4], pairs[:, 1, 0:4]], axis=1)
    return piece_of(jnp.concatenate([high.reshape(64, channels), low.reshape(64, channels)], axis=0))


def quadrant_of(first, second, last):
    channels = first.shape[0]
    first = first.astype(F32).T.reshape(16, 8, channels)
    second = second.astype(F32).T.reshape(16, 8, channels)
    last = last.astype(F32).T
    high = last[:64].reshape(8, 8, channels)
    low = last[64:].reshape(8, 8, channels)
    even = jnp.concatenate([low[:, 0:4]], axis=1)
    odd = low[:, 4:8]
    low = jnp.stack([even, odd], axis=1).reshape(16, 4, channels)
    high = jnp.stack([high[:, 0:4], high[:, 4:8]], axis=1).reshape(16, 4, channels)
    whole = jnp.concatenate([low, first, second, high], axis=1)
    return whole.reshape(4, 4, 24, channels).astype(BF16)


def pack_kernel(tokens_ref, cot_ref, *refs):
    first_refs, rest_refs, (buffer, sems) = refs[:4], refs[4:8], refs[8:]
    copies = [
        pltpu.make_async_copy(
            source.at[pl.ds(2 * x, 2)], buffer.at[which, pl.ds(2 * x, 2)], sems.at[which, x]
        )
        for which, source in enumerate((tokens_ref, cot_ref))
        for x in range(4)
    ]
    for copy in copies:
        copy.start()
    for which in range(2):
        for copy in copies[4 * which : 4 * which + 4]:
            copy.wait()
        for i, quad in enumerate(quadrants(buffer[which].astype(F32))):
            first_refs[i][which] = piece_of(quad[:, 4:12])
            rest_refs[i][0, which] = last_piece_of(quad)
            rest_refs[i][1, which] = piece_of(quad[:, 12:20])


def packed(tokens, cotangent):
    channels = tokens.shape[-1]
    S = jax.ShapeDtypeStruct
    outs = pl.pallas_call(
        pack_kernel,
        out_shape=(S((2, channels, LANES), BF16),) * 4 + (S((2, 2, channels, LANES), BF16),) * 4,
        in_specs=[pl.BlockSpec(memory_space=pltpu.HBM)] * 2,
        out_specs=(VMEM,) * 8,
        scratch_shapes=[pltpu.VMEM((2, *tokens.shape), BF16), pltpu.SemaphoreType.DMA((2, 4))],
        compiler_params=pltpu.CompilerParams(vmem_limit_bytes=62 * 2**20),
        name="pack",
    )(tokens, cotangent)
    return outs[:4], outs[4:]


def prepare_kernel(
    gain_ref, bias_ref, wqkv_ref, proj_ref,
    gain_out, bias_out, wqkv_t_out, proj_t_out, kf_out, qf_out,
):
    gain_out[...] = gain_ref[...].T
    bias_out[...] = bias_ref[...].T
    wqkv_t_out[...] = wqkv_ref[...].astype(F32).T.astype(BF16)
    proj_t_out[...] = proj_ref[...].astype(F32).T.astype(BF16)
    edge_x = lax.axis_index("gx") == lax.axis_size("gx") - 1
    edge_y = lax.axis_index("gy") == lax.axis_size("gy") - 1
    shape = kf_out.shape[1:]
    row = lax.broadcasted_iota(jnp.int32, shape, 0)
    lane = lax.broadcasted_iota(jnp.int32, shape, 1)
    for layout, span in enumerate((LANES, LANES // 2)):
        quad = (lane // span) % 4
        far_x = jnp.where(jnp.logical_and(quad // 2 == 0, edge_x), 1.0, 0.0)
        far_y = jnp.where(jnp.logical_and(quad % 2 == 0, edge_y), 1.0, 0.0)
        key = jnp.where(row == 0, far_x, jnp.where(row == 1, 1 - far_x, jnp.where(row == 2, far_y, 1 - far_y)))
        query = jnp.where(row == 0, 1 - far_x, jnp.where(row == 1, far_x, jnp.where(row == 2, 1 - far_y, far_y)))
        kf_out[layout] = jnp.where(row < 4, key, 0.0).astype(BF16)
        qf_out[layout] = jnp.where(row < 4, query * -MASKED, 0.0).astype(BF16)


def prepared(gain, bias, wqkv, proj):
    channels = gain.shape[0]
    cells = 4 * LANES
    S = jax.ShapeDtypeStruct
    return pl.pallas_call(
        prepare_kernel,
        out_shape=(
            S((channels, 1), F32),
            S((channels, 1), F32),
            S((3 * channels, channels), BF16),
            S((channels, channels), BF16),
            S((2, 16, cells), BF16),
            S((2, 16, cells), BF16),
        ),
        in_specs=[VMEM] * 4,
        out_specs=(VMEM,) * 6,
        compiler_params=pltpu.CompilerParams(vmem_limit_bytes=40 * 2**20),
        name="prepare",
    )(gain[None], bias[None], wqkv, proj)


def unpack_kernel(low_y_ref, paired_low, paired_high, middle_low, middle_high, *outs):
    for which, out in enumerate(outs):
        for xh, (paired, middle) in enumerate(
            ((paired_low, middle_low), (paired_high, middle_high))
        ):
            for yh in range(2):
                if yh:
                    first, last = paired[1, 0, which], paired[1, 1, which]
                    second = middle[1, which]
                else:
                    first, last = low_y_ref[2 * xh, which], low_y_ref[2 * xh + 1, which]
                    second = low_y_ref[4 + xh, which]
                quad = quadrant_of(first, second, last)
                out[xh * 4 : xh * 4 + 4, yh * 4 : yh * 4 + 4] = quad


def unpacked(low_y, paired, middle, shape):
    return pl.pallas_call(
        unpack_kernel,
        out_shape=(jax.ShapeDtypeStruct(shape, BF16),) * 2,
        in_specs=[VMEM] * 5,
        out_specs=(VMEM,) * 2,
        compiler_params=pltpu.CompilerParams(vmem_limit_bytes=40 * 2**20),
        name="unpack",
    )(low_y, *paired, *middle)


def attend_kernel(
    turn,
    q00_ref, q01_ref, q10_ref, q11_ref,
    kf_ref, qf_ref, gain_ref, bias_ref, wqkv_t_ref, wqkv_ref, proj_ref, proj_t_ref,
    *refs,
):
    halves = turn == 1
    given = (0, 3, 1)[turn]
    earlier_refs, refs = refs[:given], refs[given:]
    y_refs, grads_ref, scratch = refs[:2], refs[2], refs[3:]
    (qkv_s, gm_s, mix_s, gqkv_s, k_s, q_s, v_s, g_s, e_s, p_s, pb_s, dp_s, ds_s, dst_s, r_s, d_s) = scratch
    quads = (q00_ref, q01_ref, q10_ref, q11_ref)
    if turn:
        quads = [quad.at[turn - 1] for quad in quads]
    channels = q00_ref.shape[-2]
    hd = channels // HEADS
    cells = 4 * LANES
    half = LANES // 2

    def whole(which):
        if halves:
            parts = [q[which].astype(F32) for q in quads]
            return jnp.concatenate(
                [p[:, :half] for p in parts] + [p[:, half:] for p in parts], axis=1
            )
        return jnp.concatenate([q[which].astype(F32) for q in quads], axis=1)

    xf = whole(0)
    gf = whole(1)
    g = gf.astype(BF16)
    mean = jnp.mean(xf, axis=0, keepdims=True)
    centered = xf - mean
    var = jnp.mean(centered * centered, axis=0, keepdims=True)
    inv = lax.rsqrt(var + 1e-5)
    std = centered * inv
    gain = gain_ref[...]
    normed = (std * gain + bias_ref[...]).astype(BF16)
    qkv = dot(wqkv_t_ref[...], normed).astype(BF16)
    qkv_s[...] = qkv
    gm_s[...] = dot(proj_ref[...], g).astype(BF16)

    layout = 1 if halves else 0
    size = cells // 2 if halves else cells
    groups = [slice(start, start + size) for start in range(0, cells, size)]
    chunks = [
        (gi, slice(c, c + LANES), slice(c - group.start, c - group.start + LANES), group)
        for gi, group in enumerate(groups)
        for c in range(group.start, group.stop, LANES)
    ]
    part = cells // 2
    parts = [
        (groups[min(i, len(groups) - 1)], slice(i * part, (i + 1) * part),
         slice(i * part % size, i * part % size + part))
        for i in range(2)
    ]
    scale = hd**-0.5

    def head_rows(base, h):
        if isinstance(h, int):
            return slice(base + h * hd, base + (h + 1) * hd)
        return pl.ds(pl.multiple_of(base + h * hd, hd), hd)

    def q_rows(h):
        return head_rows(0, h)

    def k_rows(h):
        return head_rows(channels, h)

    def v_rows(h):
        return head_rows(2 * channels, h)

    def folded(x):
        return jnp.sum(x.reshape(-1, 8, x.shape[-1]), axis=0)

    def added(total, gi, x):
        total[gi] = x if total[gi] is None else total[gi] + x

    def prepare(h, slot):
        k = qkv_s[k_rows(h)]
        qf = qkv_s[q_rows(h)].astype(F32) * (scale * LOG2E)
        q_hi = qf.astype(BF16)
        q_lo = (qf - q_hi.astype(F32)).astype(BF16)
        k_s[slot] = jnp.concatenate([k, k, kf_ref[layout]], axis=0).T
        q_s[slot] = jnp.concatenate([q_hi, q_lo, qf_ref[layout]], axis=0)
        v_s[slot] = qkv_s[v_rows(h)].T
        g_s[slot] = gm_s[q_rows(h)]

    def exponentials(slot, chunk, total):
        gi, rows, _, cols = chunk
        e = jnp.exp2(dot(k_s[slot, rows], q_s[slot, :, cols]))
        e_s[slot, rows] = e
        added(total, gi, folded(e))

    def attention(slot, chunk, total):
        gi, rows, _, cols = chunk
        p = e_s[slot, rows] * r_s[slot, 0:1, cols]
        p_s[slot, rows] = p
        pb_s[slot, rows] = p.astype(BF16)
        dp = dot(v_s[slot, rows], g_s[slot, :, cols])
        dp_s[slot, rows] = dp
        added(total, gi, folded(p * dp))

    def grad_scores(slot, chunk):
        _, rows, place, cols = chunk
        ds = (p_s[slot, rows] * (dp_s[slot, rows] - d_s[slot, 0:1, cols])).astype(BF16)
        ds_s[slot, rows] = ds
        dst_s[slot, cols, place] = ds.T

    def mixed_part(h, slot, i):
        over, out, place = parts[i]
        mix_s[q_rows(h), out] = dot(qkv_s[v_rows(h), over], pb_s[slot, over, place]).astype(BF16)

    def grad_values_part(h, slot, i):
        over, out, _ = parts[i]
        gv = lax.dot_general(
            gm_s[q_rows(h), over], pb_s[slot, out], NT, preferred_element_type=F32
        )
        gqkv_s[v_rows(h), out] = gv.astype(BF16)

    def grad_queries_part(h, slot, i):
        over, out, place = parts[i]
        gq = dot(qkv_s[k_rows(h), over], ds_s[slot, over, place]) * scale
        gqkv_s[q_rows(h), out] = gq.astype(BF16)

    def grad_keys_part(h, slot, i):
        over, out, place = parts[i]
        gk = dot(qkv_s[q_rows(h), over], dst_s[slot, over, place]) * scale
        gqkv_s[k_rows(h), out] = gk.astype(BF16)

    def kept(ref, slot, total, of):
        for gi, cols in enumerate(groups):
            ref[slot, 0:1, cols] = of(jnp.sum(total[gi], axis=0, keepdims=True))

    def step(i, slot, one=True, two=True, three=True, four=True, ahead=True):
        sums = [None] * len(groups)
        inner = [None] * len(groups)
        for c, chunk in enumerate(chunks):
            if c % 2 == 0 and three:
                mixed_part(i - 2, slot, c // 2)
                grad_values_part(i - 2, slot, c // 2)
            if c % 2 == 1 and four:
                grad_queries_part(i - 3, 1 - slot, c // 2)
                grad_keys_part(i - 3, 1 - slot, c // 2)
            if one:
                exponentials(slot, chunk, sums)
            if two:
                attention(1 - slot, chunk, inner)
            if three:
                grad_scores(slot, chunk)
        if one:
            kept(r_s, slot, sums, lambda total: 1.0 / total)
        if two:
            kept(d_s, 1 - slot, inner, lambda total: total)
        if ahead:
            prepare(i + 1, 1 - slot)

    squares = jnp.square(qkv[: 2 * channels].astype(F32)).reshape(2 * HEADS, hd, cells)
    longest = jnp.max(jnp.sum(squares, axis=1), axis=1, keepdims=True)
    bound = jnp.max(longest[:HEADS] * longest[HEADS:]) * (scale * LOG2E) ** 2
    in_range = bound <= 110.0**2

    @pl.when(in_range)
    def _():
        prepare(0, 0)
        step(0, 0, two=False, three=False, four=False)
        step(1, 1, three=False, four=False)
        step(2, 0, four=False)

        for i in range(3, HEADS - 1):
            step(i, i % 2)
        step(HEADS - 1, 1, ahead=False)
        step(HEADS, 0, one=False, ahead=False)
        step(HEADS + 1, 1, one=False, two=False, ahead=False)
        step(HEADS + 2, 0, one=False, two=False, three=False, ahead=False)

    @pl.when(jnp.logical_not(in_range))
    def _():
        def head(h, carry):
            prepare(h, 0)
            for cols in groups:
                s = dot(k_s[0, cols], q_s[0, :, cols])
                e = jnp.exp2(s - jnp.max(s, axis=0, keepdims=True))
                p = e * (1.0 / jnp.sum(e, axis=0, keepdims=True))
                pb_s[0, cols] = p.astype(BF16)
                dp = dot(v_s[0, cols], g_s[0, :, cols])
                inner = jnp.sum(p * dp, axis=0, keepdims=True)
                ds = (p * (dp - inner)).astype(BF16)
                ds_s[0, cols] = ds
                dst_s[0, cols] = ds.T
            for i in range(2):
                mixed_part(h, 0, i)
                grad_values_part(h, 0, i)
                grad_queries_part(h, 0, i)
                grad_keys_part(h, 0, i)
            return carry

        lax.fori_loop(0, HEADS, head, 0)

    mixed = mix_s[...]
    block_out = xf + dot(proj_t_ref[...], mixed)
    gqkv = gqkv_s[...]
    gn = dot(wqkv_ref[...], gqkv)
    scaled = gn * gain
    gx = inv * (
        scaled
        - jnp.mean(scaled, axis=0, keepdims=True)
        - std * jnp.mean(scaled * std, axis=0, keepdims=True)
    )
    d_tokens = gf + gx
    for which, y in enumerate((block_out, d_tokens)):
        for i in range(4):
            ref, yh = y_refs[i // 2], i % 2
            if halves:
                lo = y[:, i * half : (i + 1) * half]
                hi = y[:, cells // 2 + i * half : cells // 2 + (i + 1) * half]
                part = jnp.concatenate([lo, hi], axis=1)
                ref[yh, 0, which] = earlier_refs[i // 2][yh, which]
                ref[yh, 1, which] = part.astype(BF16)
            else:
                ref[yh, which] = y[:, i * LANES : (i + 1) * LANES].astype(BF16)

    dw = lax.dot_general(normed, gqkv, NT, preferred_element_type=F32)
    dproj = lax.dot_general(mixed, g, NT, preferred_element_type=F32)
    dgain = jnp.sum(gn * std, axis=1, keepdims=True)
    dbias = jnp.sum(gn, axis=1, keepdims=True)
    joined = jnp.concatenate([dw, dproj], axis=1)
    blocks = [joined[:, i * LANES : (i + 1) * LANES] for i in range(joined.shape[1] // LANES)]
    lane = lax.broadcasted_iota(jnp.int32, (channels, LANES), 1)
    tail = jnp.where(lane == 0, dgain, jnp.where(lane == 1, dbias, 0.0)).T[:8]
    used = len(blocks) * channels
    grads = jnp.concatenate(blocks, axis=0)
    pad = jnp.zeros((8, 2 * LANES - channels), F32)
    extra = jnp.concatenate(
        [tail[:, :LANES], jnp.concatenate([tail[:, LANES:], pad], axis=1)], axis=0
    )
    if turn:
        grads = grads + earlier_refs[-1][:used]
        extra = extra + earlier_refs[-1][used : used + 16]
    grads_ref[:used] = grads.astype(grads_ref.dtype)
    grads_ref[used : used + 16] = extra.astype(grads_ref.dtype)
    grads_ref[used + 16 :] = jnp.zeros(
        (grads_ref.shape[0] - used - 16, LANES), grads_ref.dtype
    )


GRAD_ROWS = 1280


def attend(turn, quads, features, weights, earlier):
    channels = quads[0].shape[-2]
    cells = 4 * LANES
    width = cells // 2 if turn == 1 else cells
    S = jax.ShapeDtypeStruct
    piece = (2, channels, LANES)
    return pl.pallas_call(
        functools.partial(attend_kernel, turn),
        out_shape=(S((2, 2, *piece) if turn == 1 else (2, *piece), BF16),) * 2
        + (S((GRAD_ROWS, LANES), BF16 if turn == 2 else F32),),
        in_specs=[VMEM] * (12 + len(earlier)),
        out_specs=(VMEM,) * 3,
        scratch_shapes=[
            pltpu.VMEM((3 * channels, cells), BF16),
            pltpu.VMEM((channels, cells), BF16),
            pltpu.VMEM((channels, cells), BF16),
            pltpu.VMEM((3 * channels, cells), BF16),
            pltpu.VMEM((2, cells, 48), BF16),
            pltpu.VMEM((2, 48, cells), BF16),
            pltpu.VMEM((2, cells, 16), BF16),
            pltpu.VMEM((2, 16, cells), BF16),
            pltpu.VMEM((2, cells, width), F32),
            pltpu.VMEM((2, cells, width), F32),
            pltpu.VMEM((2, cells, width), BF16),
            pltpu.VMEM((2, cells, width), F32),
            pltpu.VMEM((2, cells, width), BF16),
            pltpu.VMEM((2, cells, width), BF16),
            pltpu.VMEM((2, 8, cells), F32),
            pltpu.VMEM((2, 8, cells), F32),
        ],
        compiler_params=pltpu.CompilerParams(vmem_limit_bytes=40 * 2**20),
        cost_estimate=pl.CostEstimate(
            flops=12 * 12 * 512 * 512 * 256, bytes_accessed=4 * 2**20, transcendentals=12 * 512 * 512
        ),
        name="attend",
    )(*quads, *features, *weights, *earlier)


def moved(block, step_x, step_y):
    nx, ny = lax.axis_size("gx"), lax.axis_size("gy")
    route = []
    for i in range(nx):
        for j in range(ny):
            to = ((i + step_x) % nx) * ny + (j + step_y) % ny
            route.append((i * ny + j, to))
    return lax.ppermute(block, ("gx", "gy"), route)


def summed(rows, paired, middle):
    nx, ny = lax.axis_size("gx"), lax.axis_size("gy")
    near = 2 * ny
    planes = [[near * i + j for j in range(near)] for i in range(nx // 2)]
    across = [list(ids) for ids in zip(*planes)]

    def exchanged(pieces, groups):
        return lax.all_to_all(pieces, ("gx", "gy"), 0, 0, axis_index_groups=groups)

    def copies(piece, count):
        return jnp.broadcast_to(piece[None], (count, *piece.shape))

    got = exchanged(rows.reshape(near, -1, LANES), planes)
    middle = (moved(middle[0], 1, 0), middle[1])
    got, middle = lax.optimization_barrier((got, middle))
    mine = jnp.sum(got.astype(F32), axis=0).astype(BF16)
    got = exchanged(copies(mine, nx // 2), across)
    low_y = moved(jnp.concatenate([paired[0][0], paired[1][0], middle[0][:1], middle[1][:1]]), 0, 1)
    got, low_y = lax.optimization_barrier((got, low_y))
    total = jnp.sum(got.astype(F32), axis=0).astype(BF16)
    return exchanged(copies(total, near), planes).reshape(rows.shape), low_y, middle


def grads_kernel(factor, rows_ref, dw_ref, dproj_ref, gain_ref, bias_ref):
    channels = dw_ref.shape[0]
    blocks = 4 * channels // LANES
    joined = jnp.concatenate(
        [rows_ref[i * channels : (i + 1) * channels].astype(F32) for i in range(blocks)], axis=1
    ) * factor
    dw_ref[...] = joined[:, : 3 * channels]
    dproj_ref[...] = joined[:, 3 * channels :]
    used = blocks * channels
    tail = rows_ref[used : used + 16].astype(F32) * factor
    tail = jnp.concatenate([tail[:8], tail[8:]], axis=1)[:, :channels]
    gain_ref[...] = tail[0:1]
    bias_ref[...] = tail[1:2]


def grads_of(rows, channels, factor):
    S = jax.ShapeDtypeStruct
    return pl.pallas_call(
        functools.partial(grads_kernel, factor),
        out_shape=(
            S((channels, 3 * channels), F32),
            S((channels, channels), F32),
            S((1, channels), F32),
            S((1, channels), F32),
        ),
        in_specs=[VMEM],
        out_specs=(VMEM,) * 4,
        name="unpack_grads",
    )(rows)


def shards(tokens, cotangent, ln_gain, ln_bias, qkv_weight, proj_weight):
    tile_x, tile_y, depth, channels = tokens.shape
    nx, ny = lax.axis_size("gx"), lax.axis_size("gy")
    first, rest = packed(tokens, cotangent)
    first, proj_weight = lax.optimization_barrier((first, proj_weight))
    gain, bias, wqkv_t, proj_t, *features = prepared(ln_gain, ln_bias, qkv_weight, proj_weight)
    weights = (gain, bias, wqkv_t, qkv_weight, proj_weight, proj_t)

    steps = ((1, 1), (1, 0), (0, 1))

    def gathered(quads):
        return [moved(quad, -x, -y) for quad, (x, y) in zip(quads, steps)] + [quads[3]]

    first, rest = gathered(first), gathered(rest)
    low, high, sums = attend(0, first, features, weights, ())
    low, high, sums = attend(1, rest, features, weights, (low, high, sums))
    paired = (moved(low, 1, 0), high)
    *middle, sums = attend(2, rest, features, weights, (sums,))
    sums, paired = lax.optimization_barrier((sums, paired))
    total, low_y, middle = summed(sums, paired, middle)
    block_out, d_tokens = unpacked(low_y, paired, middle, tokens.shape)
    factor = 1.0 / math.sqrt(tile_x * nx * tile_y * ny * depth)
    dw, dproj, dgain, dbias = grads_of(total, channels, factor)
    return block_out, d_tokens, dw, dproj, dgain[0], dbias[0]


def solution(mesh):
    placed = (P("gx", "gy", None, None), P("gx", "gy", None, None), P(), P(), P(), P())
    return jax.shard_map(
        shards,
        mesh=mesh,
        in_specs=placed,
        out_specs=(P("gx", "gy", None, None), P("gx", "gy", None, None), P(), P(), P(), P()),
        check_vma=False,
    )
```

```python
import functools
import math

import jax
import jax.numpy as jnp
from jax import lax
from jax.experimental import pallas as pl
from jax.experimental.pallas import tpu as pltpu
from jax.sharding import PartitionSpec as P

HEADS = 12
WIN = 8
SHIFT = 4
F32 = jnp.float32
BF16 = jnp.bfloat16
LOG2E = math.log2(math.e)
MASKED = 2.0**100
LANES = 128
VMEM = pl.BlockSpec(memory_space=pltpu.VMEM)

NT = (((1,), (1,)), ((), ()))
TN = (((0,), (0,)), ((), ()))


def dot(a, b):
    return jnp.dot(a, b, preferred_element_type=F32)


def quadrants(block):
    shape = (16, *block.shape[2:])
    return [
        block[x : x + 4, y : y + 4].reshape(shape) for x in (0, 4) for y in (0, 4)
    ]


def piece_of(cells):
    return cells.reshape(LANES, cells.shape[-1]).T.astype(BF16)


def last_piece_of(quad):
    channels = quad.shape[-1]
    pairs = quad.reshape(8, 2, *quad.shape[1:])
    high = jnp.concatenate([pairs[:, 0, 20:24], pairs[:, 1, 20:24]], axis=1)
    low = jnp.concatenate([pairs[:, 0, 0:4], pairs[:, 1, 0:4]], axis=1)
    return piece_of(jnp.concatenate([high.reshape(64, channels), low.reshape(64, channels)], axis=0))


def quadrant_of(first, second, last):
    channels = first.shape[0]
    first = first.astype(F32).T.reshape(16, 8, channels)
    second = second.astype(F32).T.reshape(16, 8, channels)
    last = last.astype(F32).T
    high = last[:64].reshape(8, 8, channels)
    low = last[64:].reshape(8, 8, channels)
    even = jnp.concatenate([low[:, 0:4]], axis=1)
    odd = low[:, 4:8]
    low = jnp.stack([even, odd], axis=1).reshape(16, 4, channels)
    high = jnp.stack([high[:, 0:4], high[:, 4:8]], axis=1).reshape(16, 4, channels)
    whole = jnp.concatenate([low, first, second, high], axis=1)
    return whole.reshape(4, 4, 24, channels).astype(BF16)


def read_block(sources, buffer, sems, depth):
    copies = [
        pltpu.make_async_copy(
            source.at[pl.ds(2 * x, 2), :, pl.ds(0, depth)],
            buffer.at[which, pl.ds(2 * x, 2)],
            sems.at[which, x],
        )
        for which, source in enumerate(sources)
        for x in range(4)
    ]
    for copy in copies:
        copy.start()
    return copies


def pack_first_kernel(tokens_ref, cot_ref, *refs):
    outs, (buffer, sems) = refs[:4], refs[4:]
    copies = read_block((tokens_ref, cot_ref), buffer, sems, buffer.shape[3])
    for which in range(2):
        for copy in copies[4 * which : 4 * which + 4]:
            copy.wait()
        for i, quad in enumerate(quadrants(buffer[which].astype(F32))):
            outs[i][which] = piece_of(quad[:, 4:12])


def pack_rest_kernel(tokens_ref, cot_ref, *refs):
    outs, (buffer, sems) = refs[:4], refs[4:]
    copies = read_block((tokens_ref, cot_ref), buffer, sems, buffer.shape[3])
    for which in range(2):
        for copy in copies[4 * which : 4 * which + 4]:
            copy.wait()
        for i, quad in enumerate(quadrants(buffer[which].astype(F32))):
            outs[i][0, which] = last_piece_of(quad)
            outs[i][1, which] = piece_of(quad[:, 12:20])


def packed(tokens, cotangent, first):
    tile_x, tile_y, depth, channels = tokens.shape
    piece = (2, channels, LANES)
    shape = piece if first else (2, *piece)
    held = 2 * WIN if first else depth
    return pl.pallas_call(
        pack_first_kernel if first else pack_rest_kernel,
        out_shape=(jax.ShapeDtypeStruct(shape, BF16),) * 4,
        in_specs=[pl.BlockSpec(memory_space=pltpu.HBM)] * 2,
        out_specs=(VMEM,) * 4,
        scratch_shapes=[
            pltpu.VMEM((2, tile_x, tile_y, held, channels), BF16),
            pltpu.SemaphoreType.DMA((2, 4)),
        ],
        compiler_params=pltpu.CompilerParams(vmem_limit_bytes=62 * 2**20),
        name="pack_first" if first else "pack_rest",
    )(tokens, cotangent)


def prepare_kernel(
    gain_ref, bias_ref, wqkv_ref, proj_ref,
    gain_out, bias_out, wqkv_t_out, proj_t_out, kf_out, qf_out,
):
    gain_out[...] = gain_ref[...].T
    bias_out[...] = bias_ref[...].T
    wqkv_t_out[...] = wqkv_ref[...].astype(F32).T.astype(BF16)
    proj_t_out[...] = proj_ref[...].astype(F32).T.astype(BF16)
    edge_x = lax.axis_index("gx") == lax.axis_size("gx") - 1
    edge_y = lax.axis_index("gy") == lax.axis_size("gy") - 1
    shape = kf_out.shape[1:]
    row = lax.broadcasted_iota(jnp.int32, shape, 0)
    lane = lax.broadcasted_iota(jnp.int32, shape, 1)
    for layout, span in enumerate((LANES, LANES // 2)):
        quad = (lane // span) % 4
        far_x = jnp.where(jnp.logical_and(quad // 2 == 0, edge_x), 1.0, 0.0)
        far_y = jnp.where(jnp.logical_and(quad % 2 == 0, edge_y), 1.0, 0.0)
        key = jnp.where(row == 0, far_x, jnp.where(row == 1, 1 - far_x, jnp.where(row == 2, far_y, 1 - far_y)))
        query = jnp.where(row == 0, 1 - far_x, jnp.where(row == 1, far_x, jnp.where(row == 2, 1 - far_y, far_y)))
        kf_out[layout] = jnp.where(row < 4, key, 0.0).astype(BF16)
        qf_out[layout] = jnp.where(row < 4, query * -MASKED, 0.0).astype(BF16)


def prepared(gain, bias, wqkv, proj):
    channels = gain.shape[0]
    cells = 4 * LANES
    S = jax.ShapeDtypeStruct
    return pl.pallas_call(
        prepare_kernel,
        out_shape=(
            S((channels, 1), F32),
            S((channels, 1), F32),
            S((3 * channels, channels), BF16),
            S((channels, channels), BF16),
            S((2, 16, cells), BF16),
            S((2, 16, cells), BF16),
        ),
        in_specs=[VMEM] * 4,
        out_specs=(VMEM,) * 6,
        compiler_params=pltpu.CompilerParams(vmem_limit_bytes=40 * 2**20),
        name="prepare",
    )(gain[None], bias[None], wqkv, proj)


def unpack_kernel(low_y_ref, paired_low, paired_high, middle_low, middle_high, *outs):
    for which, out in enumerate(outs):
        for xh, (paired, middle) in enumerate(
            ((paired_low, middle_low), (paired_high, middle_high))
        ):
            for yh in range(2):
                if yh:
                    first, last = paired[1, 0, which], paired[1, 1, which]
                    second = middle[1, which]
                else:
                    first, last = low_y_ref[2 * xh, which], low_y_ref[2 * xh + 1, which]
                    second = low_y_ref[4 + xh, which]
                quad = quadrant_of(first, second, last)
                out[xh * 4 : xh * 4 + 4, yh * 4 : yh * 4 + 4] = quad


def unpacked(low_y, paired, middle, shape):
    return pl.pallas_call(
        unpack_kernel,
        out_shape=(jax.ShapeDtypeStruct(shape, BF16),) * 2,
        in_specs=[VMEM] * 5,
        out_specs=(VMEM,) * 2,
        compiler_params=pltpu.CompilerParams(vmem_limit_bytes=40 * 2**20),
        name="unpack",
    )(low_y, *paired, *middle)


def attend_kernel(
    turn,
    q00_ref, q01_ref, q10_ref, q11_ref,
    kf_ref, qf_ref, gain_ref, bias_ref, wqkv_t_ref, wqkv_ref, proj_ref, proj_t_ref,
    *refs,
):
    halves = turn == 1
    given = (0, 3, 1)[turn]
    earlier_refs, refs = refs[:given], refs[given:]
    y_refs, grads_ref, scratch = refs[:2], refs[2], refs[3:]
    (qkv_s, gm_s, mix_s, gqkv_s, k_s, q_s, v_s, g_s, e_s, p_s, pb_s, dp_s, ds_s, dst_s, r_s, d_s) = scratch
    quads = (q00_ref, q01_ref, q10_ref, q11_ref)
    if turn:
        quads = [quad.at[turn - 1] for quad in quads]
    channels = q00_ref.shape[-2]
    hd = channels // HEADS
    cells = 4 * LANES
    half = LANES // 2

    def whole(which):
        if halves:
            parts = [q[which].astype(F32) for q in quads]
            return jnp.concatenate(
                [p[:, :half] for p in parts] + [p[:, half:] for p in parts], axis=1
            )
        return jnp.concatenate([q[which].astype(F32) for q in quads], axis=1)

    xf = whole(0)
    gf = whole(1)
    g = gf.astype(BF16)
    mean = jnp.mean(xf, axis=0, keepdims=True)
    centered = xf - mean
    var = jnp.mean(centered * centered, axis=0, keepdims=True)
    inv = lax.rsqrt(var + 1e-5)
    std = centered * inv
    gain = gain_ref[...]
    normed = (std * gain + bias_ref[...]).astype(BF16)
    qkv = dot(wqkv_t_ref[...], normed).astype(BF16)
    qkv_s[...] = qkv
    gm_s[...] = dot(proj_ref[...], g).astype(BF16)

    layout = 1 if halves else 0
    size = cells // 2 if halves else cells
    groups = [slice(start, start + size) for start in range(0, cells, size)]
    chunks = [
        (gi, slice(c, c + LANES), slice(c - group.start, c - group.start + LANES), group)
        for gi, group in enumerate(groups)
        for c in range(group.start, group.stop, LANES)
    ]
    part = cells // 2
    parts = [
        (groups[min(i, len(groups) - 1)], slice(i * part, (i + 1) * part),
         slice(i * part % size, i * part % size + part))
        for i in range(2)
    ]
    scale = hd**-0.5

    def head_rows(base, h):
        if isinstance(h, int):
            return slice(base + h * hd, base + (h + 1) * hd)
        return pl.ds(pl.multiple_of(base + h * hd, hd), hd)

    def q_rows(h):
        return head_rows(0, h)

    def k_rows(h):
        return head_rows(channels, h)

    def v_rows(h):
        return head_rows(2 * channels, h)

    def folded(x):
        return jnp.sum(x.reshape(-1, 8, x.shape[-1]), axis=0)

    def added(total, gi, x):
        total[gi] = x if total[gi] is None else total[gi] + x

    def prepare(h, slot):
        k = qkv_s[k_rows(h)]
        qf = qkv_s[q_rows(h)].astype(F32) * (scale * LOG2E)
        q_hi = qf.astype(BF16)
        q_lo = (qf - q_hi.astype(F32)).astype(BF16)
        k_s[slot] = jnp.concatenate([k, k, kf_ref[layout]], axis=0).T
        q_s[slot] = jnp.concatenate([q_hi, q_lo, qf_ref[layout]], axis=0)
        v_s[slot] = qkv_s[v_rows(h)].T
        g_s[slot] = gm_s[q_rows(h)]

    def exponentials(slot, chunk, total):
        gi, rows, _, cols = chunk
        e = jnp.exp2(dot(k_s[slot, rows], q_s[slot, :, cols]))
        e_s[slot, rows] = e
        added(total, gi, folded(e))

    def attention(slot, chunk, total):
        gi, rows, _, cols = chunk
        p = e_s[slot, rows] * r_s[slot, 0:1, cols]
        p_s[slot, rows] = p
        pb_s[slot, rows] = p.astype(BF16)
        dp = dot(v_s[slot, rows], g_s[slot, :, cols])
        dp_s[slot, rows] = dp
        added(total, gi, folded(p * dp))

    def grad_scores(slot, chunk):
        _, rows, place, cols = chunk
        ds = (p_s[slot, rows] * (dp_s[slot, rows] - d_s[slot, 0:1, cols])).astype(BF16)
        ds_s[slot, rows] = ds
        dst_s[slot, cols, place] = ds.T

    def mixed_part(h, slot, i):
        over, out, place = parts[i]
        mix_s[q_rows(h), out] = dot(qkv_s[v_rows(h), over], pb_s[slot, over, place]).astype(BF16)

    def grad_values_part(h, slot, i):
        over, out, _ = parts[i]
        gv = lax.dot_general(
            gm_s[q_rows(h), over], pb_s[slot, out], NT, preferred_element_type=F32
        )
        gqkv_s[v_rows(h), out] = gv.astype(BF16)

    def grad_queries_part(h, slot, i):
        over, out, place = parts[i]
        gq = dot(qkv_s[k_rows(h), over], ds_s[slot, over, place]) * scale
        gqkv_s[q_rows(h), out] = gq.astype(BF16)

    def grad_keys_part(h, slot, i):
        over, out, place = parts[i]
        gk = dot(qkv_s[q_rows(h), over], dst_s[slot, over, place]) * scale
        gqkv_s[k_rows(h), out] = gk.astype(BF16)

    def kept(ref, slot, total, of):
        for gi, cols in enumerate(groups):
            ref[slot, 0:1, cols] = of(jnp.sum(total[gi], axis=0, keepdims=True))

    def step(i, slot, one=True, two=True, three=True, four=True, ahead=True):
        sums = [None] * len(groups)
        inner = [None] * len(groups)
        for c, chunk in enumerate(chunks):
            if c % 2 == 0 and three:
                mixed_part(i - 2, slot, c // 2)
                grad_values_part(i - 2, slot, c // 2)
            if c % 2 == 1 and four:
                grad_queries_part(i - 3, 1 - slot, c // 2)
                grad_keys_part(i - 3, 1 - slot, c // 2)
            if one:
                exponentials(slot, chunk, sums)
            if two:
                attention(1 - slot, chunk, inner)
            if three:
                grad_scores(slot, chunk)
        if one:
            kept(r_s, slot, sums, lambda total: 1.0 / total)
        if two:
            kept(d_s, 1 - slot, inner, lambda total: total)
        if ahead:
            prepare(i + 1, 1 - slot)

    squares = jnp.square(qkv[: 2 * channels].astype(F32)).reshape(2 * HEADS, hd, cells)
    longest = jnp.max(jnp.sum(squares, axis=1), axis=1, keepdims=True)
    bound = jnp.max(longest[:HEADS] * longest[HEADS:]) * (scale * LOG2E) ** 2
    in_range = bound <= 110.0**2

    @pl.when(in_range)
    def _():
        prepare(0, 0)
        step(0, 0, two=False, three=False, four=False)
        step(1, 1, three=False, four=False)
        step(2, 0, four=False)

        for i in range(3, HEADS - 1):
            step(i, i % 2)
        step(HEADS - 1, 1, ahead=False)
        step(HEADS, 0, one=False, ahead=False)
        step(HEADS + 1, 1, one=False, two=False, ahead=False)
        step(HEADS + 2, 0, one=False, two=False, three=False, ahead=False)

    @pl.when(jnp.logical_not(in_range))
    def _():
        def head(h, carry):
            prepare(h, 0)
            for cols in groups:
                s = dot(k_s[0, cols], q_s[0, :, cols])
                e = jnp.exp2(s - jnp.max(s, axis=0, keepdims=True))
                p = e * (1.0 / jnp.sum(e, axis=0, keepdims=True))
                pb_s[0, cols] = p.astype(BF16)
                dp = dot(v_s[0, cols], g_s[0, :, cols])
                inner = jnp.sum(p * dp, axis=0, keepdims=True)
                ds = (p * (dp - inner)).astype(BF16)
                ds_s[0, cols] = ds
                dst_s[0, cols] = ds.T
            for i in range(2):
                mixed_part(h, 0, i)
                grad_values_part(h, 0, i)
                grad_queries_part(h, 0, i)
                grad_keys_part(h, 0, i)
            return carry

        lax.fori_loop(0, HEADS, head, 0)

    mixed = mix_s[...]
    block_out = xf + dot(proj_t_ref[...], mixed)
    gqkv = gqkv_s[...]
    gn = dot(wqkv_ref[...], gqkv)
    scaled = gn * gain
    gx = inv * (
        scaled
        - jnp.mean(scaled, axis=0, keepdims=True)
        - std * jnp.mean(scaled * std, axis=0, keepdims=True)
    )
    d_tokens = gf + gx
    for which, y in enumerate((block_out, d_tokens)):
        for i in range(4):
            ref, yh = y_refs[i // 2], i % 2
            if halves:
                lo = y[:, i * half : (i + 1) * half]
                hi = y[:, cells // 2 + i * half : cells // 2 + (i + 1) * half]
                part = jnp.concatenate([lo, hi], axis=1)
                ref[yh, 0, which] = earlier_refs[i // 2][yh, which]
                ref[yh, 1, which] = part.astype(BF16)
            else:
                ref[yh, which] = y[:, i * LANES : (i + 1) * LANES].astype(BF16)

    dw = lax.dot_general(normed, gqkv, NT, preferred_element_type=F32)
    dproj = lax.dot_general(mixed, g, NT, preferred_element_type=F32)
    dgain = jnp.sum(gn * std, axis=1, keepdims=True)
    dbias = jnp.sum(gn, axis=1, keepdims=True)
    joined = jnp.concatenate([dw, dproj], axis=1)
    blocks = [joined[:, i * LANES : (i + 1) * LANES] for i in range(joined.shape[1] // LANES)]
    lane = lax.broadcasted_iota(jnp.int32, (channels, LANES), 1)
    tail = jnp.where(lane == 0, dgain, jnp.where(lane == 1, dbias, 0.0)).T[:8]
    used = len(blocks) * channels
    grads = jnp.concatenate(blocks, axis=0)
    pad = jnp.zeros((8, 2 * LANES - channels), F32)
    extra = jnp.concatenate(
        [tail[:, :LANES], jnp.concatenate([tail[:, LANES:], pad], axis=1)], axis=0
    )
    if turn:
        grads = grads + earlier_refs[-1][:used]
        extra = extra + earlier_refs[-1][used : used + 16]
    grads_ref[:used] = grads.astype(grads_ref.dtype)
    grads_ref[used : used + 16] = extra.astype(grads_ref.dtype)
    grads_ref[used + 16 :] = jnp.zeros(
        (grads_ref.shape[0] - used - 16, LANES), grads_ref.dtype
    )


GRAD_ROWS = 1280


def attend(turn, quads, features, weights, earlier):
    channels = quads[0].shape[-2]
    cells = 4 * LANES
    width = cells // 2 if turn == 1 else cells
    S = jax.ShapeDtypeStruct
    piece = (2, channels, LANES)
    return pl.pallas_call(
        functools.partial(attend_kernel, turn),
        out_shape=(S((2, 2, *piece) if turn == 1 else (2, *piece), BF16),) * 2
        + (S((GRAD_ROWS, LANES), BF16 if turn == 2 else F32),),
        in_specs=[VMEM] * (12 + len(earlier)),
        out_specs=(VMEM,) * 3,
        scratch_shapes=[
            pltpu.VMEM((3 * channels, cells), BF16),
            pltpu.VMEM((channels, cells), BF16),
            pltpu.VMEM((channels, cells), BF16),
            pltpu.VMEM((3 * channels, cells), BF16),
            pltpu.VMEM((2, cells, 48), BF16),
            pltpu.VMEM((2, 48, cells), BF16),
            pltpu.VMEM((2, cells, 16), BF16),
            pltpu.VMEM((2, 16, cells), BF16),
            pltpu.VMEM((2, cells, width), F32),
            pltpu.VMEM((2, cells, width), F32),
            pltpu.VMEM((2, cells, width), BF16),
            pltpu.VMEM((2, cells, width), F32),
            pltpu.VMEM((2, cells, width), BF16),
            pltpu.VMEM((2, cells, width), BF16),
            pltpu.VMEM((2, 8, cells), F32),
            pltpu.VMEM((2, 8, cells), F32),
        ],
        compiler_params=pltpu.CompilerParams(vmem_limit_bytes=40 * 2**20),
        cost_estimate=pl.CostEstimate(
            flops=12 * 12 * 512 * 512 * 256, bytes_accessed=4 * 2**20, transcendentals=12 * 512 * 512
        ),
        name="attend",
    )(*quads, *features, *weights, *earlier)


def moved(block, step_x, step_y):
    nx, ny = lax.axis_size("gx"), lax.axis_size("gy")
    route = []
    for i in range(nx):
        for j in range(ny):
            to = ((i + step_x) % nx) * ny + (j + step_y) % ny
            route.append((i * ny + j, to))
    return lax.ppermute(block, ("gx", "gy"), route)


def summed(rows, paired, middle):
    nx, ny = lax.axis_size("gx"), lax.axis_size("gy")
    near = 2 * ny
    planes = [[near * i + j for j in range(near)] for i in range(nx // 2)]
    across = [list(ids) for ids in zip(*planes)]

    def exchanged(pieces, groups):
        return lax.all_to_all(pieces, ("gx", "gy"), 0, 0, axis_index_groups=groups)

    def copies(piece, count):
        return jnp.broadcast_to(piece[None], (count, *piece.shape))

    got = exchanged(rows.reshape(near, -1, LANES), planes)
    middle = (moved(middle[0], 1, 0), middle[1])
    got, middle = lax.optimization_barrier((got, middle))
    mine = jnp.sum(got.astype(F32), axis=0).astype(BF16)
    got = exchanged(copies(mine, nx // 2), across)
    low_y = moved(jnp.concatenate([paired[0][0], paired[1][0], middle[0][:1], middle[1][:1]]), 0, 1)
    got, low_y = lax.optimization_barrier((got, low_y))
    total = jnp.sum(got.astype(F32), axis=0).astype(BF16)
    return exchanged(copies(total, near), planes).reshape(rows.shape), low_y, middle


def grads_kernel(factor, rows_ref, dw_ref, dproj_ref, gain_ref, bias_ref):
    channels = dw_ref.shape[0]
    blocks = 4 * channels // LANES
    joined = jnp.concatenate(
        [rows_ref[i * channels : (i + 1) * channels].astype(F32) for i in range(blocks)], axis=1
    ) * factor
    dw_ref[...] = joined[:, : 3 * channels]
    dproj_ref[...] = joined[:, 3 * channels :]
    used = blocks * channels
    tail = rows_ref[used : used + 16].astype(F32) * factor
    tail = jnp.concatenate([tail[:8], tail[8:]], axis=1)[:, :channels]
    gain_ref[...] = tail[0:1]
    bias_ref[...] = tail[1:2]


def grads_of(rows, channels, factor):
    S = jax.ShapeDtypeStruct
    return pl.pallas_call(
        functools.partial(grads_kernel, factor),
        out_shape=(
            S((channels, 3 * channels), F32),
            S((channels, channels), F32),
            S((1, channels), F32),
            S((1, channels), F32),
        ),
        in_specs=[VMEM],
        out_specs=(VMEM,) * 4,
        name="unpack_grads",
    )(rows)


def shards(tokens, cotangent, ln_gain, ln_bias, qkv_weight, proj_weight):
    tile_x, tile_y, depth, channels = tokens.shape
    nx, ny = lax.axis_size("gx"), lax.axis_size("gy")
    first = packed(tokens, cotangent, True)
    first, tokens, cotangent, proj_weight = lax.optimization_barrier(
        (first, tokens, cotangent, proj_weight)
    )
    rest = packed(tokens, cotangent, False)
    gain, bias, wqkv_t, proj_t, *features = prepared(ln_gain, ln_bias, qkv_weight, proj_weight)
    weights = (gain, bias, wqkv_t, qkv_weight, proj_weight, proj_t)

    steps = ((1, 1), (1, 0), (0, 1))

    def gathered(quads):
        return [moved(quad, -x, -y) for quad, (x, y) in zip(quads, steps)] + [quads[3]]

    first, rest = gathered(first), gathered(rest)
    low, high, sums = attend(0, first, features, weights, ())
    low, high, sums = attend(1, rest, features, weights, (low, high, sums))
    paired = (moved(low, 1, 0), high)
    *middle, sums = attend(2, rest, features, weights, (sums,))
    sums, paired = lax.optimization_barrier((sums, paired))
    total, low_y, middle = summed(sums, paired, middle)
    block_out, d_tokens = unpacked(low_y, paired, middle, tokens.shape)
    factor = 1.0 / math.sqrt(tile_x * nx * tile_y * ny * depth)
    dw, dproj, dgain, dbias = grads_of(total, channels, factor)
    return block_out, d_tokens, dw, dproj, dgain[0], dbias[0]


def solution(mesh):
    placed = (P("gx", "gy", None, None), P("gx", "gy", None, None), P(), P(), P(), P())
    return jax.shard_map(
        shards,
        mesh=mesh,
        in_specs=placed,
        out_specs=(P("gx", "gy", None, None), P("gx", "gy", None, None), P(), P(), P(), P()),
        check_vma=False,
    )
```

```python
import functools
import math

import jax
import jax.numpy as jnp
from jax import lax
from jax.experimental import pallas as pl
from jax.experimental.pallas import tpu as pltpu
from jax.sharding import PartitionSpec as P

HEADS = 12
WIN = 8
SHIFT = 4
F32 = jnp.float32
BF16 = jnp.bfloat16
LOG2E = math.log2(math.e)
MASKED = 2.0**100
LANES = 128
VMEM = pl.BlockSpec(memory_space=pltpu.VMEM)

NT = (((1,), (1,)), ((), ()))
TN = (((0,), (0,)), ((), ()))


def dot(a, b):
    return jnp.dot(a, b, preferred_element_type=F32)


def quadrants(block):
    shape = (16, *block.shape[2:])
    return [
        block[x : x + 4, y : y + 4].reshape(shape) for x in (0, 4) for y in (0, 4)
    ]


def piece_of(cells):
    return cells.reshape(LANES, cells.shape[-1]).T.astype(BF16)


def last_piece_of(quad):
    channels = quad.shape[-1]
    pairs = quad.reshape(8, 2, *quad.shape[1:])
    high = jnp.concatenate([pairs[:, 0, 20:24], pairs[:, 1, 20:24]], axis=1)
    low = jnp.concatenate([pairs[:, 0, 0:4], pairs[:, 1, 0:4]], axis=1)
    return piece_of(jnp.concatenate([high.reshape(64, channels), low.reshape(64, channels)], axis=0))


def quadrant_of(first, second, last):
    channels = first.shape[0]
    first = first.astype(F32).T.reshape(16, 8, channels)
    second = second.astype(F32).T.reshape(16, 8, channels)
    last = last.astype(F32).T
    high = last[:64].reshape(8, 8, channels)
    low = last[64:].reshape(8, 8, channels)
    even = jnp.concatenate([low[:, 0:4]], axis=1)
    odd = low[:, 4:8]
    low = jnp.stack([even, odd], axis=1).reshape(16, 4, channels)
    high = jnp.stack([high[:, 0:4], high[:, 4:8]], axis=1).reshape(16, 4, channels)
    whole = jnp.concatenate([low, first, second, high], axis=1)
    return whole.reshape(4, 4, 24, channels).astype(BF16)


def pack_kernel(tokens_ref, cot_ref, *refs):
    first_refs, rest_refs, (buffer, sems) = refs[:4], refs[4:8], refs[8:]
    copies = [
        pltpu.make_async_copy(
            source.at[pl.ds(2 * x, 2)], buffer.at[which, pl.ds(2 * x, 2)], sems.at[which, x]
        )
        for which, source in enumerate((tokens_ref, cot_ref))
        for x in range(4)
    ]
    for copy in copies:
        copy.start()
    for which in range(2):
        for copy in copies[4 * which : 4 * which + 4]:
            copy.wait()
        for i, quad in enumerate(quadrants(buffer[which].astype(F32))):
            first_refs[i][which] = piece_of(quad[:, 4:12])
            rest_refs[i][0, which] = last_piece_of(quad)
            rest_refs[i][1, which] = piece_of(quad[:, 12:20])


def packed(tokens, cotangent):
    channels = tokens.shape[-1]
    S = jax.ShapeDtypeStruct
    outs = pl.pallas_call(
        pack_kernel,
        out_shape=(S((2, channels, LANES), BF16),) * 4 + (S((2, 2, channels, LANES), BF16),) * 4,
        in_specs=[pl.BlockSpec(memory_space=pltpu.HBM)] * 2,
        out_specs=(VMEM,) * 8,
        scratch_shapes=[pltpu.VMEM((2, *tokens.shape), BF16), pltpu.SemaphoreType.DMA((2, 4))],
        compiler_params=pltpu.CompilerParams(vmem_limit_bytes=62 * 2**20),
        name="pack",
    )(tokens, cotangent)
    return outs[:4], outs[4:]


def prepare_kernel(
    gain_ref, bias_ref, wqkv_ref, proj_ref,
    gain_out, bias_out, wqkv_t_out, proj_t_out, kf_out, qf_out,
):
    gain_out[...] = gain_ref[...].T
    bias_out[...] = bias_ref[...].T
    wqkv_t_out[...] = wqkv_ref[...].astype(F32).T.astype(BF16)
    proj_t_out[...] = proj_ref[...].astype(F32).T.astype(BF16)
    edge_x = lax.axis_index("gx") == lax.axis_size("gx") - 1
    edge_y = lax.axis_index("gy") == lax.axis_size("gy") - 1
    shape = kf_out.shape[1:]
    row = lax.broadcasted_iota(jnp.int32, shape, 0)
    lane = lax.broadcasted_iota(jnp.int32, shape, 1)
    for layout, span in enumerate((LANES, LANES // 2)):
        quad = (lane // span) % 4
        far_x = jnp.where(jnp.logical_and(quad // 2 == 0, edge_x), 1.0, 0.0)
        far_y = jnp.where(jnp.logical_and(quad % 2 == 0, edge_y), 1.0, 0.0)
        key = jnp.where(row == 0, far_x, jnp.where(row == 1, 1 - far_x, jnp.where(row == 2, far_y, 1 - far_y)))
        query = jnp.where(row == 0, 1 - far_x, jnp.where(row == 1, far_x, jnp.where(row == 2, 1 - far_y, far_y)))
        kf_out[layout] = jnp.where(row < 4, key, 0.0).astype(BF16)
        qf_out[layout] = jnp.where(row < 4, query * -MASKED, 0.0).astype(BF16)


def prepared(gain, bias, wqkv, proj):
    channels = gain.shape[0]
    cells = 4 * LANES
    S = jax.ShapeDtypeStruct
    return pl.pallas_call(
        prepare_kernel,
        out_shape=(
            S((channels, 1), F32),
            S((channels, 1), F32),
            S((3 * channels, channels), BF16),
            S((channels, channels), BF16),
            S((2, 16, cells), BF16),
            S((2, 16, cells), BF16),
        ),
        in_specs=[VMEM] * 4,
        out_specs=(VMEM,) * 6,
        compiler_params=pltpu.CompilerParams(vmem_limit_bytes=40 * 2**20),
        name="prepare",
    )(gain[None], bias[None], wqkv, proj)


def unpack_kernel(low_y_ref, paired_low, paired_high, middle_low, middle_high, *outs):
    for which, out in enumerate(outs):
        for xh, (paired, middle) in enumerate(
            ((paired_low, middle_low), (paired_high, middle_high))
        ):
            for yh in range(2):
                if yh:
                    first, last = paired[1, 0, which], paired[1, 1, which]
                    second = middle[1, which]
                else:
                    first, last = low_y_ref[2 * xh, which], low_y_ref[2 * xh + 1, which]
                    second = low_y_ref[4 + xh, which]
                quad = quadrant_of(first, second, last)
                out[xh * 4 : xh * 4 + 4, yh * 4 : yh * 4 + 4] = quad


def unpacked(low_y, paired, middle, shape):
    return pl.pallas_call(
        unpack_kernel,
        out_shape=(jax.ShapeDtypeStruct(shape, BF16),) * 2,
        in_specs=[VMEM] * 5,
        out_specs=(VMEM,) * 2,
        compiler_params=pltpu.CompilerParams(vmem_limit_bytes=40 * 2**20),
        name="unpack",
    )(low_y, *paired, *middle)


def attend_kernel(
    turn,
    q00_ref, q01_ref, q10_ref, q11_ref,
    kf_ref, qf_ref, gain_ref, bias_ref, wqkv_t_ref, wqkv_ref, proj_ref, proj_t_ref,
    *refs,
):
    halves = turn == 1
    given = (0, 3, 1)[turn]
    earlier_refs, refs = refs[:given], refs[given:]
    y_refs, grads_ref, scratch = refs[:2], refs[2], refs[3:]
    (qkv_s, gm_s, mix_s, gqkv_s, k_s, q_s, v_s, g_s, e_s, p_s, pb_s, dp_s, ds_s, dst_s, r_s, d_s) = scratch
    quads = (q00_ref, q01_ref, q10_ref, q11_ref)
    if turn:
        quads = [quad.at[turn - 1] for quad in quads]
    channels = q00_ref.shape[-2]
    hd = channels // HEADS
    cells = 4 * LANES
    half = LANES // 2

    def whole(which):
        if halves:
            parts = [q[which].astype(F32) for q in quads]
            return jnp.concatenate(
                [p[:, :half] for p in parts] + [p[:, half:] for p in parts], axis=1
            )
        return jnp.concatenate([q[which].astype(F32) for q in quads], axis=1)

    xf = whole(0)
    gf = whole(1)
    g = gf.astype(BF16)
    mean = jnp.mean(xf, axis=0, keepdims=True)
    centered = xf - mean
    var = jnp.mean(centered * centered, axis=0, keepdims=True)
    inv = lax.rsqrt(var + 1e-5)
    std = centered * inv
    gain = gain_ref[...]
    normed = (std * gain + bias_ref[...]).astype(BF16)
    qkv = dot(wqkv_t_ref[...], normed).astype(BF16)
    qkv_s[...] = qkv
    gm_s[...] = dot(proj_ref[...], g).astype(BF16)

    layout = 1 if halves else 0
    size = cells // 2 if halves else cells
    groups = [slice(start, start + size) for start in range(0, cells, size)]
    chunks = [
        (gi, slice(c, c + LANES), slice(c - group.start, c - group.start + LANES), group)
        for gi, group in enumerate(groups)
        for c in range(group.start, group.stop, LANES)
    ]
    part = cells // 2
    parts = [
        (groups[min(i, len(groups) - 1)], slice(i * part, (i + 1) * part),
         slice(i * part % size, i * part % size + part))
        for i in range(2)
    ]
    scale = hd**-0.5

    def head_rows(base, h):
        if isinstance(h, int):
            return slice(base + h * hd, base + (h + 1) * hd)
        return pl.ds(pl.multiple_of(base + h * hd, hd), hd)

    def q_rows(h):
        return head_rows(0, h)

    def k_rows(h):
        return head_rows(channels, h)

    def v_rows(h):
        return head_rows(2 * channels, h)

    def folded(x):
        return jnp.sum(x.reshape(-1, 8, x.shape[-1]), axis=0)

    def added(total, gi, x):
        total[gi] = x if total[gi] is None else total[gi] + x

    def prepare(h, slot):
        k = qkv_s[k_rows(h)]
        qf = qkv_s[q_rows(h)].astype(F32) * (scale * LOG2E)
        q_hi = qf.astype(BF16)
        q_lo = (qf - q_hi.astype(F32)).astype(BF16)
        k_s[slot] = jnp.concatenate([k, k, kf_ref[layout]], axis=0).T
        q_s[slot] = jnp.concatenate([q_hi, q_lo, qf_ref[layout]], axis=0)
        v_s[slot] = qkv_s[v_rows(h)].T
        g_s[slot] = gm_s[q_rows(h)]

    def exponentials(slot, chunk, total):
        gi, rows, _, cols = chunk
        e = jnp.exp2(dot(k_s[slot, rows], q_s[slot, :, cols]))
        e_s[slot, rows] = e
        added(total, gi, folded(e))

    def attention(slot, chunk, total):
        gi, rows, _, cols = chunk
        p = e_s[slot, rows] * r_s[slot, 0:1, cols]
        p_s[slot, rows] = p
        pb_s[slot, rows] = p.astype(BF16)
        dp = dot(v_s[slot, rows], g_s[slot, :, cols])
        dp_s[slot, rows] = dp
        added(total, gi, folded(p * dp))

    def grad_scores(slot, chunk):
        _, rows, place, cols = chunk
        ds = (p_s[slot, rows] * (dp_s[slot, rows] - d_s[slot, 0:1, cols])).astype(BF16)
        ds_s[slot, rows] = ds
        dst_s[slot, cols, place] = ds.T

    def mixed_part(h, slot, i):
        over, out, place = parts[i]
        mix_s[q_rows(h), out] = dot(qkv_s[v_rows(h), over], pb_s[slot, over, place]).astype(BF16)

    def grad_values_part(h, slot, i):
        over, out, _ = parts[i]
        gv = lax.dot_general(
            gm_s[q_rows(h), over], pb_s[slot, out], NT, preferred_element_type=F32
        )
        gqkv_s[v_rows(h), out] = gv.astype(BF16)

    def grad_queries_part(h, slot, i):
        over, out, place = parts[i]
        gq = dot(qkv_s[k_rows(h), over], ds_s[slot, over, place]) * scale
        gqkv_s[q_rows(h), out] = gq.astype(BF16)

    def grad_keys_part(h, slot, i):
        over, out, place = parts[i]
        gk = dot(qkv_s[q_rows(h), over], dst_s[slot, over, place]) * scale
        gqkv_s[k_rows(h), out] = gk.astype(BF16)

    def kept(ref, slot, total, of):
        for gi, cols in enumerate(groups):
            ref[slot, 0:1, cols] = of(jnp.sum(total[gi], axis=0, keepdims=True))

    def step(i, slot, one=True, two=True, three=True, four=True, ahead=True):
        sums = [None] * len(groups)
        inner = [None] * len(groups)
        for c, chunk in enumerate(chunks):
            if c % 2 == 0 and three:
                mixed_part(i - 2, slot, c // 2)
                grad_values_part(i - 2, slot, c // 2)
            if c % 2 == 1 and four:
                grad_queries_part(i - 3, 1 - slot, c // 2)
                grad_keys_part(i - 3, 1 - slot, c // 2)
            if one:
                exponentials(slot, chunk, sums)
            if two:
                attention(1 - slot, chunk, inner)
            if three:
                grad_scores(slot, chunk)
        if one:
            kept(r_s, slot, sums, lambda total: 1.0 / total)
        if two:
            kept(d_s, 1 - slot, inner, lambda total: total)
        if ahead:
            prepare(i + 1, 1 - slot)

    squares = jnp.square(qkv[: 2 * channels].astype(F32)).reshape(2 * HEADS, hd, cells)
    longest = jnp.max(jnp.sum(squares, axis=1), axis=1, keepdims=True)
    bound = jnp.max(longest[:HEADS] * longest[HEADS:]) * (scale * LOG2E) ** 2
    in_range = bound <= 110.0**2

    @pl.when(in_range)
    def _():
        prepare(0, 0)
        step(0, 0, two=False, three=False, four=False)
        step(1, 1, three=False, four=False)
        step(2, 0, four=False)

        for i in range(3, HEADS - 1):
            step(i, i % 2)
        step(HEADS - 1, 1, ahead=False)
        step(HEADS, 0, one=False, ahead=False)
        step(HEADS + 1, 1, one=False, two=False, ahead=False)
        step(HEADS + 2, 0, one=False, two=False, three=False, ahead=False)

    @pl.when(jnp.logical_not(in_range))
    def _():
        def head(h, carry):
            prepare(h, 0)
            for cols in groups:
                s = dot(k_s[0, cols], q_s[0, :, cols])
                e = jnp.exp2(s - jnp.max(s, axis=0, keepdims=True))
                p = e * (1.0 / jnp.sum(e, axis=0, keepdims=True))
                pb_s[0, cols] = p.astype(BF16)
                dp = dot(v_s[0, cols], g_s[0, :, cols])
                inner = jnp.sum(p * dp, axis=0, keepdims=True)
                ds = (p * (dp - inner)).astype(BF16)
                ds_s[0, cols] = ds
                dst_s[0, cols] = ds.T
            for i in range(2):
                mixed_part(h, 0, i)
                grad_values_part(h, 0, i)
                grad_queries_part(h, 0, i)
                grad_keys_part(h, 0, i)
            return carry

        lax.fori_loop(0, HEADS, head, 0)

    mixed = mix_s[...]
    block_out = xf + dot(proj_t_ref[...], mixed)
    gqkv = gqkv_s[...]
    gn = dot(wqkv_ref[...], gqkv)
    scaled = gn * gain
    gx = inv * (
        scaled
        - jnp.mean(scaled, axis=0, keepdims=True)
        - std * jnp.mean(scaled * std, axis=0, keepdims=True)
    )
    d_tokens = gf + gx
    for which, y in enumerate((block_out, d_tokens)):
        for i in range(4):
            ref, yh = y_refs[i // 2], i % 2
            if halves:
                lo = y[:, i * half : (i + 1) * half]
                hi = y[:, cells // 2 + i * half : cells // 2 + (i + 1) * half]
                part = jnp.concatenate([lo, hi], axis=1)
                ref[yh, 0, which] = earlier_refs[i // 2][yh, which]
                ref[yh, 1, which] = part.astype(BF16)
            else:
                ref[yh, which] = y[:, i * LANES : (i + 1) * LANES].astype(BF16)

    dw = lax.dot_general(normed, gqkv, NT, preferred_element_type=F32)
    dproj = lax.dot_general(mixed, g, NT, preferred_element_type=F32)
    dgain = jnp.sum(gn * std, axis=1, keepdims=True)
    dbias = jnp.sum(gn, axis=1, keepdims=True)
    joined = jnp.concatenate([dw, dproj], axis=1)
    blocks = [joined[:, i * LANES : (i + 1) * LANES] for i in range(joined.shape[1] // LANES)]
    lane = lax.broadcasted_iota(jnp.int32, (channels, LANES), 1)
    tail = jnp.where(lane == 0, dgain, jnp.where(lane == 1, dbias, 0.0)).T[:8]
    used = len(blocks) * channels
    grads = jnp.concatenate(blocks, axis=0)
    pad = jnp.zeros((8, 2 * LANES - channels), F32)
    extra = jnp.concatenate(
        [tail[:, :LANES], jnp.concatenate([tail[:, LANES:], pad], axis=1)], axis=0
    )
    if turn:
        grads = grads + earlier_refs[-1][:used]
        extra = extra + earlier_refs[-1][used : used + 16]
    grads_ref[:used] = grads.astype(grads_ref.dtype)
    grads_ref[used : used + 16] = extra.astype(grads_ref.dtype)
    grads_ref[used + 16 :] = jnp.zeros(
        (grads_ref.shape[0] - used - 16, LANES), grads_ref.dtype
    )


GRAD_ROWS = 1280


def attend(turn, quads, features, weights, earlier):
    channels = quads[0].shape[-2]
    cells = 4 * LANES
    width = cells // 2 if turn == 1 else cells
    S = jax.ShapeDtypeStruct
    piece = (2, channels, LANES)
    return pl.pallas_call(
        functools.partial(attend_kernel, turn),
        out_shape=(S((2, 2, *piece) if turn == 1 else (2, *piece), BF16),) * 2
        + (S((GRAD_ROWS, LANES), BF16 if turn == 2 else F32),),
        in_specs=[VMEM] * (12 + len(earlier)),
        out_specs=(VMEM,) * 3,
        scratch_shapes=[
            pltpu.VMEM((3 * channels, cells), BF16),
            pltpu.VMEM((channels, cells), BF16),
            pltpu.VMEM((channels, cells), BF16),
            pltpu.VMEM((3 * channels, cells), BF16),
            pltpu.VMEM((2, cells, 48), BF16),
            pltpu.VMEM((2, 48, cells), BF16),
            pltpu.VMEM((2, cells, 16), BF16),
            pltpu.VMEM((2, 16, cells), BF16),
            pltpu.VMEM((2, cells, width), F32),
            pltpu.VMEM((2, cells, width), F32),
            pltpu.VMEM((2, cells, width), BF16),
            pltpu.VMEM((2, cells, width), F32),
            pltpu.VMEM((2, cells, width), BF16),
            pltpu.VMEM((2, cells, width), BF16),
            pltpu.VMEM((2, 8, cells), F32),
            pltpu.VMEM((2, 8, cells), F32),
        ],
        compiler_params=pltpu.CompilerParams(vmem_limit_bytes=40 * 2**20),
        cost_estimate=pl.CostEstimate(
            flops=12 * 12 * 512 * 512 * 256, bytes_accessed=4 * 2**20, transcendentals=12 * 512 * 512
        ),
        name="attend",
    )(*quads, *features, *weights, *earlier)


def moved(block, step_x, step_y):
    nx, ny = lax.axis_size("gx"), lax.axis_size("gy")
    route = []
    for i in range(nx):
        for j in range(ny):
            to = ((i + step_x) % nx) * ny + (j + step_y) % ny
            route.append((i * ny + j, to))
    return lax.ppermute(block, ("gx", "gy"), route)


def summed(rows, paired, middle):
    nx, ny = lax.axis_size("gx"), lax.axis_size("gy")
    near = 2 * ny
    planes = [[near * i + j for j in range(near)] for i in range(nx // 2)]
    across = [list(ids) for ids in zip(*planes)]

    def exchanged(pieces, groups):
        return lax.all_to_all(pieces, ("gx", "gy"), 0, 0, axis_index_groups=groups)

    def copies(piece, count):
        return jnp.broadcast_to(piece[None], (count, *piece.shape))

    got = exchanged(rows.reshape(near, -1, LANES), planes)
    middle = (moved(middle[0], 1, 0), middle[1])
    got, middle = lax.optimization_barrier((got, middle))
    mine = jnp.sum(got.astype(F32), axis=0).astype(BF16)
    got = exchanged(copies(mine, nx // 2), across)
    low_y = moved(jnp.concatenate([paired[0][0], paired[1][0], middle[0][:1], middle[1][:1]]), 0, 1)
    got, low_y = lax.optimization_barrier((got, low_y))
    total = jnp.sum(got.astype(F32), axis=0).astype(BF16)
    return exchanged(copies(total, near), planes).reshape(rows.shape), low_y, middle


def grads_kernel(factor, rows_ref, dw_ref, dproj_ref, gain_ref, bias_ref):
    channels = dw_ref.shape[0]
    blocks = 4 * channels // LANES
    joined = jnp.concatenate(
        [rows_ref[i * channels : (i + 1) * channels].astype(F32) for i in range(blocks)], axis=1
    ) * factor
    dw_ref[...] = joined[:, : 3 * channels]
    dproj_ref[...] = joined[:, 3 * channels :]
    used = blocks * channels
    tail = rows_ref[used : used + 16].astype(F32) * factor
    tail = jnp.concatenate([tail[:8], tail[8:]], axis=1)[:, :channels]
    gain_ref[...] = tail[0:1]
    bias_ref[...] = tail[1:2]


def grads_of(rows, channels, factor):
    S = jax.ShapeDtypeStruct
    return pl.pallas_call(
        functools.partial(grads_kernel, factor),
        out_shape=(
            S((channels, 3 * channels), F32),
            S((channels, channels), F32),
            S((1, channels), F32),
            S((1, channels), F32),
        ),
        in_specs=[VMEM],
        out_specs=(VMEM,) * 4,
        name="unpack_grads",
    )(rows)


def shards(tokens, cotangent, ln_gain, ln_bias, qkv_weight, proj_weight):
    tile_x, tile_y, depth, channels = tokens.shape
    nx, ny = lax.axis_size("gx"), lax.axis_size("gy")
    first, rest = packed(tokens, cotangent)
    first, proj_weight = lax.optimization_barrier((first, proj_weight))
    gain, bias, wqkv_t, proj_t, *features = prepared(ln_gain, ln_bias, qkv_weight, proj_weight)
    weights = (gain, bias, wqkv_t, qkv_weight, proj_weight, proj_t)
    rest, features = lax.optimization_barrier((rest, features))

    steps = ((1, 1), (1, 0), (0, 1))

    def gathered(quads):
        order = [2, 0, 1]
        got = {i: moved(quads[i], -steps[i][0], -steps[i][1]) for i in order}
        return [got[0], got[1], got[2], quads[3]]

    first, rest = gathered(first), gathered(rest)
    low, high, sums = attend(0, first, features, weights, ())
    low, high, sums = attend(1, rest, features, weights, (low, high, sums))
    paired = (moved(low, 1, 0), high)
    *middle, sums = attend(2, rest, features, weights, (sums,))
    sums, paired = lax.optimization_barrier((sums, paired))
    total, low_y, middle = summed(sums, paired, middle)
    block_out, d_tokens = unpacked(low_y, paired, middle, tokens.shape)
    factor = 1.0 / math.sqrt(tile_x * nx * tile_y * ny * depth)
    dw, dproj, dgain, dbias = grads_of(total, channels, factor)
    return block_out, d_tokens, dw, dproj, dgain[0], dbias[0]


def solution(mesh):
    placed = (P("gx", "gy", None, None), P("gx", "gy", None, None), P(), P(), P(), P())
    return jax.shard_map(
        shards,
        mesh=mesh,
        in_specs=placed,
        out_specs=(P("gx", "gy", None, None), P("gx", "gy", None, None), P(), P(), P(), P()),
        check_vma=False,
    )
```
